32 devices in a mesh: gx: 2 (over x), gy: 4 (over z), gz: 4 (over y, core).
Axes of the slice: x: 2, y: 2, z: 4, core: 2. Of those that a mesh axis runs over, the one named last changes fastest.
Arguments:
- pressure_start: float32 [32, 256, 1024], P('gx', 'gy', 'gz'), may hold values from -6 to 6
- source: float32 [32, 256, 1024], P('gx', 'gy', 'gz'), may hold values from -16 to 16
- permeability: float32 [32, 256, 1024], P('gx', 'gy', 'gz'), may hold values from 0.1 to 10
Outputs:
- pressure: float32 [32, 256, 1024], P('gx', 'gy', 'gz')
The draws below stay inside these ranges and needn't reach their ends.
All inputs are finite; a program needn't handle non-finite values.
Results may differ from the reference program's by a relative error of at most 0.0003.
Values sent between devices are 32-bit elements; how exact they have to be, the bound alone decides.
No kernel may reach another device: no remote copies, remote signals or barrier semaphores. Data moves between devices by JAX's collectives and lax.ppermute only.
A program may use at most 128 MiB of HBM per device.

```python
import math
import jax
import jax.numpy as jnp

RATIO = 8
SWEEPS = 4
COARSE_SWEEPS = 8
NZ = 32
NY = 256
NX = 1024


def draw_source(key, part):
    shape = (NZ, NY, NX)
    cells_z, cells_y, cells_x = (NZ // RATIO, NY // RATIO, NX // RATIO)
    sign_bits = jax.random.randint(jax.random.fold_in(key, 7), (cells_z, cells_y, cells_x), 0, 2)
    signs = sign_bits.astype(jnp.float32) * 2.0 - 1.0
    signs = jnp.broadcast_to(signs[:, None, :, None, :, None], (cells_z, RATIO, cells_y, RATIO, cells_x, RATIO)).reshape(shape)
    depth_pos = jnp.arange(NZ, dtype=jnp.float32).reshape(NZ, 1, 1) / NZ
    smooth = 1.0 + 2.0 * depth_pos
    rough_key = jax.random.fold_in(key, 11)
    rough = 4.0 * jax.random.normal(rough_key, shape, jnp.float32)
    return jnp.clip(12.0 * signs + smooth + rough, -16.0, 16.0)


def level_of(rng, shape, cuts, least, largest):
    def one(axis_at, shards_of):
        draws = jax.random.uniform(jax.random.fold_in(jax.random.fold_in(rng, 6), axis_at), (shards_of,), jnp.float32, least / len(cuts), largest / len(cuts))
        return jnp.repeat(jnp.exp(draws), shape[axis_at] // shards_of).reshape((-1,) + (1,) * (len(shape) - axis_at - 1))

    gain = one(*cuts[0])
    for cut in cuts[1:]:
        gain = gain * one(*cut)
    return gain


def centred(own_key, dims, spread, bound, shards=(), kind=jnp.bfloat16):
    result = jax.random.normal(own_key, dims, jnp.float32) * spread
    if len(shards) > 0:
        result = level_of(own_key, dims, shards, -0.22, 0.18) * result
    return jnp.clip(result, min=-bound, max=bound).astype(kind)


def setup_inputs(seed: int = 0) -> dict:
    seeds = jax.random.split(jax.random.key(seed), 4)
    return {
        "pressure_start": centred(seeds[0], (NZ, NY, NX), 1.0, 6.0, ((0, 2), (1, 4), (2, 4)), jnp.float32),
        "source": draw_source(jax.random.fold_in(seeds[3], 71), 0),
        "permeability": jnp.clip(jnp.exp(math.log(10.0) - 4.6051702 * jax.random.uniform(seeds[2], (NZ, NY, NX), jnp.float32) ** level_of(seeds[2], (NZ, NY, NX), ((0, 2), (1, 4), (2, 4)), -0.2, 0.2)), 0.1, 10.0),
    }


OMEGA = 0.8
OMEGA_COARSE = 0.8


def neighbours(padded):
    return (padded[:-2, 1:-1, 1:-1], padded[2:, 1:-1, 1:-1],
            padded[1:-1, :-2, 1:-1], padded[1:-1, 2:, 1:-1],
            padded[1:-1, 1:-1, :-2], padded[1:-1, 1:-1, 2:])


def face_weights(padded):
    center = padded[1:-1, 1:-1, 1:-1]
    weights = tuple(jnp.where(beside_cell > 0.0, 0.5 * (center + beside_cell), center) for beside_cell in neighbours(padded))
    diagonal_sum = weights[0] + weights[1] + weights[2] + weights[3] + weights[4] + weights[5]
    return weights, diagonal_sum


def apply_operator(padded, weights, diagonal_sum):
    beside = neighbours(padded)
    flux = weights[0] * beside[0] + weights[1] * beside[1] + weights[2] * beside[2]
    flux = flux + weights[3] * beside[3] + weights[4] * beside[4] + weights[5] * beside[5]
    return diagonal_sum * padded[1:-1, 1:-1, 1:-1] - flux


def block_sum(values):
    depth, rows, width = values.shape
    return values.reshape(depth // RATIO, RATIO, rows // RATIO, RATIO, width // RATIO, RATIO).sum(axis=(1, 3, 5))


def coarse_faces(weights):
    depth, rows, width = weights[0].shape
    cells_z, cells_y, cells_x = depth // RATIO, rows // RATIO, width // RATIO
    low_z = weights[0][0::RATIO].reshape(cells_z, cells_y, RATIO, cells_x, RATIO).sum(axis=(2, 4))
    high_z = weights[1][RATIO - 1::RATIO].reshape(cells_z, cells_y, RATIO, cells_x, RATIO).sum(axis=(2, 4))
    low_y = weights[2][:, 0::RATIO, :].reshape(cells_z, RATIO, cells_y, cells_x, RATIO).sum(axis=(1, 4))
    high_y = weights[3][:, RATIO - 1::RATIO, :].reshape(cells_z, RATIO, cells_y, cells_x, RATIO).sum(axis=(1, 4))
    low_x = weights[4][:, :, 0::RATIO].reshape(cells_z, RATIO, cells_y, RATIO, cells_x).sum(axis=(1, 3))
    high_x = weights[5][:, :, RATIO - 1::RATIO].reshape(cells_z, RATIO, cells_y, RATIO, cells_x).sum(axis=(1, 3))
    return (low_z, high_z, low_y, high_y, low_x, high_x)


def prolong_add(fine, correction):
    depth, rows, width = fine.shape
    blocks = fine.reshape(depth // RATIO, RATIO, rows // RATIO, RATIO, width // RATIO, RATIO)
    return (blocks + correction[:, None, :, None, :, None]).reshape(depth, rows, width)


def coarse_sweeps(coarse_rhs, faces, diagonal_sum):
    correction = OMEGA_COARSE * coarse_rhs / diagonal_sum
    for sweep_index in range(COARSE_SWEEPS - 1):
        applied = apply_operator(jnp.pad(correction, 1), faces, diagonal_sum)
        correction = correction + OMEGA_COARSE * (coarse_rhs - applied) / diagonal_sum
    applied = apply_operator(jnp.pad(correction, 1), faces, diagonal_sum)
    leftover = jnp.sum(coarse_rhs - applied)
    shift = leftover / jnp.sum(diagonal_sum)
    return correction + shift


def reference(pressure_start, source, permeability):
    weights, diagonal_sum = face_weights(jnp.pad(permeability, 1))
    applied = apply_operator(jnp.pad(pressure_start, 1), weights, diagonal_sum)
    start_residual = source - applied
    pressure_now = pressure_start + OMEGA * start_residual / diagonal_sum
    for sweep_index in range(SWEEPS - 1):
        applied = apply_operator(jnp.pad(pressure_now, 1), weights, diagonal_sum)
        pressure_now = pressure_now + OMEGA * (source - applied) / diagonal_sum
    faces = coarse_faces(weights)
    coarse_diagonal = faces[0] + faces[1] + faces[2] + faces[3] + faces[4] + faces[5]
    correction = coarse_sweeps(block_sum(start_residual), faces, coarse_diagonal)
    return prolong_add(pressure_now, correction)
```

```python
import functools

import jax
import jax.numpy as jnp
from jax import lax
from jax.experimental import pallas as pl
from jax.experimental.pallas import tpu as pltpu
from jax.sharding import PartitionSpec as P

RATIO = 8
SWEEPS = 4
COARSE_SWEEPS = 8
OMEGA = 0.8
OMEGA_COARSE = 0.8

LANES = 128
ROWS = 8
DEPTH = SWEEPS
SLOTS = LANES // DEPTH
F32 = jnp.float32
VMEM_LIMIT = 12 * 1024 * 1024


def pairs(count, odd):
    start = 1 if odd else 0
    out = []
    for low in range(start, count + start - 1, 2):
        high = (low + 1) % count
        out += [(low, high), (high, low)]
    return out


def flips(count, bit):
    return [(i, i ^ bit) for i in range(count)]


def on_chip(value):
    return pltpu.with_memory_space_constraint(value, pltpu.VMEM)


def run(kernel, outs, args, scratch=(), flops=1000, name=None, out_spaces=None):
    whole = pl.BlockSpec(memory_space=pltpu.VMEM)
    shapes = [pltpu.VMEM(shape, F32) for shape in outs] if out_spaces is None else out_spaces
    result = pl.pallas_call(
        kernel,
        out_shape=shapes,
        in_specs=[whole] * len(args),
        out_specs=[whole] * len(outs),
        scratch_shapes=list(scratch),
        compiler_params=pltpu.CompilerParams(vmem_limit_bytes=VMEM_LIMIT),
        cost_estimate=pl.CostEstimate(flops=flops, bytes_accessed=0, transcendentals=0),
        name=name,
    )(*[on_chip(a) for a in args])
    return result


def lane_of(shape):
    return lax.broadcasted_iota(jnp.int32, shape, len(shape) - 1)


def row_of(shape):
    return lax.broadcasted_iota(jnp.int32, shape, len(shape) - 2)


def roll(values, shift, axis):
    size = values.shape[axis]
    if isinstance(shift, int):
        shift = shift % size
        if shift == 0:
            return values
    return pltpu.roll(values, shift, axis)


def face(one, other):
    half = jnp.where(jnp.minimum(one, other) > 0.0, 0.5, 1.0)
    return half * (one + other)


def group_rows(values):
    rows, width = values.shape
    return values.reshape(rows // RATIO, RATIO, width).sum(axis=1)


def split3(values):
    a = values.astype(jnp.bfloat16)
    rest = values - a.astype(F32)
    b = rest.astype(jnp.bfloat16)
    c = (rest - b.astype(F32)).astype(jnp.bfloat16)
    return jnp.concatenate([a, b, c], axis=0)


def exact_dot(values, onehot):
    rows = values.shape[0]
    out = jnp.dot(split3(values), onehot, preferred_element_type=F32)
    return out[:rows] + out[rows : 2 * rows] + out[2 * rows :]


class Grid:
    def __init__(self, shape):
        self.Z, self.Y, self.X = shape
        self.nz, self.ny, self.nx = (lax.axis_size("gx"), lax.axis_size("gy"), lax.axis_size("gz"))
        self.cz, self.cy, self.cx = (n // RATIO for n in shape)
        self.blocks = -(-3 * self.Z // SLOTS)
        self.XE = self.X + LANES
        self.YE = self.Y + ROWS
        self.ZE = self.Z + 2 * DEPTH
        self.zsides = 1 if self.nz == 2 else 2
        self.ysides = 1 if self.ny == 2 else 2
        self.xsides = 1 if self.nx == 2 else 2
        assert 2 * DEPTH == ROWS and 2 * self.Z <= SLOTS and self.Z % 2 == 0
        assert self.blocks * LANES <= self.X and self.cy == ROWS
        assert self.cx * self.nx == LANES

    def where(self):
        return lax.axis_index("gx"), lax.axis_index("gy"), lax.axis_index("gz")

    def slot(self, q, z):
        index = q * self.Z + z
        return index // SLOTS, (index % SLOTS) * DEPTH


def pack_kernel(g, *refs):
    src = refs[:3]
    z_out = refs[3 : 3 + g.zsides]
    x_out = refs[3 + g.zsides :]
    zi, yi, xi = g.where()
    for side, out in enumerate(z_out):
        high = (zi % 2) == side
        at = jnp.where(high, g.Z - DEPTH, 0)
        out[0:DEPTH] = src[0][pl.ds(at, DEPTH)]
        out[DEPTH : 2 * DEPTH] = src[1][pl.ds(at, DEPTH)]
        at = jnp.where(high, g.Z - DEPTH + 1, 0)
        out[2 * DEPTH :] = src[2][pl.ds(at, DEPTH - 1)]
    lane = lane_of((g.Y, LANES))
    packs = []
    for high in (True, False):
        acc = [jnp.zeros((g.Y, LANES), F32) for _ in range(g.blocks)]
        for q in range(3):
            for z in range(g.Z):
                block, at = g.slot(q, z)
                if high:
                    moved = roll(src[q][z, :, g.X - LANES :], at + DEPTH, 1)
                else:
                    moved = roll(src[q][z, :, :LANES], at, 1)
                acc[block] = jnp.where((lane >= at) & (lane < at + DEPTH), moved, acc[block])
        packs.append(acc)
    even = (xi % 2) == 0
    for block in range(g.blocks):
        hi, lo = packs[0][block], packs[1][block]
        for side, out in enumerate(x_out):
            out[block] = jnp.where(even == (side == 0), hi, lo)


def pick(first, second, even, inside):
    if second is None:
        return jnp.where(even & inside, first, 0.0)
    return jnp.where(inside, jnp.where(even, first, second), 0.0)


def from_high(index, count, bufs, view):
    even = (index % 2) == 0
    second = view(bufs[1]) if len(bufs) > 1 else None
    return pick(view(bufs[0]), second, even, index < count - 1)


def from_low(index, count, bufs, view):
    odd = (index % 2) == 1
    second = view(bufs[1]) if len(bufs) > 1 else None
    return pick(view(bufs[0]), second, odd, index > 0)


def pack_rows_kernel(g, *refs):
    src = refs[:3]
    x_in = refs[3 : 3 + g.xsides]
    y_out = refs[3 + g.xsides :]
    zi, yi, xi = g.where()
    half = g.Z // 2
    last = g.Y - ROWS
    for side, out in enumerate(y_out):
        high = (yi % 2) == side

        def fill(top, out=out):
            for q in range(3):
                for pair in range(half):
                    a, b = src[q][2 * pair], src[q][2 * pair + 1]
                    if top:
                        part = jnp.concatenate([a[g.Y - DEPTH :], b[g.Y - DEPTH :]], axis=0)
                    else:
                        part = jnp.concatenate([a[:DEPTH], b[:DEPTH]], axis=0)
                    out[q * half + pair] = part
            rows = slice(g.Y - DEPTH, g.Y) if top else slice(0, DEPTH)
            for block in range(g.blocks):
                hi = from_high(xi, g.nx, x_in, lambda r: r[block, rows, :])
                lo = from_low(xi, g.nx, x_in, lambda r: r[block, rows, :])
                out[3 * half, :, block * LANES : (block + 1) * LANES] = jnp.concatenate(
                    [hi, lo], axis=0
                )

        pl.when(high)(functools.partial(fill, True))
        pl.when(jnp.logical_not(high))(functools.partial(fill, False))


def gather_rows(g, yi, y_in, hy, ly):
    hy[...] = from_high(yi, g.ny, y_in, lambda r: r[...])
    ly[...] = from_low(yi, g.ny, y_in, lambda r: r[...])


def gather_strips(g, xi, x_in, hy, ly, xh, xl):
    half = g.Z // 2
    for block in range(g.blocks):
        lanes = slice(block * LANES, (block + 1) * LANES)
        xh[block, : g.Y] = from_high(xi, g.nx, x_in, lambda r: r[block])
        xl[block, : g.Y] = from_low(xi, g.nx, x_in, lambda r: r[block])
        top, low = hy[3 * half, :, lanes], ly[3 * half, :, lanes]
        xh[block, g.Y :] = jnp.concatenate([top[:DEPTH], low[:DEPTH]], axis=0)
        xl[block, g.Y :] = jnp.concatenate([top[DEPTH:], low[DEPTH:]], axis=0)


def row_halo(g, hy, ly, q, z):
    half = g.Z // 2
    at = (z % 2) * DEPTH
    block = q * half + z // 2
    return jnp.concatenate([hy[block, at : at + DEPTH], ly[block, at : at + DEPTH]], axis=0)


def restrict_kernel(g, *refs):
    n = 3
    src = refs[:n]
    z_in = refs[n : n + g.zsides]
    n += g.zsides
    y_in = refs[n : n + g.ysides]
    n += g.ysides
    x_in = refs[n : n + g.xsides]
    n += g.xsides
    x_own = refs[n : n + g.xsides]
    n += g.xsides
    outs = refs[n : n + g.zsides]
    n += g.zsides
    hy, ly, xh, xl = refs[n:]
    p, k, s = src
    zi, yi, xi = g.where()
    gather_rows(g, yi, y_in, hy, ly)
    gather_strips(g, xi, x_in, hy, ly, xh, xl)
    Z, Y, X = g.Z, g.Y, g.X
    half = Z // 2

    zero = jnp.zeros((Y, X), F32)
    flux_z, weight_z = [], []
    for layer in range(0, Z + 1, RATIO):
        if layer == 0:
            p0 = from_low(zi, g.nz, z_in, lambda r: r[DEPTH - 1])
            k0 = from_low(zi, g.nz, z_in, lambda r: r[2 * DEPTH - 1])
        else:
            p0, k0 = p[layer - 1], k[layer - 1]
        if layer == Z:
            p1 = from_high(zi, g.nz, z_in, lambda r: r[0])
            k1 = from_high(zi, g.nz, z_in, lambda r: r[DEPTH])
        else:
            p1, k1 = p[layer], k[layer]
        w = face(k0, k1)
        weight_z.append(group_rows(w))
        flux_z.append(group_rows(w * (p1 - p0)))

    lane = lane_of((Y, LANES))
    even = (xi % 2) == 0
    if g.xsides == 1:
        own_hi = own_lo = x_own[0][0]
    else:
        own_hi = jnp.where(even, x_own[0][0], x_own[1][0])
        own_lo = jnp.where(even, x_own[1][0], x_own[0][0])

    def side_sums(own, other, lane_in, flip):
        wk = face(roll(own, -Z * DEPTH, 1), roll(other, -Z * DEPTH, 1))
        diff = (other - own) if flip else (own - other)
        keep = (lane % DEPTH == lane_in) & (lane < Z * DEPTH)
        w = jnp.where(keep, wk, 0.0)
        result = []
        for value in (w, w * diff):
            total = group_rows(value)
            step = DEPTH
            while step < RATIO * DEPTH:
                total = total + roll(total, -step, 1)
                step *= 2
            result.append(total)
        return result

    low_w, low_f = side_sums(own_lo, roll(xl[0, :Y], -(DEPTH - 1), 1), 0, False)
    high_w, high_f = side_sums(own_hi, roll(xh[0, :Y], DEPTH - 1, 1), DEPTH - 1, True)
    lane8 = lane_of((ROWS, X))
    row8 = row_of((ROWS, X))
    row = row_of((Y, X))
    inner = (lane8 % RATIO == 0) & (lane8 > 0)

    def widen(value, at, cell):
        moved = roll(value, (at % LANES) - cell, 1)
        wide = jnp.concatenate([moved] * (X // LANES), axis=1)
        return jnp.where(lane8 == at, wide, 0.0)

    rows = []
    for cz in range(g.cz):
        acc_s = zero
        acc_w = zero
        acc_f = zero
        acc_wy = zero
        acc_fy = zero
        low_wy = low_fy = top_w = top_f = jnp.zeros((1, X), F32)
        for z in range(cz * RATIO, (cz + 1) * RATIO):
            pz, kz = p[z], k[z]
            acc_s = acc_s + s[z]
            w = 0.5 * (kz + roll(kz, 1, 1))
            acc_w = acc_w + w
            acc_f = acc_f + w * (pz - roll(pz, 1, 1))
            w = 0.5 * (kz + roll(kz, 1, 0))
            acc_wy = acc_wy + w
            acc_fy = acc_fy + w * (pz - roll(pz, 1, 0))
            at = (z % 2) * DEPTH
            below = [ly[q * half + z // 2, at + DEPTH - 1 : at + DEPTH, :] for q in range(2)]
            above = [hy[q * half + z // 2, at : at + 1, :] for q in range(2)]
            w = face(kz[:1], below[1])
            low_wy = low_wy + w
            low_fy = low_fy + w * (pz[:1] - below[0])
            w = face(kz[Y - 1 :], above[1])
            top_w = top_w + w
            top_f = top_f + w * (above[0] - pz[Y - 1 :])

        def lower(acc, low):
            kept = group_rows(jnp.where(row % RATIO == 0, acc, 0.0))
            return jnp.where(row8 == 0, jnp.broadcast_to(low, (ROWS, X)), kept)

        weight_y = lower(acc_wy, low_wy)
        flux_y = lower(acc_fy, low_fy)

        def upper(values, top):
            return jnp.where(
                row8 == g.cy - 1, jnp.broadcast_to(top, (ROWS, X)), roll(values, -1, 0)
            )

        weight_x = jnp.where(inner, group_rows(acc_w), 0.0)
        flux_x = jnp.where(inner, group_rows(acc_f), 0.0)
        cell = cz * RATIO * DEPTH
        x_low = widen(low_w, 0, cell)
        x_high = widen(high_w, X - 1, cell + DEPTH - 1)
        f_low = widen(low_f, 0, cell)
        f_high = widen(high_f, X - 1, cell + DEPTH - 1)
        rhs = (
            group_rows(acc_s)
            - (flux_z[cz] - flux_z[cz + 1])
            - (flux_y - upper(flux_y, top_f))
            - (flux_x - roll(flux_x, -1, 1))
            - (f_low - f_high)
        )
        diagonal = (
            weight_z[cz]
            + weight_z[cz + 1]
            + weight_y
            + upper(weight_y, top_w)
            + weight_x
            + roll(weight_x, -1, 1)
            + x_low
            + x_high
        )
        rows.append([rhs, diagonal, weight_z[cz], weight_y, weight_x + x_low])

    items = [rows[cz][q] for q in range(5) for cz in range(g.cz)]
    onehot = (
        lax.broadcasted_iota(jnp.int32, (X, LANES), 0) // RATIO
        == lax.broadcasted_iota(jnp.int32, (X, LANES), 1)
    ).astype(jnp.bfloat16)
    summed = exact_dot(jnp.concatenate(items, axis=0), onehot)
    per = LANES // g.cx
    cells = [jnp.zeros((ROWS, LANES), F32) for _ in range(coarse_blocks(g))]
    for m in range(len(items)):
        place = lax.rem(m % per + xi, per) * g.cx
        cells[m // per] = cells[m // per] + pltpu.roll(
            summed[m * ROWS : (m + 1) * ROWS], place, 1
        )
    for block, value in enumerate(cells):
        outs[0][block] = value

    for side, out in enumerate(outs):
        base = coarse_blocks(g) if side == 0 else 0
        high = (zi % 2) == side

        def fill(top, out=out, base=base):
            first = Z - DEPTH if top else 0
            for q in range(3):
                for d in range(DEPTH):
                    part = row_halo(g, hy, ly, q, first + d)
                    for half_lane in range(X // LANES):
                        out[base + (q * DEPTH + d) * (X // LANES) + half_lane] = part[
                            :, half_lane * LANES : (half_lane + 1) * LANES
                        ]
            at_block = base + 3 * DEPTH * (X // LANES)
            wide = lane_of((g.YE, LANES))
            acc = jnp.zeros((g.YE, LANES), F32)
            span = DEPTH * DEPTH
            for piece, (ref, q) in enumerate((r, q) for r in (xh, xl) for q in range(3)):
                block, lane_at = g.slot(q, first)
                moved = roll(ref[block], piece * span - lane_at, 1)
                acc = jnp.where((wide >= piece * span) & (wide < (piece + 1) * span), moved, acc)
            out[at_block:] = acc.reshape(g.YE // ROWS, ROWS, LANES)

        pl.when(high)(functools.partial(fill, True))
        pl.when(jnp.logical_not(high))(functools.partial(fill, False))


def coarse_blocks(g):
    per = LANES // g.cx
    return -(-5 * g.cz // per)


def relay_blocks(g):
    return 3 * DEPTH * (g.X // LANES) + g.YE // ROWS


def extend_kernel(g, *refs):
    n = 3
    src = refs[:n]
    y_in = refs[n : n + g.ysides]
    n += g.ysides
    x_in = refs[n : n + g.xsides]
    n += g.xsides
    outs = refs[n : n + 3]
    hy, ly, xh, xl = refs[n + 3 :]
    zi, yi, xi = g.where()
    gather_rows(g, yi, y_in, hy, ly)
    gather_strips(g, xi, x_in, hy, ly, xh, xl)
    lane = lane_of((g.YE, LANES))
    for q in range(3):
        for z in range(g.Z):
            outs[q][z, : g.Y, : g.X] = src[q][z]
            outs[q][z, g.Y :, : g.X] = row_halo(g, hy, ly, q, z)
            block, at = g.slot(q, z)
            hi = roll(xh[block], -at, 1)
            lo = roll(xl[block], -at - DEPTH, 1)
            outs[q][z, :, g.X :] = jnp.where(
                lane < DEPTH, hi, jnp.where(lane >= LANES - DEPTH, lo, 0.0)
            )


def sweep_range(g, zi, sweep):
    reach = SWEEPS - sweep
    low = jnp.where(zi > 0, DEPTH - reach, DEPTH)
    high = jnp.where(zi < g.nz - 1, DEPTH + g.Z + reach, DEPTH + g.Z)
    return low, high


def weights_kernel(g, *refs):
    own = refs[:3]
    n = 3
    z_in = refs[n : n + g.zsides]
    n += g.zsides
    relay = refs[n : n + g.zsides]
    n += g.zsides
    pe, se, fz, fy, fx, dinv = refs[n : n + 6]
    ke = refs[n + 6]
    zi, yi, xi = g.where()
    Z, Y, X = g.Z, g.Y, g.X
    ext = (pe, ke, se)
    for q in range(3):
        ext[q][DEPTH : DEPTH + Z] = own[q][...]
    zero = jnp.zeros((g.YE, g.XE), F32)
    lane = lane_of((g.YE, LANES))
    for side in range(g.zsides):
        base = coarse_blocks(g) if side == 0 else 0
        above = (zi % 2) == side

        def fill(top, side=side, base=base):
            first = DEPTH + Z if top else 0
            for q in range(3):
                for d in range(DEPTH):
                    if q < 2:
                        at = q * DEPTH + d
                    else:
                        at = 2 * DEPTH + (d if top else d - 1)
                        if (top and d == DEPTH - 1) or (not top and d == 0):
                            ext[q][first + d] = zero
                            continue
                    ext[q][first + d, :Y, :X] = z_in[side][at]
                    for part in range(X // LANES):
                        ext[q][first + d, Y:, part * LANES : (part + 1) * LANES] = relay[side][
                            base + (q * DEPTH + d) * (X // LANES) + part
                        ]
                    strip = relay[side][base + 3 * DEPTH * (X // LANES) :].reshape(g.YE, LANES)
                    at_hi = (q * DEPTH + d) * DEPTH
                    at_lo = ((3 + q) * DEPTH + d) * DEPTH
                    hi = roll(strip, -at_hi, 1)
                    lo = roll(strip, -at_lo - DEPTH, 1)
                    ext[q][first + d, :, X:] = jnp.where(
                        lane < DEPTH, hi, jnp.where(lane >= LANES - DEPTH, lo, 0.0)
                    )

        pl.when(above & (zi < g.nz - 1))(functools.partial(fill, True))
        pl.when(jnp.logical_not(above) & (zi > 0))(functools.partial(fill, False))

    @pl.when(zi == 0)
    def _():
        pe[DEPTH - 1] = zero
        ke[DEPTH - 1] = zero

    @pl.when(zi == g.nz - 1)
    def _():
        pe[DEPTH + Z] = zero
        ke[DEPTH + Z] = zero

    low, high = sweep_range(g, zi, 1)
    fz[low] = face(ke[low], ke[low - 1])

    def body(z, carry):
        kz = ke[z]
        above = face(ke[z + 1], kz)
        fz[z + 1] = above
        wy = face(kz, roll(kz, 1, 0))
        wx = face(kz, roll(kz, 1, 1))
        fy[z] = wy
        fx[z] = wx
        total = fz[z] + above + wy + roll(wy, -1, 0) + wx + roll(wx, -1, 1)
        dinv[z] = jnp.where(kz > 0.0, OMEGA / total, 0.0)
        return carry

    lax.fori_loop(low, high, body, 0)


def sweep_kernel(g, sweep, *refs):
    v, s, fz, fy, fx, dinv, out = refs
    zi, yi, xi = g.where()
    final = sweep == SWEEPS
    low, high = sweep_range(g, zi, sweep)

    def body(z, carry):
        vz = v[z]
        wy, wx = fy[z], fx[z]
        total = s[z] + fz[z] * v[z - 1] + fz[z + 1] * v[z + 1]
        total = total + wy * roll(vz, 1, 0) + roll(wy * vz, -1, 0)
        total = total + wx * roll(vz, 1, 1) + roll(wx * vz, -1, 1)
        new = (1.0 - OMEGA) * vz + dinv[z] * total
        if final:
            out[z - DEPTH] = new[: g.Y, : g.X]
        else:
            out[z] = new
        return carry

    lax.fori_loop(low, high, body, 0)
    if not final:
        zero = jnp.zeros((g.YE, g.XE), F32)

        @pl.when(zi == 0)
        def _():
            out[DEPTH - 1] = zero

        @pl.when(zi == g.nz - 1)
        def _():
            out[DEPTH + g.Z] = zero


def solve_kernel(g, gathered, fine, out):
    zi, yi, xi = g.where()
    per = LANES // g.cx
    group = lane_of((ROWS, LANES)) // g.cx

    def relative(a, b, c):
        d = jnp.bitwise_xor(a, zi) + g.nz * jnp.bitwise_xor(b, yi)
        e = jnp.bitwise_xor(c, xi)
        rev = 0
        bits = g.nx.bit_length() - 1
        for bit in range(bits):
            rev = rev + ((e >> bit) & 1) * (1 << (bits - 1 - bit))
        return d + g.nz * g.ny * rev

    layers = g.nz * g.cz
    height = g.ny * g.cy
    fields = []
    for q in range(5):
        planes = []
        for layer in range(layers):
            a, cz = divmod(layer, g.cz)
            m = q * g.cz + cz
            tiles = []
            for b in range(g.ny):
                value = gathered[relative(a, b, 0), m // per]
                for c in range(1, g.nx):
                    value = jnp.where(
                        group == (m % per + c) % per, gathered[relative(a, b, c), m // per], value
                    )
                tiles.append(roll(value, -(m % per) * g.cx, 1))
            planes.append(jnp.concatenate(tiles, axis=0))
        fields.append(planes)
    rhs, diagonal, wz, wy, wx = fields
    shape = (height, LANES)
    zero = jnp.zeros(shape, F32)
    wz = [zero] + wz[1:]
    wy = [jnp.where(row_of(shape) == 0, 0.0, w) for w in wy]
    wx = [jnp.where(lane_of(shape) == 0, 0.0, w) for w in wx]
    scale = [OMEGA_COARSE / d for d in diagonal]

    def flux(e):
        result = []
        for i in range(layers):
            total = wy[i] * roll(e[i], 1, 0) + roll(wy[i] * e[i], -1, 0)
            total = total + wx[i] * roll(e[i], 1, 1) + roll(wx[i] * e[i], -1, 1)
            if i > 0:
                total = total + wz[i] * e[i - 1]
            if i < layers - 1:
                total = total + wz[i + 1] * e[i + 1]
            result.append(total)
        return result

    e = [sc * r for sc, r in zip(scale, rhs)]
    for _ in range(COARSE_SWEEPS - 1):
        f = flux(e)
        e = [(1.0 - OMEGA_COARSE) * e[i] + scale[i] * (rhs[i] + f[i]) for i in range(layers)]
    f = flux(e)
    left = zero
    total = zero
    for i in range(layers):
        left = left + (rhs[i] - diagonal[i] * e[i] + f[i])
        total = total + diagonal[i]
    shift = jnp.sum(left) / jnp.sum(total)

    own = []
    for cz in range(g.cz):
        mine = jnp.zeros((ROWS, LANES), F32)
        for a in range(g.nz):
            for b in range(g.ny):
                here = (zi == a) & (yi == b)
                mine = jnp.where(here, e[a * g.cz + cz][b * ROWS : (b + 1) * ROWS], mine)
        own.append(mine)
    onehot = (
        lax.broadcasted_iota(jnp.int32, (LANES, g.X), 0)
        == xi * g.cx + lax.broadcasted_iota(jnp.int32, (LANES, g.X), 1) // RATIO
    ).astype(jnp.bfloat16)
    wide = exact_dot(jnp.concatenate(own, axis=0), onehot) + shift
    for cz in range(g.cz):
        block = wide[cz * ROWS : (cz + 1) * ROWS]
        spread = jnp.broadcast_to(block[:, None, :], (g.cy, RATIO, g.X)).reshape(g.Y, g.X)
        for z in range(cz * RATIO, (cz + 1) * RATIO):
            out[z] = fine[z] + spread


def exchange(bufs, axis, count):
    return [lax.ppermute(b, axis, pairs(count, odd)) for odd, b in enumerate(bufs)]


def shards(pressure_start, source, permeability):
    g = Grid(pressure_start.shape)
    Z, Y, X = g.Z, g.Y, g.X
    fields = [on_chip(a) for a in (pressure_start, permeability, source)]
    z_shape = (3 * DEPTH - 1, Y, X)
    x_shape = (g.blocks, Y, LANES)
    y_shape = (3 * Z // 2 + 1, ROWS, X)
    sent = run(
        functools.partial(pack_kernel, g),
        [z_shape] * g.zsides + [x_shape] * g.xsides,
        fields,
        name="pack_faces",
    )
    z_sent, x_sent = sent[: g.zsides], sent[g.zsides :]
    z_got = exchange(z_sent, "gx", g.nz)
    x_got = exchange(x_sent, "gz", g.nx)
    y_sent = run(
        functools.partial(pack_rows_kernel, g), [y_shape] * g.ysides, fields + x_got, name="pack_rows"
    )
    y_got = exchange(y_sent, "gy", g.ny)

    halo_scratch = [
        pltpu.VMEM(y_shape, F32),
        pltpu.VMEM(y_shape, F32),
        pltpu.VMEM((g.blocks, g.YE, LANES), F32),
        pltpu.VMEM((g.blocks, g.YE, LANES), F32),
    ]
    nc, nr = coarse_blocks(g), relay_blocks(g)
    packed = run(
        functools.partial(restrict_kernel, g),
        [(nc + nr, ROWS, LANES)] + [(nr, ROWS, LANES)] * (g.zsides - 1),
        fields + z_got + y_got + x_got + list(x_sent),
        scratch=halo_scratch,
        name="restrict",
    )
    relay = exchange(packed, "gx", g.nz)
    cells = jnp.stack([packed[0][:nc], relay[0][:nc]])
    bit = 2
    while bit < g.nz:
        cells = jnp.concatenate([cells, lax.ppermute(cells, "gx", flips(g.nz, bit))])
        bit *= 2
    bit = 1
    while bit < g.ny:
        cells = jnp.concatenate([cells, lax.ppermute(cells, "gy", flips(g.ny, bit))])
        bit *= 2
    bit = g.nx // 2
    while bit >= 1:
        cells = jnp.concatenate([cells, lax.ppermute(cells, "gz", flips(g.nx, bit))])
        bit //= 2

    own = (Z, g.YE, g.XE)
    ext = (g.ZE, g.YE, g.XE)
    extended = run(
        functools.partial(extend_kernel, g),
        [own] * 3,
        fields + y_got + x_got,
        scratch=halo_scratch,
        name="extend",
    )
    pe, se, fz, fy, fx, dinv = run(
        functools.partial(weights_kernel, g),
        [ext] * 6,
        list(extended) + z_got + relay,
        scratch=[pltpu.VMEM(ext, F32)],
        name="weights",
    )
    v = pe
    for sweep in range(1, SWEEPS + 1):
        shape = (Z, Y, X) if sweep == SWEEPS else ext
        (v,) = run(
            functools.partial(sweep_kernel, g, sweep),
            [shape],
            [v, se, fz, fy, fx, dinv],
            name=f"sweep_{sweep}",
        )
    (out,) = run(
        functools.partial(solve_kernel, g),
        [(Z, Y, X)],
        [cells, v],
        name="solve",
        out_spaces=[jax.ShapeDtypeStruct((Z, Y, X), F32)],
    )
    return out


def solution(mesh):
    return jax.shard_map(
        shards,
        mesh=mesh,
        in_specs=(P("gx", "gy", "gz"), P("gx", "gy", "gz"), P("gx", "gy", "gz")),
        out_specs=P("gx", "gy", "gz"),
        check_vma=False,
    )
```

```python
import functools

import jax
import jax.numpy as jnp
from jax import lax
from jax.experimental import pallas as pl
from jax.experimental.pallas import tpu as pltpu
from jax.sharding import PartitionSpec as P

RATIO = 8
SWEEPS = 4
COARSE_SWEEPS = 8
OMEGA = 0.8
OMEGA_COARSE = 0.8

LANES = 128
ROWS = 8
DEPTH = SWEEPS
SLOTS = LANES // DEPTH
F32 = jnp.float32
VMEM_LIMIT = 12 * 1024 * 1024


def pairs(count, odd):
    start = 1 if odd else 0
    out = []
    for low in range(start, count + start - 1, 2):
        high = (low + 1) % count
        out += [(low, high), (high, low)]
    return out


def spread_pairs(outer, inner):
    out = []
    for i in range(outer):
        for j in range(inner):
            if i in (0, outer - 1):
                target = i * inner + (j ^ 1)
            else:
                target = (i + 1 if i % 2 else i - 1) * inner + j
            out.append((i * inner + j, target))
    return out


def flips(count, bit):
    return [(i, i ^ bit) for i in range(count)]


def on_chip(value):
    return pltpu.with_memory_space_constraint(value, pltpu.VMEM)


def run(kernel, outs, args, scratch=(), us=1.0, name=None, spaces=None, far=False, aliases=None):
    whole = pl.BlockSpec(memory_space=pltpu.VMEM)
    shapes = [pltpu.VMEM(shape, F32) for shape in outs] if spaces is None else spaces
    return pl.pallas_call(
        kernel,
        out_shape=shapes,
        in_specs=[pl.BlockSpec(memory_space=pltpu.HBM) if far else whole] * len(args),
        out_specs=[whole] * len(outs),
        scratch_shapes=list(scratch),
        input_output_aliases=aliases or {},
        compiler_params=pltpu.CompilerParams(vmem_limit_bytes=VMEM_LIMIT),
        cost_estimate=pl.CostEstimate(
            flops=1000, bytes_accessed=int(us * 3_500_000), transcendentals=0
        ),
        name=name,
    )(*[pltpu.with_memory_space_constraint(a, pltpu.HBM) if far else on_chip(a) for a in args])


def lane_of(shape):
    return lax.broadcasted_iota(jnp.int32, shape, len(shape) - 1)


def row_of(shape):
    return lax.broadcasted_iota(jnp.int32, shape, len(shape) - 2)


def roll(values, shift, axis):
    size = values.shape[axis]
    if isinstance(shift, int):
        shift = shift % size
        if shift == 0:
            return values
    return pltpu.roll(values, shift, axis)


def face(one, other):
    half = jnp.where(jnp.minimum(one, other) > 0.0, 0.5, 1.0)
    return half * (one + other)


def group_rows(values):
    rows, width = values.shape
    return values.reshape(rows // RATIO, RATIO, width).sum(axis=1)


def split3(values):
    a = values.astype(jnp.bfloat16)
    rest = values - a.astype(F32)
    b = rest.astype(jnp.bfloat16)
    c = (rest - b.astype(F32)).astype(jnp.bfloat16)
    return jnp.concatenate([a, b, c], axis=0)


def exact_dot(values, onehot):
    rows = values.shape[0]
    out = jnp.dot(split3(values), onehot, preferred_element_type=F32)
    return out[:rows] + out[rows : 2 * rows] + out[2 * rows :]


class Grid:
    def __init__(self, shape):
        self.Z, self.Y, self.X = shape
        self.nz, self.ny, self.nx = (lax.axis_size("gx"), lax.axis_size("gy"), lax.axis_size("gz"))
        self.cz, self.cy, self.cx = (n // RATIO for n in shape)
        self.blocks = -(-3 * self.Z // SLOTS)
        self.XE = self.X + LANES
        self.YE = self.Y + ROWS
        self.ZE = self.Z + 2 * DEPTH
        self.zsides = 1 if self.nz == 2 else 2
        self.ysides = 1 if self.ny == 2 else 2
        self.xsides = 1 if self.nx == 2 else 2
        assert 2 * DEPTH == ROWS and 2 * self.Z <= SLOTS and self.Z % 2 == 0
        assert self.blocks * LANES <= self.X and self.cy == ROWS
        assert self.cx * self.nx == LANES

    def where(self):
        return lax.axis_index("gx"), lax.axis_index("gy"), lax.axis_index("gz")

    def steps(self):
        bits = [("gx", 1 << i) for i in range(1, self.nz.bit_length() - 1)]
        bits += [("gy", 1 << i) for i in reversed(range(1, self.ny.bit_length() - 1))]
        bits += [("gz", 1 << i) for i in reversed(range(1, self.nx.bit_length() - 1))]
        return bits + [("gy", 1), ("gz", 1)]

    def slot(self, q, z):
        index = q * self.Z + z
        return index // SLOTS, (index % SLOTS) * DEPTH


def pack_kernel(g, *refs):
    src = refs[:3]
    fields = refs[3:6]
    n = 6
    near = refs[n : n + g.zsides]
    n += g.zsides
    deep = refs[n : n + g.zsides]
    n += g.zsides
    x_out = refs[n : n + g.xsides]
    sems = refs[n + g.xsides]
    zi, yi, xi = g.where()
    copies = []

    def send(q, at, size, out, place):
        source = src[q].at[pl.ds(at, size)]
        target = out.at[pl.ds(place, size)]
        copies.append(pltpu.make_async_copy(source, target, sems.at[3 + len(copies)]))

    rest = DEPTH - 1
    for side in range(g.zsides):
        high = (zi % 2) == side
        for q in range(2):
            send(q, jnp.where(high, g.Z - 1, 0), 1, near[side], q)
        for q in range(3):
            first = jnp.where(high, g.Z - rest if q == 2 else g.Z - DEPTH, 0 if q == 2 else 1)
            send(q, first, rest, deep[side], q * rest)
    loads = [pltpu.make_async_copy(src[q], fields[q], sems.at[q]) for q in range(3)]
    for copy in loads + copies:
        copy.start()
    lane = lane_of((g.Y, LANES))
    hi_pack = [jnp.zeros((g.Y, LANES), F32) for _ in range(g.blocks)]
    lo_pack = list(hi_pack)
    for q in range(3):
        loads[q].wait()
        for z in range(g.Z):
            block, at = g.slot(q, z)
            keep = (lane >= at) & (lane < at + DEPTH)
            moved = roll(fields[q][z, :, g.X - LANES :], at + DEPTH, 1)
            hi_pack[block] = jnp.where(keep, moved, hi_pack[block])
            moved = roll(fields[q][z, :, :LANES], at, 1)
            lo_pack[block] = jnp.where(keep, moved, lo_pack[block])
    even = (xi % 2) == 0
    for block in range(g.blocks):
        for side, out in enumerate(x_out):
            out[block] = jnp.where(even == (side == 0), hi_pack[block], lo_pack[block])
    for copy in copies:
        copy.wait()


def pick(first, second, even, inside):
    if second is None:
        return jnp.where(even & inside, first, 0.0)
    return jnp.where(inside, jnp.where(even, first, second), 0.0)


def from_high(index, count, bufs, view):
    even = (index % 2) == 0
    second = view(bufs[1]) if len(bufs) > 1 else None
    return pick(view(bufs[0]), second, even, index < count - 1)


def from_low(index, count, bufs, view):
    odd = (index % 2) == 1
    second = view(bufs[1]) if len(bufs) > 1 else None
    return pick(view(bufs[0]), second, odd, index > 0)


def pack_rows_kernel(g, *refs):
    src = refs[:3]
    x_in = refs[3 : 3 + g.xsides]
    y_out = refs[3 + g.xsides + g.zsides :]
    zi, yi, xi = g.where()
    half = g.Z // 2
    last = g.Y - ROWS
    for side, out in enumerate(y_out):
        high = (yi % 2) == side

        def fill(top, out=out):
            for q in range(3):
                for pair in range(half):
                    a, b = src[q][2 * pair], src[q][2 * pair + 1]
                    if top:
                        part = jnp.concatenate([a[g.Y - DEPTH :], b[g.Y - DEPTH :]], axis=0)
                    else:
                        part = jnp.concatenate([a[:DEPTH], b[:DEPTH]], axis=0)
                    out[q * half + pair] = part
            rows = slice(g.Y - DEPTH, g.Y) if top else slice(0, DEPTH)
            for block in range(g.blocks):
                hi = from_high(xi, g.nx, x_in, lambda r: r[block, rows, :])
                lo = from_low(xi, g.nx, x_in, lambda r: r[block, rows, :])
                out[3 * half, :, block * LANES : (block + 1) * LANES] = jnp.concatenate(
                    [hi, lo], axis=0
                )

        pl.when(high)(functools.partial(fill, True))
        pl.when(jnp.logical_not(high))(functools.partial(fill, False))


def gather_rows(g, yi, y_in, hy, ly):
    hy[...] = from_high(yi, g.ny, y_in, lambda r: r[...])
    ly[...] = from_low(yi, g.ny, y_in, lambda r: r[...])


def gather_strips(g, xi, x_in, hy, ly, xh, xl):
    half = g.Z // 2
    for block in range(g.blocks):
        lanes = slice(block * LANES, (block + 1) * LANES)
        xh[block, : g.Y] = from_high(xi, g.nx, x_in, lambda r: r[block])
        xl[block, : g.Y] = from_low(xi, g.nx, x_in, lambda r: r[block])
        top, low = hy[3 * half, :, lanes], ly[3 * half, :, lanes]
        xh[block, g.Y :] = jnp.concatenate([top[:DEPTH], low[:DEPTH]], axis=0)
        xl[block, g.Y :] = jnp.concatenate([top[DEPTH:], low[DEPTH:]], axis=0)


def row_halo(g, hy, ly, q, z):
    half = g.Z // 2
    at = (z % 2) * DEPTH
    block = q * half + z // 2
    return jnp.concatenate([hy[block, at : at + DEPTH], ly[block, at : at + DEPTH]], axis=0)


def restrict_kernel(g, *refs):
    n = 3
    src = refs[:n]
    z_in = refs[n : n + g.zsides]
    n += g.zsides
    y_in = refs[n : n + g.ysides]
    n += g.ysides
    x_in = refs[n : n + g.xsides]
    n += g.xsides
    x_own = refs[n : n + g.xsides]
    n += g.xsides
    outs = refs[n : n + g.zsides]
    n += g.zsides
    hy, ly, xh, xl = refs[n:]
    p, k, s = src
    zi, yi, xi = g.where()
    gather_rows(g, yi, y_in, hy, ly)
    gather_strips(g, xi, x_in, hy, ly, xh, xl)
    Z, Y, X = g.Z, g.Y, g.X
    half = Z // 2

    zero = jnp.zeros((Y, X), F32)
    flux_z, weight_z = [], []
    for layer in range(0, Z + 1, RATIO):
        if layer == 0:
            p0 = from_low(zi, g.nz, z_in, lambda r: r[0])
            k0 = from_low(zi, g.nz, z_in, lambda r: r[1])
        else:
            p0, k0 = p[layer - 1], k[layer - 1]
        if layer == Z:
            p1 = from_high(zi, g.nz, z_in, lambda r: r[0])
            k1 = from_high(zi, g.nz, z_in, lambda r: r[1])
        else:
            p1, k1 = p[layer], k[layer]
        w = face(k0, k1)
        weight_z.append(group_rows(w))
        flux_z.append(group_rows(w * (p1 - p0)))

    lane = lane_of((Y, LANES))
    even = (xi % 2) == 0
    if g.xsides == 1:
        own_hi = own_lo = x_own[0][0]
    else:
        own_hi = jnp.where(even, x_own[0][0], x_own[1][0])
        own_lo = jnp.where(even, x_own[1][0], x_own[0][0])

    def side_sums(own, other, lane_in, flip):
        wk = face(roll(own, -Z * DEPTH, 1), roll(other, -Z * DEPTH, 1))
        diff = (other - own) if flip else (own - other)
        keep = (lane % DEPTH == lane_in) & (lane < Z * DEPTH)
        w = jnp.where(keep, wk, 0.0)
        result = []
        for value in (w, w * diff):
            total = group_rows(value)
            step = DEPTH
            while step < RATIO * DEPTH:
                total = total + roll(total, -step, 1)
                step *= 2
            result.append(total)
        return result

    low_w, low_f = side_sums(own_lo, roll(xl[0, :Y], -(DEPTH - 1), 1), 0, False)
    high_w, high_f = side_sums(own_hi, roll(xh[0, :Y], DEPTH - 1, 1), DEPTH - 1, True)
    lane8 = lane_of((ROWS, X))
    row8 = row_of((ROWS, X))
    row = row_of((Y, X))
    inner = (lane8 % RATIO == 0) & (lane8 > 0)

    def widen(value, at, cell):
        moved = roll(value, (at % LANES) - cell, 1)
        wide = jnp.concatenate([moved] * (X // LANES), axis=1)
        return jnp.where(lane8 == at, wide, 0.0)

    rows = []
    for cz in range(g.cz):
        acc_s = zero
        acc_w = zero
        acc_f = zero
        acc_wy = zero
        acc_fy = zero
        low_wy = low_fy = top_w = top_f = jnp.zeros((1, X), F32)
        for z in range(cz * RATIO, (cz + 1) * RATIO):
            pz, kz = p[z], k[z]
            acc_s = acc_s + s[z]
            w = 0.5 * (kz + roll(kz, 1, 1))
            acc_w = acc_w + w
            acc_f = acc_f + w * (pz - roll(pz, 1, 1))
            w = 0.5 * (kz + roll(kz, 1, 0))
            acc_wy = acc_wy + w
            acc_fy = acc_fy + w * (pz - roll(pz, 1, 0))
            at = (z % 2) * DEPTH
            below = [ly[q * half + z // 2, at + DEPTH - 1 : at + DEPTH, :] for q in range(2)]
            above = [hy[q * half + z // 2, at : at + 1, :] for q in range(2)]
            w = face(kz[:1], below[1])
            low_wy = low_wy + w
            low_fy = low_fy + w * (pz[:1] - below[0])
            w = face(kz[Y - 1 :], above[1])
            top_w = top_w + w
            top_f = top_f + w * (above[0] - pz[Y - 1 :])

        def lower(acc, low):
            kept = group_rows(jnp.where(row % RATIO == 0, acc, 0.0))
            return jnp.where(row8 == 0, jnp.broadcast_to(low, (ROWS, X)), kept)

        weight_y = lower(acc_wy, low_wy)
        flux_y = lower(acc_fy, low_fy)

        def upper(values, top):
            return jnp.where(
                row8 == g.cy - 1, jnp.broadcast_to(top, (ROWS, X)), roll(values, -1, 0)
            )

        weight_x = jnp.where(inner, group_rows(acc_w), 0.0)
        flux_x = jnp.where(inner, group_rows(acc_f), 0.0)
        cell = cz * RATIO * DEPTH
        x_low = widen(low_w, 0, cell)
        x_high = widen(high_w, X - 1, cell + DEPTH - 1)
        f_low = widen(low_f, 0, cell)
        f_high = widen(high_f, X - 1, cell + DEPTH - 1)
        rhs = (
            group_rows(acc_s)
            - (flux_z[cz] - flux_z[cz + 1])
            - (flux_y - upper(flux_y, top_f))
            - (flux_x - roll(flux_x, -1, 1))
            - (f_low - f_high)
        )
        diagonal = (
            weight_z[cz]
            + weight_z[cz + 1]
            + weight_y
            + upper(weight_y, top_w)
            + weight_x
            + roll(weight_x, -1, 1)
            + x_low
            + x_high
        )
        rows.append([rhs, diagonal, weight_z[cz], weight_y, weight_x + x_low])

    items = [rows[cz][q] for q in range(5) for cz in range(g.cz)]
    onehot = (
        lax.broadcasted_iota(jnp.int32, (X, LANES), 0) // RATIO
        == lax.broadcasted_iota(jnp.int32, (X, LANES), 1)
    ).astype(jnp.bfloat16)
    summed = exact_dot(jnp.concatenate(items, axis=0), onehot)
    per = LANES // g.cx
    cells = [jnp.zeros((ROWS, LANES), F32) for _ in range(coarse_blocks(g))]
    for m in range(len(items)):
        place = lax.rem(m % per + xi, per) * g.cx
        cells[m // per] = cells[m // per] + pltpu.roll(
            summed[m * ROWS : (m + 1) * ROWS], place, 1
        )
    for block, value in enumerate(cells):
        outs[0][block] = value

    for side, out in enumerate(outs):
        base = coarse_blocks(g) if side == 0 else 0
        high = (zi % 2) == side

        def fill(top, out=out, base=base):
            first = Z - DEPTH if top else 0
            for q in range(3):
                for d in range(DEPTH):
                    part = row_halo(g, hy, ly, q, first + d)
                    for half_lane in range(X // LANES):
                        out[base + (q * DEPTH + d) * (X // LANES) + half_lane] = part[
                            :, half_lane * LANES : (half_lane + 1) * LANES
                        ]
            at_block = base + 3 * DEPTH * (X // LANES)
            wide = lane_of((g.YE, LANES))
            acc = jnp.zeros((g.YE, LANES), F32)
            span = DEPTH * DEPTH
            for piece, (ref, q) in enumerate((r, q) for r in (xh, xl) for q in range(3)):
                block, lane_at = g.slot(q, first)
                moved = roll(ref[block], piece * span - lane_at, 1)
                acc = jnp.where((wide >= piece * span) & (wide < (piece + 1) * span), moved, acc)
            out[at_block:] = acc.reshape(g.YE // ROWS, ROWS, LANES)

        pl.when(high)(functools.partial(fill, True))
        pl.when(jnp.logical_not(high))(functools.partial(fill, False))


def coarse_blocks(g):
    per = LANES // g.cx
    return -(-5 * g.cz // per)


def relay_blocks(g):
    return 3 * DEPTH * (g.X // LANES) + g.YE // ROWS


def strip_tile(g, hi, lo):
    lane = lane_of((g.YE, LANES))
    return jnp.where(lane < DEPTH, hi, jnp.where(lane >= LANES - DEPTH, lo, 0.0))


def side_faces(kz):
    wy = face(kz, roll(kz, 1, 0))
    wx = face(kz, roll(kz, 1, 1))
    return wy, wx, wy + roll(wy, -1, 0) + wx + roll(wx, -1, 1)


def scale_of(kz, total):
    return jnp.where(kz > 0.0, OMEGA / total, 0.0)


def extend_kernel(g, *refs):
    n = 3
    src = refs[:n]
    y_in = refs[n : n + g.ysides]
    n += g.ysides
    x_in = refs[n : n + g.xsides]
    n += g.xsides
    pe, ke, se, fz, fy, fx, dinv, token = refs[n : n + 8]
    hy, ly, xh, xl = refs[n + 8 :]
    token[...] = jnp.zeros((ROWS, LANES), F32)
    zi, yi, xi = g.where()
    gather_rows(g, yi, y_in, hy, ly)
    gather_strips(g, xi, x_in, hy, ly, xh, xl)
    for q, out in enumerate((pe, ke, se)):
        for z in range(g.Z):
            out[z, : g.Y, : g.X] = src[q][z]
            out[z, g.Y :, : g.X] = row_halo(g, hy, ly, q, z)
            block, at = g.slot(q, z)
            hi = roll(xh[block], -at, 1)
            lo = roll(xl[block], -at - DEPTH, 1)
            out[z, :, g.X :] = strip_tile(g, hi, lo)
    fy[0], fx[0], _ = side_faces(ke[0])
    fz[1] = face(ke[1], ke[0])

    def body(z, carry):
        kz = ke[z]
        above = face(ke[z + 1], kz)
        fz[z + 1] = above
        wy, wx, total = side_faces(kz)
        fy[z] = wy
        fx[z] = wx
        dinv[z] = scale_of(kz, total + fz[z] + above)
        return carry

    lax.fori_loop(1, g.Z - 1, body, 0)
    fy[g.Z - 1], fx[g.Z - 1], _ = side_faces(ke[g.Z - 1])


def halo_kernel(g, *refs):
    ke, fy, fx, fz = refs[:4]
    n = 4
    near = refs[n : n + g.zsides]
    n += g.zsides
    deep = refs[n : n + g.zsides]
    n += g.zsides
    relay = refs[n : n + g.zsides]
    n += g.zsides
    ph, sh, hz, hy, hx, hd = refs[n : n + 6]
    kh = refs[n + 6]
    zi, yi, xi = g.where()
    Z, Y, X = g.Z, g.Y, g.X
    parts = X // LANES
    zero = jnp.zeros((g.YE, g.XE), F32)

    def k_at(z):
        return ke[z] if 0 <= z < Z else kh[z + DEPTH if z < 0 else z - Z + DEPTH]

    def own_faces(z):
        wy, wx = fy[z], fx[z]
        return wy + roll(wy, -1, 0) + wx + roll(wx, -1, 1)

    def fill(top, side):
        base = coarse_blocks(g) if side == 0 else 0
        first = DEPTH if top else 0
        strip = relay[side][base + 3 * DEPTH * parts :].reshape(g.YE, LANES)
        for q, out in enumerate((ph, kh, sh)):
            for d in range(DEPTH):
                rest = DEPTH - 1
                if q < 2 and d == (0 if top else rest):
                    plane = near[side][q]
                elif q < 2:
                    plane = deep[side][q * rest + (d - 1 if top else d)]
                elif d == (rest if top else 0):
                    continue
                else:
                    plane = deep[side][q * rest + (d if top else d - 1)]
                out[first + d, :Y, :X] = plane
                for part in range(parts):
                    lanes = slice(part * LANES, (part + 1) * LANES)
                    out[first + d, Y:, lanes] = relay[side][base + (q * DEPTH + d) * parts + part]
                hi = roll(strip, -(q * DEPTH + d) * DEPTH, 1)
                lo = roll(strip, -((3 + q) * DEPTH + d) * DEPTH - DEPTH, 1)
                out[first + d, :, X:] = strip_tile(g, hi, lo)
        if top:
            layers = range(Z, Z + DEPTH - 1)
            kz = k_at(Z - 1)
            below = face(k_at(Z), kz)
            hz[DEPTH] = below
            hd[DEPTH] = scale_of(kz, own_faces(Z - 1) + fz[Z - 1] + below)
            for z in layers:
                kz = k_at(z)
                above = face(k_at(z + 1), kz)
                hz[z + 1 - Z + DEPTH] = above
                wy, wx, total = side_faces(kz)
                hy[z - Z + DEPTH] = wy
                hx[z - Z + DEPTH] = wx
                hd[z + 1 - Z + DEPTH] = scale_of(kz, total + below + above)
                below = above
        else:
            kz = k_at(0)
            above = face(kz, k_at(-1))
            hz[DEPTH - 1] = above
            hd[DEPTH - 1] = scale_of(kz, own_faces(0) + fz[1] + above)
            for z in range(-1, -DEPTH, -1):
                kz = k_at(z)
                below = face(kz, k_at(z - 1))
                hz[z + DEPTH - 1] = below
                wy, wx, total = side_faces(kz)
                hy[z + DEPTH] = wy
                hx[z + DEPTH] = wx
                hd[z + DEPTH - 1] = scale_of(kz, total + below + above)
                above = below

    for side in range(g.zsides):
        above = (zi % 2) == side
        pl.when(above & (zi < g.nz - 1))(functools.partial(fill, True, side))
        pl.when(jnp.logical_not(above) & (zi > 0))(functools.partial(fill, False, side))

    @pl.when(zi == 0)
    def _():
        ph[DEPTH - 1] = zero
        kz = ke[0]
        hz[DEPTH - 1] = kz
        hd[DEPTH - 1] = scale_of(kz, own_faces(0) + fz[1] + kz)

    @pl.when(zi == g.nz - 1)
    def _():
        ph[DEPTH] = zero
        kz = ke[Z - 1]
        hz[DEPTH] = kz
        hd[DEPTH] = scale_of(kz, own_faces(Z - 1) + fz[Z - 1] + kz)


def sweep_kernel(g, sweep, *refs):
    v, vh, s, fz, fy, fx, dinv, sh, hz, hy, hx, hd = refs[:12]
    out = refs[12]
    refs[-1][...] = jnp.zeros((ROWS, LANES), F32)
    out_halo = refs[13]
    zi, yi, xi = g.where()
    Z = g.Z
    final = sweep == SWEEPS
    reach = SWEEPS - sweep

    def update(vz, low, high, source, z_low, z_high, wy, wx, scale):
        total = source + z_low * low + z_high * high
        total = total + wy * roll(vz, 1, 0) + roll(wy * vz, -1, 0)
        total = total + wx * roll(vz, 1, 1) + roll(wx * vz, -1, 1)
        return (1.0 - OMEGA) * vz + scale * total

    def store(z, new):
        out[z] = new[: g.Y, : g.X] if final else new

    def pick_layer(own, halo, z):
        return own[z] if 0 <= z < Z else halo[z + DEPTH if z < 0 else z - Z + DEPTH]

    def z_face(z):
        return fz[z] if 1 <= z < Z else hz[z + DEPTH - 1 if z < 1 else z - Z + DEPTH]

    def edge(z):
        scale = dinv[z] if 0 < z < Z - 1 else hd[z + DEPTH - 1 if z < 1 else z - Z + 1 + DEPTH]
        return update(
            pick_layer(v, vh, z),
            pick_layer(v, vh, z - 1),
            pick_layer(v, vh, z + 1),
            pick_layer(s, sh, z),
            z_face(z),
            z_face(z + 1),
            pick_layer(fy, hy, z),
            pick_layer(fx, hx, z),
            scale,
        )

    store(0, edge(0))

    def body(z, carry):
        store(z, update(v[z], v[z - 1], v[z + 1], s[z], fz[z], fz[z + 1], fy[z], fx[z], dinv[z]))
        return carry

    lax.fori_loop(1, Z - 1, body, 0)
    store(Z - 1, edge(Z - 1))
    if final:
        return
    zero = jnp.zeros((g.YE, g.XE), F32)

    def halo(layers):
        for z in layers:
            out_halo[z + DEPTH if z < 0 else z - Z + DEPTH] = edge(z)

    def outside(at):
        out_halo[at] = zero

    pl.when(zi > 0)(functools.partial(halo, range(-reach, 0)))
    pl.when(zi < g.nz - 1)(functools.partial(halo, range(Z, Z + reach)))
    pl.when(zi == 0)(functools.partial(outside, DEPTH - 1))
    pl.when(zi == g.nz - 1)(functools.partial(outside, DEPTH))


def solve_kernel(g, gathered, fine, out):
    zi, yi, xi = g.where()
    per = LANES // g.cx
    group = lane_of((ROWS, LANES)) // g.cx

    order = [("gx", 1)] + g.steps()

    def relative(a, b, c):
        apart = {
            "gx": jnp.bitwise_xor(a, zi),
            "gy": jnp.bitwise_xor(b, yi),
            "gz": jnp.bitwise_xor(c, xi),
        }
        at = 0
        for number, (axis, bit) in enumerate(order):
            at = at + (1 << number) * ((apart[axis] & bit) // bit)
        return at

    layers = g.nz * g.cz
    height = g.ny * g.cy
    fields = []
    for q in range(5):
        planes = []
        for layer in range(layers):
            a, cz = divmod(layer, g.cz)
            m = q * g.cz + cz
            tiles = []
            for b in range(g.ny):
                value = gathered[relative(a, b, 0), m // per]
                for c in range(1, g.nx):
                    value = jnp.where(
                        group == (m % per + c) % per, gathered[relative(a, b, c), m // per], value
                    )
                tiles.append(roll(value, -(m % per) * g.cx, 1))
            planes.append(jnp.concatenate(tiles, axis=0))
        fields.append(planes)
    rhs, diagonal, wz, wy, wx = fields
    shape = (height, LANES)
    zero = jnp.zeros(shape, F32)
    wz = [zero] + wz[1:]
    wy = [jnp.where(row_of(shape) == 0, 0.0, w) for w in wy]
    wx = [jnp.where(lane_of(shape) == 0, 0.0, w) for w in wx]
    scale = [OMEGA_COARSE / d for d in diagonal]

    def flux(e):
        result = []
        for i in range(layers):
            total = wy[i] * roll(e[i], 1, 0) + roll(wy[i] * e[i], -1, 0)
            total = total + wx[i] * roll(e[i], 1, 1) + roll(wx[i] * e[i], -1, 1)
            if i > 0:
                total = total + wz[i] * e[i - 1]
            if i < layers - 1:
                total = total + wz[i + 1] * e[i + 1]
            result.append(total)
        return result

    e = [sc * r for sc, r in zip(scale, rhs)]
    for _ in range(COARSE_SWEEPS - 1):
        f = flux(e)
        e = [(1.0 - OMEGA_COARSE) * e[i] + scale[i] * (rhs[i] + f[i]) for i in range(layers)]
    f = flux(e)
    left = zero
    total = zero
    for i in range(layers):
        left = left + (rhs[i] - diagonal[i] * e[i] + f[i])
        total = total + diagonal[i]
    shift = jnp.sum(left) / jnp.sum(total)

    own = []
    for cz in range(g.cz):
        mine = jnp.zeros((ROWS, LANES), F32)
        for a in range(g.nz):
            for b in range(g.ny):
                here = (zi == a) & (yi == b)
                mine = jnp.where(here, e[a * g.cz + cz][b * ROWS : (b + 1) * ROWS], mine)
        own.append(mine)
    onehot = (
        lax.broadcasted_iota(jnp.int32, (LANES, g.X), 0)
        == xi * g.cx + lax.broadcasted_iota(jnp.int32, (LANES, g.X), 1) // RATIO
    ).astype(jnp.bfloat16)
    wide = exact_dot(jnp.concatenate(own, axis=0), onehot) + shift
    for cz in range(g.cz):
        block = wide[cz * ROWS : (cz + 1) * ROWS]
        spread = jnp.broadcast_to(block[:, None, :], (g.cy, RATIO, g.X)).reshape(g.Y, g.X)
        for z in range(cz * RATIO, (cz + 1) * RATIO):
            out[z] = fine[z] + spread


def merge_kernel(cells, got, token, out):
    count = cells.shape[0]
    out[:count] = cells[...]
    out[count:] = got[...]


def merge(cells, got, token):
    shape = (2 * cells.shape[0],) + cells.shape[1:]
    (out,) = run(merge_kernel, [shape], [cells, got, token], us=0.05, name="merge")
    return out


def exchange(bufs, axis, count, beside=None):
    got = [lax.ppermute(bufs[0], axis, pairs(count, 0))]
    if len(bufs) > 1:
        if beside is None:
            got.append(lax.ppermute(bufs[1], axis, pairs(count, 1)))
        else:
            perm = spread_pairs(count, lax.axis_size(beside))
            got.append(lax.ppermute(bufs[1], (axis, beside), perm))
    return got


def shards(pressure_start, source, permeability):
    g = Grid(pressure_start.shape)
    Z, Y, X = g.Z, g.Y, g.X
    fields = [pressure_start, permeability, source]
    x_shape = (g.blocks, Y, LANES)
    y_shape = (3 * Z // 2 + 1, ROWS, X)
    sent = run(
        functools.partial(pack_kernel, g),
        [(Z, Y, X)] * 3
        + [(2, Y, X)] * g.zsides
        + [(3 * (DEPTH - 1), Y, X)] * g.zsides
        + [x_shape] * g.xsides,
        fields,
        scratch=[pltpu.SemaphoreType.DMA((3 + 5 * g.zsides,))],
        name="pack_faces",
        far=True,
    )
    sent = list(sent)
    fields, near, deep = sent[:3], sent[3 : 3 + g.zsides], sent[3 + g.zsides : 3 + 2 * g.zsides]
    x_sent = sent[3 + 2 * g.zsides :]
    near_got = exchange(near, "gx", g.nz, "gz")
    x_got = exchange(x_sent, "gz", g.nx)
    deep_got = exchange(deep, "gx", g.nz, "gz")
    y_sent = run(
        functools.partial(pack_rows_kernel, g), [y_shape] * g.ysides, fields + x_got + near_got, name="pack_rows"
    )
    y_got = exchange(y_sent, "gy", g.ny, "gz")

    halo_scratch = [
        pltpu.VMEM(y_shape, F32),
        pltpu.VMEM(y_shape, F32),
        pltpu.VMEM((g.blocks, g.YE, LANES), F32),
        pltpu.VMEM((g.blocks, g.YE, LANES), F32),
    ]
    nc, nr = coarse_blocks(g), relay_blocks(g)
    packed = run(
        functools.partial(restrict_kernel, g),
        [(nc + nr, ROWS, LANES)] + [(nr, ROWS, LANES)] * (g.zsides - 1),
        fields + near_got + y_got + x_got + x_sent,
        scratch=halo_scratch,
        name="restrict",
    )
    relay = exchange(packed, "gx", g.nz, "gz")
    tile = (ROWS, LANES)
    own = (Z, g.YE, g.XE)
    far = (2 * DEPTH, g.YE, g.XE)
    pe, ke, se, fz, fy, fx, dinv, token = run(
        functools.partial(extend_kernel, g),
        [own] * 7 + [tile],
        fields + y_got + x_got,
        scratch=halo_scratch,
        us=0.5,
        name="extend",
    )
    ph, sh, hz, hy, hx, hd = run(
        functools.partial(halo_kernel, g),
        [far] * 6,
        [ke, fy, fx, fz] + near_got + deep_got + relay,
        scratch=[pltpu.VMEM(far, F32)],
        us=0.1,
        name="halo",
    )
    cells = merge(packed[0][None, :nc], relay[0][None, :nc], token)
    v, vh = pe, ph
    steps = g.steps()
    for number in range(max(len(steps), SWEEPS)):
        if number < len(steps):
            axis, bit = steps[number]
            got = lax.ppermute(cells, axis, flips(lax.axis_size(axis), bit))
        if number < SWEEPS:
            final = number == SWEEPS - 1
            result = run(
                functools.partial(sweep_kernel, g, number + 1),
                ([(Z, Y, X)] if final else [own, far]) + [tile],
                [v, vh, se, fz, fy, fx, dinv, sh, hz, hy, hx, hd],
                us=0.5,
                name=f"sweep_{number + 1}",
            )
            v, vh, token = result[0], result[1], result[-1]
        if number < len(steps):
            cells = merge(cells, got, token)
    (out,) = run(
        functools.partial(solve_kernel, g),
        [(Z, Y, X)],
        [cells, v],
        us=2.0,
        name="solve",
        spaces=[jax.ShapeDtypeStruct((Z, Y, X), F32)],
    )
    return out


def solution(mesh):
    return jax.shard_map(
        shards,
        mesh=mesh,
        in_specs=(P("gx", "gy", "gz"), P("gx", "gy", "gz"), P("gx", "gy", "gz")),
        out_specs=P("gx", "gy", "gz"),
        check_vma=False,
    )
```

```python
import functools

import jax
import jax.numpy as jnp
from jax import lax
from jax.experimental import pallas as pl
from jax.experimental.pallas import tpu as pltpu
from jax.sharding import PartitionSpec as P

RATIO = 8
SWEEPS = 4
COARSE_SWEEPS = 8
OMEGA = 0.8
OMEGA_COARSE = 0.8

LANES = 128
ROWS = 8
DEPTH = SWEEPS
SLOTS = LANES // DEPTH
F32 = jnp.float32
VMEM_LIMIT = 12 * 1024 * 1024
US = dict(local=1.2, rows=0.1, side=0.8, weights=3.2, restrict=0.6, extend=1.0, halo=1.4, outer=0.8, sweep=2.2, solve=2.2)


def pairs(count, odd):
    start = 1 if odd else 0
    out = []
    for low in range(start, count + start - 1, 2):
        high = (low + 1) % count
        out += [(low, high), (high, low)]
    return out


def spread_pairs(outer, inner):
    out = []
    for i in range(outer):
        for j in range(inner):
            if i in (0, outer - 1):
                target = i * inner + (j ^ 1)
            else:
                target = (i + 1 if i % 2 else i - 1) * inner + j
            out.append((i * inner + j, target))
    return out


def flips(count, bit):
    return [(i, i ^ bit) for i in range(count)]


def on_chip(value):
    return pltpu.with_memory_space_constraint(value, pltpu.VMEM)


def run(kernel, outs, args, scratch=(), us=1.0, name=None, spaces=None, far=False, aliases=None):
    whole = pl.BlockSpec(memory_space=pltpu.VMEM)
    shapes = [pltpu.VMEM(shape, F32) for shape in outs] if spaces is None else spaces
    return pl.pallas_call(
        kernel,
        out_shape=shapes,
        in_specs=[pl.BlockSpec(memory_space=pltpu.HBM) if far else whole] * len(args),
        out_specs=[whole] * len(outs),
        scratch_shapes=list(scratch),
        input_output_aliases=aliases or {},
        compiler_params=pltpu.CompilerParams(vmem_limit_bytes=VMEM_LIMIT),
        cost_estimate=pl.CostEstimate(
            flops=1000, bytes_accessed=int(us * 3_500_000), transcendentals=0
        ),
        name=name,
    )(*[pltpu.with_memory_space_constraint(a, pltpu.HBM) if far else on_chip(a) for a in args])


def lane_of(shape):
    return lax.broadcasted_iota(jnp.int32, shape, len(shape) - 1)


def row_of(shape):
    return lax.broadcasted_iota(jnp.int32, shape, len(shape) - 2)


def roll(values, shift, axis):
    size = values.shape[axis]
    if isinstance(shift, int):
        shift = shift % size
        if shift == 0:
            return values
    return pltpu.roll(values, shift, axis)


def face(one, other):
    half = jnp.where(jnp.minimum(one, other) > 0.0, 0.5, 1.0)
    return half * (one + other)


def group_rows(values):
    rows, width = values.shape
    return values.reshape(rows // RATIO, RATIO, width).sum(axis=1)


def split3(values):
    a = values.astype(jnp.bfloat16)
    rest = values - a.astype(F32)
    b = rest.astype(jnp.bfloat16)
    c = (rest - b.astype(F32)).astype(jnp.bfloat16)
    return jnp.concatenate([a, b, c], axis=0)


def exact_dot(values, onehot):
    rows = values.shape[0]
    out = jnp.dot(split3(values), onehot, preferred_element_type=F32)
    return out[:rows] + out[rows : 2 * rows] + out[2 * rows :]


class Grid:
    def __init__(self, shape):
        self.Z, self.Y, self.X = shape
        self.nz, self.ny, self.nx = (lax.axis_size("gx"), lax.axis_size("gy"), lax.axis_size("gz"))
        self.cz, self.cy, self.cx = (n // RATIO for n in shape)
        self.blocks = -(-3 * self.Z // SLOTS)
        self.XE = self.X + LANES
        self.YE = self.Y + ROWS
        self.ZE = self.Z + 2 * DEPTH
        self.zsides = 1 if self.nz == 2 else 2
        self.ysides = 1 if self.ny == 2 else 2
        self.xsides = 1 if self.nx == 2 else 2
        assert 2 * DEPTH == ROWS and 2 * self.Z <= SLOTS and self.Z % 2 == 0
        assert self.blocks * LANES <= self.X and self.cy == ROWS
        assert self.cx * self.nx == LANES

    def where(self):
        return lax.axis_index("gx"), lax.axis_index("gy"), lax.axis_index("gz")

    def steps(self):
        bits = [("gx", 1 << i) for i in reversed(range(1, self.nz.bit_length() - 1))]
        bits += [("gy", 1 << i) for i in reversed(range(1, self.ny.bit_length() - 1))]
        bits += [("gz", 1 << i) for i in reversed(range(1, self.nx.bit_length() - 1))]
        return bits + [("gy", 1), ("gx", 1), ("gz", 1)]

    def slot(self, q, z):
        index = q * self.Z + z
        return index // SLOTS, (index % SLOTS) * DEPTH


def pack_kernel(g, *refs):
    src = refs[:3]
    fields = refs[3:6]
    n = 6
    near = refs[n : n + g.zsides]
    n += g.zsides
    x_out = refs[n : n + g.xsides]
    sems = refs[n + g.xsides]
    zi, yi, xi = g.where()
    copies = []

    def send(q, at, size, out, place):
        source = src[q].at[pl.ds(at, size)]
        target = out.at[pl.ds(place, size)]
        copies.append(pltpu.make_async_copy(source, target, sems.at[3 + len(copies)]))

    for side in range(g.zsides):
        high = (zi % 2) == side
        for q in range(2):
            send(q, jnp.where(high, g.Z - 1, 0), 1, near[side], q)
    loads = [pltpu.make_async_copy(src[q], fields[q], sems.at[q]) for q in range(3)]
    for copy in loads + copies:
        copy.start()
    lane = lane_of((g.Y, LANES))
    hi_pack = [jnp.zeros((g.Y, LANES), F32) for _ in range(g.blocks)]
    lo_pack = list(hi_pack)
    for q in range(3):
        loads[q].wait()
        for z in range(g.Z):
            block, at = g.slot(q, z)
            keep = (lane >= at) & (lane < at + DEPTH)
            moved = roll(fields[q][z, :, g.X - LANES :], at + DEPTH, 1)
            hi_pack[block] = jnp.where(keep, moved, hi_pack[block])
            moved = roll(fields[q][z, :, :LANES], at, 1)
            lo_pack[block] = jnp.where(keep, moved, lo_pack[block])
    even = (xi % 2) == 0
    for block in range(g.blocks):
        for side, out in enumerate(x_out):
            out[block] = jnp.where(even == (side == 0), hi_pack[block], lo_pack[block])
    for copy in copies:
        copy.wait()


def pick(first, second, even, inside):
    if second is None:
        return jnp.where(even & inside, first, 0.0)
    return jnp.where(inside, jnp.where(even, first, second), 0.0)


def from_high(index, count, bufs, view):
    even = (index % 2) == 0
    second = view(bufs[1]) if len(bufs) > 1 else None
    return pick(view(bufs[0]), second, even, index < count - 1)


def from_low(index, count, bufs, view):
    odd = (index % 2) == 1
    second = view(bufs[1]) if len(bufs) > 1 else None
    return pick(view(bufs[0]), second, odd, index > 0)


def pack_rows_kernel(g, *refs):
    src = refs[:3]
    x_in = refs[3 : 3 + g.xsides]
    y_out = refs[len(refs) - g.ysides :]
    zi, yi, xi = g.where()
    half = g.Z // 2
    last = g.Y - ROWS
    for side, out in enumerate(y_out):
        high = (yi % 2) == side

        def fill(top, out=out):
            for q in range(3):
                for pair in range(half):
                    a, b = src[q][2 * pair], src[q][2 * pair + 1]
                    if top:
                        part = jnp.concatenate([a[g.Y - DEPTH :], b[g.Y - DEPTH :]], axis=0)
                    else:
                        part = jnp.concatenate([a[:DEPTH], b[:DEPTH]], axis=0)
                    out[q * half + pair] = part
            rows = slice(g.Y - DEPTH, g.Y) if top else slice(0, DEPTH)
            for block in range(g.blocks):
                hi = from_high(xi, g.nx, x_in, lambda r: r[block, rows, :])
                lo = from_low(xi, g.nx, x_in, lambda r: r[block, rows, :])
                out[3 * half, :, block * LANES : (block + 1) * LANES] = jnp.concatenate(
                    [hi, lo], axis=0
                )

        pl.when(high)(functools.partial(fill, True))
        pl.when(jnp.logical_not(high))(functools.partial(fill, False))


def gather_rows(g, yi, y_in, hy, ly):
    hy[...] = from_high(yi, g.ny, y_in, lambda r: r[...])
    ly[...] = from_low(yi, g.ny, y_in, lambda r: r[...])


def gather_strips(g, xi, x_in, hy, ly, xh, xl):
    half = g.Z // 2
    for block in range(g.blocks):
        lanes = slice(block * LANES, (block + 1) * LANES)
        xh[block, : g.Y] = from_high(xi, g.nx, x_in, lambda r: r[block])
        xl[block, : g.Y] = from_low(xi, g.nx, x_in, lambda r: r[block])
        top, low = hy[3 * half, :, lanes], ly[3 * half, :, lanes]
        xh[block, g.Y :] = jnp.concatenate([top[:DEPTH], low[:DEPTH]], axis=0)
        xl[block, g.Y :] = jnp.concatenate([top[DEPTH:], low[DEPTH:]], axis=0)


def row_halo(g, hy, ly, q, z):
    half = g.Z // 2
    at = (z % 2) * DEPTH
    block = q * half + z // 2
    return jnp.concatenate([hy[block, at : at + DEPTH], ly[block, at : at + DEPTH]], axis=0)


def deep_kernel(g, p, k, s, after, *deep):
    rest = DEPTH - 1
    zi = g.where()[0]
    for side in range(g.zsides):
        high = (zi % 2) == side
        for q, src in enumerate((p, k, s)):
            first = jnp.where(high, g.Z - rest if q == 2 else g.Z - DEPTH, 0 if q == 2 else 1)
            deep[side][q * rest : (q + 1) * rest] = src[pl.ds(first, rest)]


def local_kernel(g, p, k, s, out, token):
    token[...] = jnp.zeros((ROWS, LANES), F32)
    Z, Y, X = g.Z, g.Y, g.X
    zero = jnp.zeros((Y, X), F32)
    none = jnp.zeros((ROWS, X), F32)
    flux_z, weight_z = [none], [none]
    for layer in range(RATIO, Z, RATIO):
        w = 0.5 * (k[layer] + k[layer - 1])
        weight_z.append(group_rows(w))
        flux_z.append(group_rows(w * (p[layer] - p[layer - 1])))
    weight_z.append(none)
    flux_z.append(none)
    inner_x = (lane_of((ROWS, X)) % RATIO == 0) & (lane_of((ROWS, X)) > 0)
    first_y = row_of((Y, X)) % RATIO == 0
    row8 = row_of((ROWS, X))
    for cz in range(g.cz):
        acc_s = acc_wx = acc_fx = acc_wy = acc_fy = zero
        for z in range(cz * RATIO, (cz + 1) * RATIO):
            pz, kz = p[z], k[z]
            acc_s = acc_s + s[z]
            w = kz + roll(kz, 1, 1)
            acc_wx = acc_wx + w
            acc_fx = acc_fx + w * (pz - roll(pz, 1, 1))
            w = kz + roll(kz, 1, 0)
            acc_wy = acc_wy + w
            acc_fy = acc_fy + w * (pz - roll(pz, 1, 0))
        weight_x = jnp.where(inner_x, 0.5 * group_rows(acc_wx), 0.0)
        flux_x = jnp.where(inner_x, 0.5 * group_rows(acc_fx), 0.0)
        weight_y, flux_y = (
            jnp.where(row8 > 0, 0.5 * group_rows(jnp.where(first_y, acc, 0.0)), 0.0)
            for acc in (acc_wy, acc_fy)
        )
        out[0, cz] = (
            group_rows(acc_s)
            - (flux_z[cz] - flux_z[cz + 1])
            - (flux_y - roll(flux_y, -1, 0))
            - (flux_x - roll(flux_x, -1, 1))
        )
        out[1, cz] = (
            weight_z[cz]
            + weight_z[cz + 1]
            + weight_y
            + roll(weight_y, -1, 0)
            + weight_x
            + roll(weight_x, -1, 1)
        )
        out[2, cz] = weight_z[cz]
        out[3, cz] = weight_y
        out[4, cz] = weight_x


def side_kernel(g, *refs):
    p, k, s, sums = refs[:4]
    n = 4
    x_in = refs[n : n + g.xsides]
    n += g.xsides
    x_own = refs[n : n + g.xsides]
    n += g.xsides
    n += g.ysides
    out, xp, xk, xs, token = refs[n : n + 5]
    xh, xl = refs[n + 5 :]
    zi, yi, xi = g.where()
    Z, Y, X = g.Z, g.Y, g.X
    token[...] = jnp.zeros((ROWS, LANES), F32)
    for block in range(g.blocks):
        xh[block] = from_high(xi, g.nx, x_in, lambda r: r[block])
        xl[block] = from_low(xi, g.nx, x_in, lambda r: r[block])

    lane = lane_of((Y, LANES))
    even = (xi % 2) == 0
    if g.xsides == 1:
        own_hi = own_lo = x_own[0][0]
    else:
        own_hi = jnp.where(even, x_own[0][0], x_own[1][0])
        own_lo = jnp.where(even, x_own[1][0], x_own[0][0])

    def side_sums(own, other, lane_in, flip):
        wk = face(roll(own, -Z * DEPTH, 1), roll(other, -Z * DEPTH, 1))
        diff = (other - own) if flip else (own - other)
        keep = (lane % DEPTH == lane_in) & (lane < Z * DEPTH)
        w = jnp.where(keep, wk, 0.0)
        result = []
        for value in (w, w * diff):
            total = group_rows(value)
            step = DEPTH
            while step < RATIO * DEPTH:
                total = total + roll(total, -step, 1)
                step *= 2
            result.append(total)
        return result

    low_w, low_f = side_sums(own_lo, roll(xl[0], -(DEPTH - 1), 1), 0, False)
    high_w, high_f = side_sums(own_hi, roll(xh[0], DEPTH - 1, 1), DEPTH - 1, True)
    lane8 = lane_of((ROWS, X))

    def widen(value, at, cell):
        moved = roll(value, (at % LANES) - cell, 1)
        wide = jnp.concatenate([moved] * (X // LANES), axis=1)
        return jnp.where(lane8 == at, wide, 0.0)

    for cz in range(g.cz):
        cell = cz * RATIO * DEPTH
        x_low = widen(low_w, 0, cell)
        x_high = widen(high_w, X - 1, cell + DEPTH - 1)
        f_low = widen(low_f, 0, cell)
        f_high = widen(high_f, X - 1, cell + DEPTH - 1)
        out[0, cz] = sums[0, cz] - (f_low - f_high)
        out[1, cz] = sums[1, cz] + x_low + x_high
        out[2, cz] = sums[2, cz]
        out[3, cz] = sums[3, cz]
        out[4, cz] = sums[4, cz] + x_low

    for q, dst in enumerate((xp, xk, xs)):
        for z in range(Z):
            block, at = g.slot(q, z)
            hi = roll(xh[block], -at, 1)
            lo = roll(xl[block], -at - DEPTH, 1)
            dst[z] = strip_tile(hi, lo)


def weights_kernel(g, k, xk, after, fz, fy, fx, dinv, token):
    token[...] = jnp.zeros((ROWS, LANES), F32)
    Z = g.Z

    def k_at(z):
        return jnp.concatenate([k[z], xk[z]], axis=1)

    fy[0], fx[0], _ = side_faces(k_at(0))
    fz[1] = face(k_at(1), k_at(0))

    def body(z, carry):
        kz = k_at(z)
        above = face(k_at(z + 1), kz)
        fz[z + 1] = above
        wy, wx, total = side_faces(kz)
        fy[z] = wy
        fx[z] = wx
        dinv[z] = scale_of(kz, total + fz[z] + above)
        return carry

    lax.fori_loop(1, Z - 1, body, 0)
    fy[Z - 1], fx[Z - 1], _ = side_faces(k_at(Z - 1))


def restrict_kernel(g, *refs):
    p, k, sums = refs[:3]
    n = 3
    near = refs[n : n + g.zsides]
    n += g.zsides
    y_in = refs[n : n + g.ysides]
    n += g.ysides
    out = refs[n + 1]
    zi, yi, xi = g.where()
    Z, Y, X = g.Z, g.Y, g.X
    half = Z // 2
    row8 = row_of((ROWS, X))
    p0, k0 = (from_low(zi, g.nz, near, lambda r, q=q: r[q]) for q in range(2))
    w = face(k0, k[0])
    low_wz, low_fz = group_rows(w), group_rows(w * (p[0] - p0))
    p1, k1 = (from_high(zi, g.nz, near, lambda r, q=q: r[q]) for q in range(2))
    w = face(k[Z - 1], k1)
    top_wz, top_fz = group_rows(w), group_rows(w * (p1 - p[Z - 1]))
    items = []
    for cz in range(g.cz):
        low_w = low_f = top_w = top_f = jnp.zeros((1, X), F32)
        for z in range(cz * RATIO, (cz + 1) * RATIO):
            at = (z % 2) * DEPTH
            below, above = [], []
            for q in range(2):
                block = q * half + z // 2
                row = at + DEPTH - 1
                below.append(from_low(yi, g.ny, y_in, lambda r: r[block, row : row + 1, :]))
                above.append(from_high(yi, g.ny, y_in, lambda r: r[block, at : at + 1, :]))
            kz, pz = k[z, 0:1, :], p[z, 0:1, :]
            w = face(kz, below[1])
            low_w = low_w + w
            low_f = low_f + w * (pz - below[0])
            kz, pz = k[z, Y - 1 :, :], p[z, Y - 1 :, :]
            w = face(kz, above[1])
            top_w = top_w + w
            top_f = top_f + w * (above[0] - pz)

        def at_row(row, value):
            return jnp.where(row8 == row, jnp.broadcast_to(value, (ROWS, X)), 0.0)

        low_wy = at_row(0, low_w)
        rhs = sums[0, cz] - at_row(0, low_f) + at_row(g.cy - 1, top_f)
        diagonal = sums[1, cz] + low_wy + at_row(g.cy - 1, top_w)
        wz = sums[2, cz]
        if cz == 0:
            rhs = rhs - low_fz
            diagonal = diagonal + low_wz
            wz = wz + low_wz
        if cz == g.cz - 1:
            rhs = rhs + top_fz
            diagonal = diagonal + top_wz
        items.append([rhs, diagonal, wz, sums[3, cz] + low_wy, sums[4, cz]])
    items = [items[cz][q] for q in range(5) for cz in range(g.cz)]
    onehot = (
        lax.broadcasted_iota(jnp.int32, (X, LANES), 0) // RATIO
        == lax.broadcasted_iota(jnp.int32, (X, LANES), 1)
    ).astype(jnp.bfloat16)
    summed = exact_dot(jnp.concatenate(items, axis=0), onehot)
    per = LANES // g.cx
    cells = [jnp.zeros((ROWS, LANES), F32) for _ in range(coarse_blocks(g))]
    for m in range(len(items)):
        place = lax.rem(m % per + xi, per) * g.cx
        cells[m // per] = cells[m // per] + pltpu.roll(
            summed[m * ROWS : (m + 1) * ROWS], place, 1
        )
    for block, value in enumerate(cells):
        out[0, block] = value


def fill_relay(g, hy, ly, xh, xl, outs, zi):
    Z, X = g.Z, g.X
    for side, out in enumerate(outs):
        high = (zi % 2) == side

        def fill(top, out=out):
            first = Z - DEPTH if top else 0
            for q in range(3):
                for d in range(DEPTH):
                    part = row_halo(g, hy, ly, q, first + d)
                    for half_lane in range(X // LANES):
                        out[(q * DEPTH + d) * (X // LANES) + half_lane] = part[
                            :, half_lane * LANES : (half_lane + 1) * LANES
                        ]
            at_block = 3 * DEPTH * (X // LANES)
            wide = lane_of((g.YE, LANES))
            acc = jnp.zeros((g.YE, LANES), F32)
            span = DEPTH * DEPTH
            for piece, (ref, q) in enumerate((r, q) for r in (xh, xl) for q in range(3)):
                block, lane_at = g.slot(q, first)
                moved = roll(ref[block], piece * span - lane_at, 1)
                acc = jnp.where((wide >= piece * span) & (wide < (piece + 1) * span), moved, acc)
            out[at_block:] = acc.reshape(g.YE // ROWS, ROWS, LANES)

        pl.when(high)(functools.partial(fill, True))
        pl.when(jnp.logical_not(high))(functools.partial(fill, False))


def coarse_blocks(g):
    per = LANES // g.cx
    return -(-5 * g.cz // per)


def relay_blocks(g):
    return 3 * DEPTH * (g.X // LANES) + g.YE // ROWS


def strip_tile(hi, lo):
    lane = lane_of(hi.shape)
    return jnp.where(lane < DEPTH, hi, jnp.where(lane >= LANES - DEPTH, lo, 0.0))


def side_faces(kz):
    wy = face(kz, roll(kz, 1, 0))
    wx = face(kz, roll(kz, 1, 1))
    return wy, wx, wy + roll(wy, -1, 0) + wx + roll(wx, -1, 1)


def scale_of(kz, total):
    return jnp.where(kz > 0.0, OMEGA / total, 0.0)


class Fields:
    def __init__(self, main, side, rows):
        self.parts = main, side, rows

    def __getitem__(self, z):
        main, side, rows = self.parts
        wide = jnp.concatenate([main[z], side[z]], axis=1)
        return jnp.concatenate([wide, rows[z]], axis=0)


class Rows:
    def __init__(self, main, edge, head, tail):
        self.main, self.edge, self.head, self.tail = main, edge, head, tail

    def __getitem__(self, z):
        rows = self.main.shape[1]
        middle = self.main[z, self.head * ROWS : rows - self.tail * ROWS]
        parts = [middle, self.edge[z, self.head * ROWS :]]
        if self.head:
            parts = [self.edge[z, : self.head * ROWS]] + parts
        return jnp.concatenate(parts, axis=0)


def extend_kernel(g, *refs):
    k, xk, fz, fy, fx = refs[:5]
    n = 5
    y_in = refs[n : n + g.ysides]
    n += g.ysides
    x_in = refs[n : n + g.xsides]
    n += g.xsides
    n += 1
    yp, yk, ys, fz_y, fx_y, fy_e, dinv_e, token = refs[n : n + 8]
    n += 8
    relay = refs[n : n + g.zsides]
    n += g.zsides
    hy, ly, xh, xl = refs[n:]
    zi, yi, xi = g.where()
    Z, Y, X = g.Z, g.Y, g.X
    token[...] = jnp.zeros((ROWS, LANES), F32)
    gather_rows(g, yi, y_in, hy, ly)
    gather_strips(g, xi, x_in, hy, ly, xh, xl)
    fill_relay(g, hy, ly, xh, xl, relay, zi)
    for q, out in enumerate((yp, yk, ys)):
        for z in range(Z):
            out[z, :, :X] = row_halo(g, hy, ly, q, z)
            block, at = g.slot(q, z)
            hi = roll(xh[block, Y:], -at, 1)
            lo = roll(xl[block, Y:], -at - DEPTH, 1)
            out[z, :, X:] = strip_tile(hi, lo)

    def edge_rows(z):
        first = jnp.concatenate([k[z, :ROWS], xk[z, :ROWS]], axis=1)
        last = jnp.concatenate([k[z, Y - ROWS :], xk[z, Y - ROWS :]], axis=1)
        return last, yk[z], first

    for z in range(Z):
        last, beyond, first = edge_rows(z)
        tiles = jnp.concatenate([last, beyond, first], axis=0)
        wy = face(tiles, roll(tiles, 1, 0))
        fy_e[z, :ROWS] = wy[2 * ROWS :]
        fy_e[z, ROWS:] = wy[ROWS : 2 * ROWS]
        wx = face(beyond, roll(beyond, 1, 1))
        fx_y[z] = wx
        if z > 0:
            fz_y[z] = face(beyond, yk[z - 1])
    for z in range(1, Z - 1):
        last, beyond, first = edge_rows(z)
        tiles = jnp.concatenate([last, beyond, first], axis=0)
        wy = jnp.concatenate(
            [fy[z, Y - ROWS :], fy_e[z, ROWS:], fy_e[z, :ROWS], fy[z, ROWS : 2 * ROWS]], axis=0
        )
        wy = (wy + roll(wy, -1, 0))[: 3 * ROWS]
        wx = jnp.concatenate([fx[z, Y - ROWS :], fx_y[z], fx[z, :ROWS]], axis=0)
        wz = [
            jnp.concatenate([fz[i, Y - ROWS :], fz_y[i], fz[i, :ROWS]], axis=0) for i in (z, z + 1)
        ]
        scale = scale_of(tiles, wy + wx + roll(wx, -1, 1) + wz[0] + wz[1])
        dinv_e[z, :ROWS] = scale[2 * ROWS :]
        dinv_e[z, ROWS : 2 * ROWS] = scale[:ROWS]
        dinv_e[z, 2 * ROWS :] = scale[ROWS : 2 * ROWS]


def beyond(g, z):
    return z + DEPTH if z < DEPTH else z - g.Z + 3 * DEPTH


def face_at(g, z):
    return z + DEPTH - 1 if z <= 0 else z - g.Z + DEPTH


def scale_at(g, z):
    return z + DEPTH - 1 if z <= 0 else z - g.Z + 1 + DEPTH


def own_weights(refs):
    fz, fz_y, fx, fx_y, fy, fy_e = refs
    return Rows(fz, fz_y, 0, 0), Rows(fx, fx_y, 0, 0), Rows(fy, fy_e, 1, 0)


def halo_kernel(g, *refs):
    own_k = Fields(*refs[:3])
    fz, fx, fy = own_weights(refs[3:9])
    n = 9
    near = refs[n : n + g.zsides]
    n += g.zsides
    deep = refs[n : n + g.zsides]
    n += g.zsides
    relay = refs[n : n + g.zsides]
    n += g.zsides
    n += 1
    ph, sh, hz, hy, hx, hd, token = refs[n : n + 7]
    kh = refs[n + 7]
    token[...] = jnp.zeros((ROWS, LANES), F32)
    zi, yi, xi = g.where()
    Z, Y, X = g.Z, g.Y, g.X
    parts = X // LANES
    rest = DEPTH - 1
    zero = jnp.zeros((g.YE, g.XE), F32)

    def k_at(z):
        return own_k[z] if 0 <= z < Z else kh[beyond(g, z)]

    def own_faces(z):
        wy, wx = fy[z], fx[z]
        return wy + roll(wy, -1, 0) + wx + roll(wx, -1, 1)

    def fill(top, side):
        strip = relay[side][3 * DEPTH * parts :].reshape(g.YE, LANES)
        for q, out in enumerate((ph, kh, sh)):
            for d in range(DEPTH):
                at = beyond(g, Z + d if top else d - DEPTH)
                if q < 2 and d == (0 if top else rest):
                    plane = near[side][q]
                elif q < 2:
                    plane = deep[side][q * rest + (d - 1 if top else d)]
                elif d == (rest if top else 0):
                    continue
                else:
                    plane = deep[side][q * rest + (d if top else d - 1)]
                out[at, :Y, :X] = plane
                for part in range(parts):
                    lanes = slice(part * LANES, (part + 1) * LANES)
                    out[at, Y:, lanes] = relay[side][(q * DEPTH + d) * parts + part]
                hi = roll(strip, -(q * DEPTH + d) * DEPTH, 1)
                lo = roll(strip, -((3 + q) * DEPTH + d) * DEPTH - DEPTH, 1)
                out[at, :, X:] = strip_tile(hi, lo)
        z = Z - 1 if top else 0
        step = 1 if top else -1
        kz = k_at(z)
        outer = face(k_at(z + step), kz)
        hz[face_at(g, z + 1 if top else z)] = outer
        inner = fz[z if top else z + 1]
        hd[scale_at(g, z)] = scale_of(kz, own_faces(z) + inner + outer)
        for _ in range(DEPTH - 1):
            z += step
            inner = outer
            kz = k_at(z)
            outer = face(k_at(z + step), kz)
            hz[face_at(g, z + 1 if top else z)] = outer
            wy, wx, total = side_faces(kz)
            hy[beyond(g, z)] = wy
            hx[beyond(g, z)] = wx
            hd[scale_at(g, z)] = scale_of(kz, total + inner + outer)

    def boundary(top):
        z = Z - 1 if top else 0
        kz = k_at(z)
        ph[beyond(g, z + 1 if top else z - 1)] = zero
        hz[face_at(g, z + 1 if top else z)] = kz
        hd[scale_at(g, z)] = scale_of(kz, own_faces(z) + fz[z if top else z + 1] + kz)

    for side in range(g.zsides):
        above = (zi % 2) == side
        pl.when(above & (zi < g.nz - 1))(functools.partial(fill, True, side))
        pl.when(jnp.logical_not(above) & (zi > 0))(functools.partial(fill, False, side))
    pl.when(zi == 0)(functools.partial(boundary, False))
    pl.when(zi == g.nz - 1)(functools.partial(boundary, True))


def sweep_kernel(g, sweep, inside, *refs):
    refs = list(refs)
    Z = g.Z
    final = sweep == SWEEPS
    own_s = Fields(*refs[:3])
    fz, fx, fy = own_weights(refs[3:9])
    dinv = Rows(refs[9], refs[10], 1, 1)
    n = 11
    if sweep == 1:
        v = Fields(*refs[n : n + 3])
        n += 3
    else:
        v = refs[n]
        n += 1
    if not inside:
        vh, sh, hz, hy, hx, hd = refs[n : n + 6]
        n += 6
    if final and inside:
        out = refs[n]
    elif final:
        earlier, out = refs[n : n + 2]
    else:
        out = refs[n]
    refs[-1][...] = jnp.zeros((ROWS, LANES), F32)
    zi, yi, xi = g.where()
    reach = SWEEPS - sweep

    def update(vz, low, high, source, z_low, z_high, wy, wx, scale):
        total = source + z_low * low + z_high * high
        total = total + wy * roll(vz, 1, 0) + roll(wy * vz, -1, 0)
        total = total + wx * roll(vz, 1, 1) + roll(wx * vz, -1, 1)
        return (1.0 - OMEGA) * vz + scale * total

    if inside:

        def body(z, carry):
            new = update(
                v[z], v[z - 1], v[z + 1], own_s[z], fz[z], fz[z + 1], fy[z], fx[z], dinv[z]
            )
            if final:
                out[z] = new[: g.Y, : g.X]
            else:
                out[z] = new
            return carry

        lax.fori_loop(sweep, Z - sweep, body, 0)
        return

    def v_at(z):
        return v[z] if sweep - 1 <= z <= Z - sweep else vh[beyond(g, z)]

    def z_face(z):
        return fz[z] if 1 <= z < Z else hz[face_at(g, z)]

    def edge(z):
        own = 0 <= z < Z
        at = beyond(g, z)
        new = update(
            v_at(z),
            v_at(z - 1),
            v_at(z + 1),
            own_s[z] if own else sh[at],
            z_face(z),
            z_face(z + 1),
            fy[z] if own else hy[at],
            fx[z] if own else hx[at],
            dinv[z] if 0 < z < Z - 1 else hd[scale_at(g, z)],
        )
        if final:
            out[z] = new[: g.Y, : g.X]
        else:
            out[at] = new

    for z in range(sweep):
        edge(z)
        edge(Z - 1 - z)
    if final:
        for z in range(sweep, Z - sweep):
            out[z] = earlier[z]
        return
    zero = jnp.zeros((g.YE, g.XE), F32)

    def halo(layers):
        for z in layers:
            edge(z)

    def clear(z):
        out[beyond(g, z)] = zero

    pl.when(zi > 0)(functools.partial(halo, range(-reach, 0)))
    pl.when(zi < g.nz - 1)(functools.partial(halo, range(Z, Z + reach)))
    pl.when(zi == 0)(functools.partial(clear, -1))
    pl.when(zi == g.nz - 1)(functools.partial(clear, Z))


def solve_kernel(g, gathered, fine, out):
    zi, yi, xi = g.where()
    per = LANES // g.cx
    group = lane_of((ROWS, LANES)) // g.cx

    order = g.steps()

    def relative(a, b, c):
        apart = {
            "gx": jnp.bitwise_xor(a, zi),
            "gy": jnp.bitwise_xor(b, yi),
            "gz": jnp.bitwise_xor(c, xi),
        }
        at = 0
        for number, (axis, bit) in enumerate(order):
            at = at + (1 << number) * ((apart[axis] & bit) // bit)
        return at

    layers = g.nz * g.cz
    height = g.ny * g.cy
    fields = []
    for q in range(5):
        planes = []
        for layer in range(layers):
            a, cz = divmod(layer, g.cz)
            m = q * g.cz + cz
            tiles = []
            for b in range(g.ny):
                value = gathered[relative(a, b, 0), m // per]
                for c in range(1, g.nx):
                    value = jnp.where(
                        group == (m % per + c) % per, gathered[relative(a, b, c), m // per], value
                    )
                tiles.append(roll(value, -(m % per) * g.cx, 1))
            planes.append(jnp.concatenate(tiles, axis=0))
        fields.append(planes)
    rhs, diagonal, wz, wy, wx = fields
    shape = (height, LANES)
    zero = jnp.zeros(shape, F32)
    wz = [zero] + wz[1:]
    wy = [jnp.where(row_of(shape) == 0, 0.0, w) for w in wy]
    wx = [jnp.where(lane_of(shape) == 0, 0.0, w) for w in wx]
    scale = [OMEGA_COARSE / d for d in diagonal]

    def flux(e):
        result = []
        for i in range(layers):
            total = wy[i] * roll(e[i], 1, 0) + roll(wy[i] * e[i], -1, 0)
            total = total + wx[i] * roll(e[i], 1, 1) + roll(wx[i] * e[i], -1, 1)
            if i > 0:
                total = total + wz[i] * e[i - 1]
            if i < layers - 1:
                total = total + wz[i + 1] * e[i + 1]
            result.append(total)
        return result

    e = [sc * r for sc, r in zip(scale, rhs)]
    for _ in range(COARSE_SWEEPS - 1):
        f = flux(e)
        e = [(1.0 - OMEGA_COARSE) * e[i] + scale[i] * (rhs[i] + f[i]) for i in range(layers)]
    f = flux(e)
    left = zero
    total = zero
    for i in range(layers):
        left = left + (rhs[i] - diagonal[i] * e[i] + f[i])
        total = total + diagonal[i]
    shift = jnp.sum(left) / jnp.sum(total)

    own = []
    for cz in range(g.cz):
        mine = jnp.zeros((ROWS, LANES), F32)
        for a in range(g.nz):
            for b in range(g.ny):
                here = (zi == a) & (yi == b)
                mine = jnp.where(here, e[a * g.cz + cz][b * ROWS : (b + 1) * ROWS], mine)
        own.append(mine)
    onehot = (
        lax.broadcasted_iota(jnp.int32, (LANES, g.X), 0)
        == xi * g.cx + lax.broadcasted_iota(jnp.int32, (LANES, g.X), 1) // RATIO
    ).astype(jnp.bfloat16)
    wide = exact_dot(jnp.concatenate(own, axis=0), onehot) + shift
    for cz in range(g.cz):
        block = wide[cz * ROWS : (cz + 1) * ROWS]
        spread = jnp.broadcast_to(block[:, None, :], (g.cy, RATIO, g.X)).reshape(g.Y, g.X)
        for z in range(cz * RATIO, (cz + 1) * RATIO):
            out[z] = fine[z] + spread


def merge_kernel(cells, got, token, out):
    count = cells.shape[0]
    out[:count] = cells[...]
    out[count:] = got[...]


def merge(cells, got, token):
    shape = (2 * cells.shape[0],) + cells.shape[1:]
    (out,) = run(merge_kernel, [shape], [cells, got, token], us=0.05, name="merge")
    return out


def exchange(bufs, axis, count, beside=None):
    got = [lax.ppermute(bufs[0], axis, pairs(count, 0))]
    if len(bufs) > 1:
        if beside is None:
            got.append(lax.ppermute(bufs[1], axis, pairs(count, 1)))
        else:
            perm = spread_pairs(count, lax.axis_size(beside))
            got.append(lax.ppermute(bufs[1], (axis, beside), perm))
    return got


def shards(pressure_start, source, permeability):
    g = Grid(pressure_start.shape)
    Z, Y, X = g.Z, g.Y, g.X
    tile = (ROWS, LANES)
    x_shape = (g.blocks, Y, LANES)
    y_shape = (3 * Z // 2 + 1, ROWS, X)
    sums_shape = (5, g.cz, ROWS, X)
    main = (Z, Y, g.XE)
    nr = relay_blocks(g)

    sent = run(
        functools.partial(pack_kernel, g),
        [(Z, Y, X)] * 3
        + [(2, Y, X)] * g.zsides
        + [x_shape] * g.xsides,
        [pressure_start, permeability, source],
        scratch=[pltpu.SemaphoreType.DMA((3 + 2 * g.zsides,))],
        name="pack_faces",
        far=True,
    )
    sent = list(sent)
    (p, k, s), near, x_sent = sent[:3], sent[3 : 3 + g.zsides], sent[3 + g.zsides :]
    near_got = exchange(near, "gx", g.nz, "gz")
    x_got = exchange(x_sent, "gz", g.nx)
    sums, token = run(
        functools.partial(local_kernel, g),
        [sums_shape, tile],
        [p, k, s],
        us=US["local"],
        name="local_sums",
    )
    y_sent = run(
        functools.partial(pack_rows_kernel, g),
        [y_shape] * g.ysides,
        [p, k, s] + x_got + near_got + [token],
        us=US["rows"],
        name="pack_rows",
    )
    y_got = exchange(y_sent, "gy", g.ny, "gz")
    sums, xp, xk, xs, token = run(
        functools.partial(side_kernel, g),
        [sums_shape] + [(Z, Y, LANES)] * 3 + [tile],
        [p, k, s, sums] + x_got + x_sent + list(y_sent),
        scratch=[pltpu.VMEM(x_shape, F32)] * 2,
        us=US["side"],
        name="side",
    )
    deep = run(
        functools.partial(deep_kernel, g),
        [(3 * (DEPTH - 1), Y, X)] * g.zsides,
        [p, k, s, token],
        us=0.1,
        name="pack_deep",
    )
    deep_got = exchange(deep, "gx", g.nz, "gz")
    fz, fy, fx, dinv, token = run(
        functools.partial(weights_kernel, g),
        [main] * 4 + [tile],
        [k, xk, token],
        us=US["weights"],
        name="weights",
    )
    (cells,) = run(
        functools.partial(restrict_kernel, g),
        [(1, coarse_blocks(g)) + tile],
        [p, k, sums] + near_got + list(y_got) + [token],
        us=US["restrict"],
        name="restrict",
    )
    rows = (Z, ROWS, g.XE)
    halo_scratch = [pltpu.VMEM(y_shape, F32)] * 2 + [pltpu.VMEM((g.blocks, g.YE, LANES), F32)] * 2
    extended = run(
        functools.partial(extend_kernel, g),
        [rows] * 5 + [(Z, 2 * ROWS, g.XE), (Z, 3 * ROWS, g.XE), tile] + [(nr,) + tile] * g.zsides,
        [k, xk, fz, fy, fx] + list(y_got) + x_got + [cells],
        scratch=halo_scratch,
        us=US["extend"],
        name="extend",
    )
    yp, yk, ys, fz_y, fx_y, fy_e, dinv_e, token = extended[:8]
    relay = exchange(extended[8:], "gx", g.nz, "gz")
    weights = [fz, fz_y, fx, fx_y, fy, fy_e]
    common = [s, xs, ys] + weights + [dinv, dinv_e]
    own = (Z, g.YE, g.XE)
    far = (4 * DEPTH, g.YE, g.XE)
    far8 = (2 * DEPTH, g.YE, g.XE)
    inner, tokens = [[p, xp, yp]], []
    for sweep in range(1, SWEEPS + 1):
        v, token = run(
            functools.partial(sweep_kernel, g, sweep, True),
            [(Z, Y, X) if sweep == SWEEPS else own, tile],
            common + inner[-1],
            us=US["sweep"] * (Z - 2 * sweep) / Z,
            name=f"inner_{sweep}",
        )
        inner.append([v])
        tokens.append(token)
    vh, sh, hz, hy, hx, hd, token = run(
        functools.partial(halo_kernel, g),
        [far, far, far8, far, far, far8, tile],
        [k, xk, yk] + weights + near_got + deep_got + relay + [tokens[2]],
        scratch=[pltpu.VMEM(far, F32)],
        us=US["halo"],
        name="halo",
    )
    for sweep in range(1, SWEEPS + 1):
        final = sweep == SWEEPS
        vh, token = run(
            functools.partial(sweep_kernel, g, sweep, False),
            [(Z, Y, X) if final else far, tile],
            common + inner[sweep - 1] + [vh, sh, hz, hy, hx, hd] + (inner[sweep] if final else []),
            us=US["outer"],
            name=f"outer_{sweep}",
        )
        tokens.append(token)
    steps = g.steps()
    plan = [0, 1, 3, 5, 6]
    for number, (axis, bit) in enumerate(steps):
        got = lax.ppermute(cells, axis, flips(lax.axis_size(axis), bit))
        cells = merge(cells, got, tokens[plan[max(0, number - len(steps) + len(plan))]])
    (out,) = run(
        functools.partial(solve_kernel, g),
        [(Z, Y, X)],
        [cells, vh],
        us=US["solve"],
        name="solve",
        spaces=[jax.ShapeDtypeStruct((Z, Y, X), F32)],
    )
    return out


def solution(mesh):
    return jax.shard_map(
        shards,
        mesh=mesh,
        in_specs=(P("gx", "gy", "gz"), P("gx", "gy", "gz"), P("gx", "gy", "gz")),
        out_specs=P("gx", "gy", "gz"),
        check_vma=False,
    )
```

```python
import functools

import jax
import jax.numpy as jnp
from jax import lax
from jax.experimental import pallas as pl
from jax.experimental.pallas import tpu as pltpu
from jax.sharding import PartitionSpec as P

RATIO = 8
SWEEPS = 4
COARSE_SWEEPS = 8
OMEGA = 0.8
OMEGA_COARSE = 0.8

LANES = 128
ROWS = 8
DEPTH = SWEEPS
SLOTS = LANES // DEPTH
F32 = jnp.float32
VMEM_LIMIT = 12 * 1024 * 1024
US = dict(local=1.2, rows=0.1, side=0.8, weights=3.2, restrict=0.6, extend=1.0, halo=1.4, outer=0.8, sweep=2.2, solve=2.2)


def pairs(count, odd):
    start = 1 if odd else 0
    out = []
    for low in range(start, count + start - 1, 2):
        high = (low + 1) % count
        out += [(low, high), (high, low)]
    return out


def spread_pairs(outer, inner):
    out = []
    for i in range(outer):
        for j in range(inner):
            if i in (0, outer - 1):
                target = i * inner + (j ^ 1)
            else:
                target = (i + 1 if i % 2 else i - 1) * inner + j
            out.append((i * inner + j, target))
    return out


def flips(count, bit):
    return [(i, i ^ bit) for i in range(count)]


def on_chip(value):
    return pltpu.with_memory_space_constraint(value, pltpu.VMEM)


def run(kernel, outs, args, scratch=(), us=1.0, name=None, spaces=None, far=False, aliases=None):
    whole = pl.BlockSpec(memory_space=pltpu.VMEM)
    shapes = [pltpu.VMEM(shape, F32) for shape in outs] if spaces is None else spaces
    return pl.pallas_call(
        kernel,
        out_shape=shapes,
        in_specs=[pl.BlockSpec(memory_space=pltpu.HBM) if far else whole] * len(args),
        out_specs=[whole] * len(outs),
        scratch_shapes=list(scratch),
        input_output_aliases=aliases or {},
        compiler_params=pltpu.CompilerParams(vmem_limit_bytes=VMEM_LIMIT),
        cost_estimate=pl.CostEstimate(
            flops=1000, bytes_accessed=int(us * 3_500_000), transcendentals=0
        ),
        name=name,
    )(*[pltpu.with_memory_space_constraint(a, pltpu.HBM) if far else on_chip(a) for a in args])


def lane_of(shape):
    return lax.broadcasted_iota(jnp.int32, shape, len(shape) - 1)


def row_of(shape):
    return lax.broadcasted_iota(jnp.int32, shape, len(shape) - 2)


def roll(values, shift, axis):
    size = values.shape[axis]
    if isinstance(shift, int):
        shift = shift % size
        if shift == 0:
            return values
    return pltpu.roll(values, shift, axis)


def face(one, other):
    half = jnp.where(jnp.minimum(one, other) > 0.0, 0.5, 1.0)
    return half * (one + other)


def group_rows(values):
    rows, width = values.shape
    return values.reshape(rows // RATIO, RATIO, width).sum(axis=1)


def split3(values):
    a = values.astype(jnp.bfloat16)
    rest = values - a.astype(F32)
    b = rest.astype(jnp.bfloat16)
    c = (rest - b.astype(F32)).astype(jnp.bfloat16)
    return jnp.concatenate([a, b, c], axis=0)


def exact_dot(values, onehot):
    rows = values.shape[0]
    out = jnp.dot(split3(values), onehot, preferred_element_type=F32)
    return out[:rows] + out[rows : 2 * rows] + out[2 * rows :]


class Grid:
    def __init__(self, shape):
        self.Z, self.Y, self.X = shape
        self.nz, self.ny, self.nx = (lax.axis_size("gx"), lax.axis_size("gy"), lax.axis_size("gz"))
        self.cz, self.cy, self.cx = (n // RATIO for n in shape)
        self.blocks = -(-3 * self.Z // SLOTS)
        self.XE = self.X + LANES
        self.YE = self.Y + ROWS
        self.ZE = self.Z + 2 * DEPTH
        self.zsides = 1 if self.nz == 2 else 2
        self.ysides = 1 if self.ny == 2 else 2
        self.xsides = 1 if self.nx == 2 else 2
        assert 2 * DEPTH == ROWS and 2 * self.Z <= SLOTS and self.Z % 2 == 0
        assert self.blocks * LANES <= self.X and self.cy == ROWS
        assert self.cx * self.nx == LANES

    def where(self):
        return lax.axis_index("gx"), lax.axis_index("gy"), lax.axis_index("gz")

    def steps(self):
        bits = [("gy", 1 << i) for i in reversed(range(1, self.ny.bit_length() - 1))]
        bits += [("gz", 1 << i) for i in reversed(range(1, self.nx.bit_length() - 1))]
        bits += [("gy", 1)]
        bits += [("gx", 1 << i) for i in reversed(range(self.nz.bit_length() - 1))]
        return bits + [("gz", 1)]

    def slot(self, q, z):
        index = q * self.Z + z
        return index // SLOTS, (index % SLOTS) * DEPTH


def pack_kernel(g, *refs):
    src = refs[:3]
    fields = refs[3:6]
    n = 6
    near = refs[n : n + g.zsides]
    n += g.zsides
    x_out = refs[n : n + g.xsides]
    n += g.xsides
    y_out = refs[n : n + g.ysides]
    sems = refs[n + g.ysides]
    zi, yi, xi = g.where()
    copies = []

    def send(q, at, size, out, place):
        source = src[q].at[pl.ds(at, size)]
        target = out.at[pl.ds(place, size)]
        copies.append(pltpu.make_async_copy(source, target, sems.at[3 + len(copies)]))

    for side in range(g.zsides):
        high = (zi % 2) == side
        for q in range(2):
            send(q, jnp.where(high, g.Z - 1, 0), 1, near[side], q)
    loads = [pltpu.make_async_copy(src[q], fields[q], sems.at[q]) for q in range(3)]
    for copy in loads + copies:
        copy.start()
    lane = lane_of((g.Y, LANES))
    hi_pack = [jnp.zeros((g.Y, LANES), F32) for _ in range(g.blocks)]
    lo_pack = list(hi_pack)
    for q in range(3):
        loads[q].wait()
        for z in range(g.Z):
            block, at = g.slot(q, z)
            keep = (lane >= at) & (lane < at + DEPTH)
            moved = roll(fields[q][z, :, g.X - LANES :], at + DEPTH, 1)
            hi_pack[block] = jnp.where(keep, moved, hi_pack[block])
            moved = roll(fields[q][z, :, :LANES], at, 1)
            lo_pack[block] = jnp.where(keep, moved, lo_pack[block])
        if q < 2:
            for at in range(0, g.Z, ROWS):
                layers = range(at, at + ROWS)
                hi = jnp.concatenate([fields[q][z, g.Y - 1 :, :] for z in layers], axis=0)
                lo = jnp.concatenate([fields[q][z, :1, :] for z in layers], axis=0)
                for side, out in enumerate(y_out):
                    out[q, at : at + ROWS] = jnp.where((yi % 2) == side, hi, lo)
    even = (xi % 2) == 0
    for block in range(g.blocks):
        for side, out in enumerate(x_out):
            out[block] = jnp.where(even == (side == 0), hi_pack[block], lo_pack[block])
    for copy in copies:
        copy.wait()


def pick(first, second, even, inside):
    if second is None:
        return jnp.where(even & inside, first, 0.0)
    return jnp.where(inside, jnp.where(even, first, second), 0.0)


def from_high(index, count, bufs, view):
    even = (index % 2) == 0
    second = view(bufs[1]) if len(bufs) > 1 else None
    return pick(view(bufs[0]), second, even, index < count - 1)


def from_low(index, count, bufs, view):
    odd = (index % 2) == 1
    second = view(bufs[1]) if len(bufs) > 1 else None
    return pick(view(bufs[0]), second, odd, index > 0)


def pack_rows_kernel(g, *refs):
    src = refs[:3]
    x_in = refs[3 : 3 + g.xsides]
    y_out = refs[len(refs) - g.ysides :]
    zi, yi, xi = g.where()
    half = g.Z // 2
    last = g.Y - ROWS
    for side, out in enumerate(y_out):
        high = (yi % 2) == side

        def fill(top, out=out):
            for q in range(3):
                for pair in range(half):
                    a, b = src[q][2 * pair], src[q][2 * pair + 1]
                    if top:
                        part = jnp.concatenate([a[g.Y - DEPTH :], b[g.Y - DEPTH :]], axis=0)
                    else:
                        part = jnp.concatenate([a[:DEPTH], b[:DEPTH]], axis=0)
                    out[q * half + pair] = part
            rows = slice(g.Y - DEPTH, g.Y) if top else slice(0, DEPTH)
            for block in range(g.blocks):
                hi = from_high(xi, g.nx, x_in, lambda r: r[block, rows, :])
                lo = from_low(xi, g.nx, x_in, lambda r: r[block, rows, :])
                out[3 * half, :, block * LANES : (block + 1) * LANES] = jnp.concatenate(
                    [hi, lo], axis=0
                )

        pl.when(high)(functools.partial(fill, True))
        pl.when(jnp.logical_not(high))(functools.partial(fill, False))


def gather_rows(g, yi, y_in, hy, ly):
    hy[...] = from_high(yi, g.ny, y_in, lambda r: r[...])
    ly[...] = from_low(yi, g.ny, y_in, lambda r: r[...])


def gather_strips(g, xi, x_in, hy, ly, xh, xl):
    half = g.Z // 2
    for block in range(g.blocks):
        lanes = slice(block * LANES, (block + 1) * LANES)
        xh[block, : g.Y] = from_high(xi, g.nx, x_in, lambda r: r[block])
        xl[block, : g.Y] = from_low(xi, g.nx, x_in, lambda r: r[block])
        top, low = hy[3 * half, :, lanes], ly[3 * half, :, lanes]
        xh[block, g.Y :] = jnp.concatenate([top[:DEPTH], low[:DEPTH]], axis=0)
        xl[block, g.Y :] = jnp.concatenate([top[DEPTH:], low[DEPTH:]], axis=0)


def row_halo(g, hy, ly, q, z):
    half = g.Z // 2
    at = (z % 2) * DEPTH
    block = q * half + z // 2
    return jnp.concatenate([hy[block, at : at + DEPTH], ly[block, at : at + DEPTH]], axis=0)


def deep_kernel(g, p, k, s, *refs):
    deep = refs[len(refs) - g.zsides :]
    rest = DEPTH - 1
    zi = g.where()[0]
    for side in range(g.zsides):
        high = (zi % 2) == side
        for q, src in enumerate((p, k, s)):
            first = jnp.where(high, g.Z - rest if q == 2 else g.Z - DEPTH, 0 if q == 2 else 1)
            deep[side][q * rest : (q + 1) * rest] = src[pl.ds(first, rest)]


def local_kernel(g, p, k, s, out, token):
    token[...] = jnp.zeros((ROWS, LANES), F32)
    Z, Y, X = g.Z, g.Y, g.X
    zero = jnp.zeros((Y, X), F32)
    none = jnp.zeros((ROWS, X), F32)
    flux_z, weight_z = [none], [none]
    for layer in range(RATIO, Z, RATIO):
        w = 0.5 * (k[layer] + k[layer - 1])
        weight_z.append(group_rows(w))
        flux_z.append(group_rows(w * (p[layer] - p[layer - 1])))
    weight_z.append(none)
    flux_z.append(none)
    inner_x = (lane_of((ROWS, X)) % RATIO == 0) & (lane_of((ROWS, X)) > 0)
    first_y = row_of((Y, X)) % RATIO == 0
    row8 = row_of((ROWS, X))
    for cz in range(g.cz):
        acc_s = acc_wx = acc_fx = acc_wy = acc_fy = zero
        for z in range(cz * RATIO, (cz + 1) * RATIO):
            pz, kz = p[z], k[z]
            acc_s = acc_s + s[z]
            w = kz + roll(kz, 1, 1)
            acc_wx = acc_wx + w
            acc_fx = acc_fx + w * (pz - roll(pz, 1, 1))
            w = kz + roll(kz, 1, 0)
            acc_wy = acc_wy + w
            acc_fy = acc_fy + w * (pz - roll(pz, 1, 0))
        weight_x = jnp.where(inner_x, 0.5 * group_rows(acc_wx), 0.0)
        flux_x = jnp.where(inner_x, 0.5 * group_rows(acc_fx), 0.0)
        weight_y, flux_y = (
            jnp.where(row8 > 0, 0.5 * group_rows(jnp.where(first_y, acc, 0.0)), 0.0)
            for acc in (acc_wy, acc_fy)
        )
        out[0, cz] = (
            group_rows(acc_s)
            - (flux_z[cz] - flux_z[cz + 1])
            - (flux_y - roll(flux_y, -1, 0))
            - (flux_x - roll(flux_x, -1, 1))
        )
        out[1, cz] = (
            weight_z[cz]
            + weight_z[cz + 1]
            + weight_y
            + roll(weight_y, -1, 0)
            + weight_x
            + roll(weight_x, -1, 1)
        )
        out[2, cz] = weight_z[cz]
        out[3, cz] = weight_y
        out[4, cz] = weight_x


def side_kernel(g, *refs):
    x_in = refs[: g.xsides]
    xp, xk, xs, token, xh, xl = refs[g.xsides + 1 :]
    xi = g.where()[2]
    Z = g.Z
    token[...] = jnp.zeros((ROWS, LANES), F32)
    for block in range(g.blocks):
        xh[block] = from_high(xi, g.nx, x_in, lambda r: r[block])
        xl[block] = from_low(xi, g.nx, x_in, lambda r: r[block])

    for q, dst in enumerate((xp, xk, xs)):
        for z in range(Z):
            block, at = g.slot(q, z)
            hi = roll(xh[block], -at, 1)
            lo = roll(xl[block], -at - DEPTH, 1)
            dst[z] = strip_tile(hi, lo)


def weights_kernel(g, k, xk, after, fz, fy, fx, dinv, token):
    token[...] = jnp.zeros((ROWS, LANES), F32)
    Z = g.Z

    def k_at(z):
        return jnp.concatenate([k[z], xk[z]], axis=1)

    fy[0], fx[0], _ = side_faces(k_at(0))
    below = face(k_at(1), k_at(0))
    fz[1] = below
    for z in range(1, Z - 1):
        kz = k_at(z)
        above = face(k_at(z + 1), kz)
        fz[z + 1] = above
        wy, wx, total = side_faces(kz)
        fy[z] = wy
        fx[z] = wx
        dinv[z] = scale_of(kz, total + below + above)
        below = above
    fy[Z - 1], fx[Z - 1], _ = side_faces(k_at(Z - 1))


def own_sides(bufs, even, view):
    if len(bufs) == 1:
        return view(bufs[0]), view(bufs[0])
    first, second = view(bufs[0]), view(bufs[1])
    return jnp.where(even, first, second), jnp.where(even, second, first)


def restrict_kernel(g, *refs):
    p, k, sums = refs[:3]
    n = 3
    near = refs[n : n + g.zsides]
    n += g.zsides
    y_in = refs[n : n + g.ysides]
    n += g.ysides
    y_own = refs[n : n + g.ysides]
    n += g.ysides
    x_in = refs[n : n + g.xsides]
    n += g.xsides
    x_own = refs[n : n + g.xsides]
    n += g.xsides
    out, token = refs[n:]
    token[...] = jnp.zeros((ROWS, LANES), F32)
    zi, yi, xi = g.where()
    Z, Y, X = g.Z, g.Y, g.X

    p0, k0 = (from_low(zi, g.nz, near, lambda r, q=q: r[q]) for q in range(2))
    w = face(k0, k[0])
    low_wz, low_fz = group_rows(w), group_rows(w * (p[0] - p0))
    p1, k1 = (from_high(zi, g.nz, near, lambda r, q=q: r[q]) for q in range(2))
    w = face(k[Z - 1], k1)
    top_wz, top_fz = group_rows(w), group_rows(w * (p1 - p[Z - 1]))

    (p_hi, p_lo), (k_hi, k_lo) = (
        own_sides(y_own, (yi % 2) == 0, lambda r, q=q: r[q]) for q in range(2)
    )
    p0, k0 = (from_low(yi, g.ny, y_in, lambda r, q=q: r[q]) for q in range(2))
    low_wy = face(k0, k_lo)
    low_fy = low_wy * (p_lo - p0)
    p1, k1 = (from_high(yi, g.ny, y_in, lambda r, q=q: r[q]) for q in range(2))
    top_wy = face(k_hi, k1)
    top_fy = top_wy * (p1 - p_hi)

    lane = lane_of((Y, LANES))
    own_hi, own_lo = own_sides(x_own, (xi % 2) == 0, lambda r: r[0])
    next_hi = from_high(xi, g.nx, x_in, lambda r: r[0])
    next_lo = from_low(xi, g.nx, x_in, lambda r: r[0])

    def side_sums(own, other, lane_in, flip):
        wk = face(roll(own, -Z * DEPTH, 1), roll(other, -Z * DEPTH, 1))
        diff = (other - own) if flip else (own - other)
        keep = (lane % DEPTH == lane_in) & (lane < Z * DEPTH)
        w = jnp.where(keep, wk, 0.0)
        result = []
        for value in (w, w * diff):
            total = group_rows(value)
            step = DEPTH
            while step < RATIO * DEPTH:
                total = total + roll(total, -step, 1)
                step *= 2
            result.append(total)
        return result

    low_wx, low_fx = side_sums(own_lo, roll(next_lo, -(DEPTH - 1), 1), 0, False)
    top_wx, top_fx = side_sums(own_hi, roll(next_hi, DEPTH - 1, 1), DEPTH - 1, True)
    lane8 = lane_of((ROWS, X))
    row8 = row_of((ROWS, X))

    def widen(value, at, cell):
        moved = roll(value, (at % LANES) - cell, 1)
        wide = jnp.concatenate([moved] * (X // LANES), axis=1)
        return jnp.where(lane8 == at, wide, 0.0)

    def at_row(row, values, cz):
        total = values[cz * RATIO : (cz + 1) * RATIO].sum(axis=0, keepdims=True)
        return jnp.where(row8 == row, jnp.broadcast_to(total, (ROWS, X)), 0.0)

    items = []
    for cz in range(g.cz):
        cell = cz * RATIO * DEPTH
        x_low = widen(low_wx, 0, cell)
        y_low = at_row(0, low_wy, cz)
        rhs = sums[0, cz] - at_row(0, low_fy, cz) + at_row(g.cy - 1, top_fy, cz)
        rhs = rhs - widen(low_fx, 0, cell) + widen(top_fx, X - 1, cell + DEPTH - 1)
        diagonal = sums[1, cz] + y_low + at_row(g.cy - 1, top_wy, cz)
        diagonal = diagonal + x_low + widen(top_wx, X - 1, cell + DEPTH - 1)
        wz = sums[2, cz]
        if cz == 0:
            rhs = rhs - low_fz
            diagonal = diagonal + low_wz
            wz = wz + low_wz
        if cz == g.cz - 1:
            rhs = rhs + top_fz
            diagonal = diagonal + top_wz
        items.append([rhs, diagonal, wz, sums[3, cz] + y_low, sums[4, cz] + x_low])
    items = [items[cz][q] for q in range(5) for cz in range(g.cz)]
    onehot = (
        lax.broadcasted_iota(jnp.int32, (X, LANES), 0) // RATIO
        == lax.broadcasted_iota(jnp.int32, (X, LANES), 1)
    ).astype(jnp.bfloat16)
    summed = exact_dot(jnp.concatenate(items, axis=0), onehot)
    per = LANES // g.cx
    cells = [jnp.zeros((ROWS, LANES), F32) for _ in range(coarse_blocks(g))]
    for m in range(len(items)):
        place = lax.rem(m % per + xi, per) * g.cx
        cells[m // per] = cells[m // per] + pltpu.roll(
            summed[m * ROWS : (m + 1) * ROWS], place, 1
        )
    for block, value in enumerate(cells):
        out[0, block] = value


def fill_relay(g, hy, ly, xh, xl, outs, zi):
    Z, X = g.Z, g.X
    for side, out in enumerate(outs):
        high = (zi % 2) == side

        def fill(top, out=out):
            first = Z - DEPTH if top else 0
            pieces = []
            for q in range(3):
                for d in range(DEPTH):
                    count = relay_rows(q, d)
                    if count:
                        part = row_halo(g, hy, ly, q, Z - 1 - d if top else d)
                        pieces += [part[:count], part[ROWS - count :]]
            missing = relay_tiles() * ROWS - sum(piece.shape[0] for piece in pieces)
            if missing:
                pieces.append(jnp.zeros((missing, X), F32))
            packed = jnp.concatenate(pieces, axis=0)
            for tile in range(relay_tiles()):
                for part in range(X // LANES):
                    out[tile * (X // LANES) + part] = packed[
                        tile * ROWS : (tile + 1) * ROWS, part * LANES : (part + 1) * LANES
                    ]
            at_block = relay_tiles() * (X // LANES)
            wide = lane_of((g.YE, LANES))
            acc = jnp.zeros((g.YE, LANES), F32)
            span = DEPTH * DEPTH
            for piece, (ref, q) in enumerate((r, q) for r in (xh, xl) for q in range(3)):
                block, lane_at = g.slot(q, first)
                moved = roll(ref[block], piece * span - lane_at, 1)
                acc = jnp.where((wide >= piece * span) & (wide < (piece + 1) * span), moved, acc)
            out[at_block:] = acc.reshape(g.YE // ROWS, ROWS, LANES)

        pl.when(high)(functools.partial(fill, True))
        pl.when(jnp.logical_not(high))(functools.partial(fill, False))


def coarse_blocks(g):
    per = LANES // g.cx
    return -(-5 * g.cz // per)


def relay_rows(q, d):
    return max(0, DEPTH - 1 - d - (q == 2))


def relay_tiles():
    rows = sum(2 * relay_rows(q, d) for q in range(3) for d in range(DEPTH))
    return -(-rows // ROWS)


def relay_blocks(g):
    return relay_tiles() * (g.X // LANES) + g.YE // ROWS


def strip_tile(hi, lo):
    lane = lane_of(hi.shape)
    return jnp.where(lane < DEPTH, hi, jnp.where(lane >= LANES - DEPTH, lo, 0.0))


def side_faces(kz):
    wy = face(kz, roll(kz, 1, 0))
    wx = face(kz, roll(kz, 1, 1))
    return wy, wx, wy + roll(wy, -1, 0) + wx + roll(wx, -1, 1)


def scale_of(kz, total):
    return jnp.where(kz > 0.0, OMEGA / total, 0.0)


class Fields:
    def __init__(self, main, side, rows):
        self.parts = main, side, rows

    def __getitem__(self, z):
        main, side, rows = self.parts
        wide = jnp.concatenate([main[z], side[z]], axis=1)
        return jnp.concatenate([wide, rows[z]], axis=0)


class Rows:
    def __init__(self, main, edge, head, tail):
        self.main, self.edge, self.head, self.tail = main, edge, head, tail

    def __getitem__(self, z):
        rows = self.main.shape[1]
        middle = self.main[z, self.head * ROWS : rows - self.tail * ROWS]
        parts = [middle, self.edge[z, self.head * ROWS :]]
        if self.head:
            parts = [self.edge[z, : self.head * ROWS]] + parts
        return jnp.concatenate(parts, axis=0)


def extend_kernel(g, *refs):
    k, xk, fz, fy, fx = refs[:5]
    n = 5
    y_in = refs[n : n + g.ysides]
    n += g.ysides
    x_in = refs[n : n + g.xsides]
    n += g.xsides
    n += 1
    yp, yk, ys, fz_y, fx_y, fy_e, dinv_e, token = refs[n : n + 8]
    n += 8
    relay = refs[n : n + g.zsides]
    n += g.zsides
    hy, ly, xh, xl = refs[n:]
    zi, yi, xi = g.where()
    Z, Y, X = g.Z, g.Y, g.X
    token[...] = jnp.zeros((ROWS, LANES), F32)
    gather_rows(g, yi, y_in, hy, ly)
    gather_strips(g, xi, x_in, hy, ly, xh, xl)
    fill_relay(g, hy, ly, xh, xl, relay, zi)
    for q, out in enumerate((yp, yk, ys)):
        for z in range(Z):
            out[z, :, :X] = row_halo(g, hy, ly, q, z)
            block, at = g.slot(q, z)
            hi = roll(xh[block, Y:], -at, 1)
            lo = roll(xl[block, Y:], -at - DEPTH, 1)
            out[z, :, X:] = strip_tile(hi, lo)

    def edge_rows(z):
        first = jnp.concatenate([k[z, :ROWS], xk[z, :ROWS]], axis=1)
        last = jnp.concatenate([k[z, Y - ROWS :], xk[z, Y - ROWS :]], axis=1)
        return last, yk[z], first

    for z in range(Z):
        last, beyond, first = edge_rows(z)
        tiles = jnp.concatenate([last, beyond, first], axis=0)
        wy = face(tiles, roll(tiles, 1, 0))
        fy_e[z, :ROWS] = wy[2 * ROWS :]
        fy_e[z, ROWS:] = wy[ROWS : 2 * ROWS]
        wx = face(beyond, roll(beyond, 1, 1))
        fx_y[z] = wx
        if z > 0:
            fz_y[z] = face(beyond, yk[z - 1])
    for z in range(1, Z - 1):
        last, beyond, first = edge_rows(z)
        tiles = jnp.concatenate([last, beyond, first], axis=0)
        wy = jnp.concatenate(
            [fy[z, Y - ROWS :], fy_e[z, ROWS:], fy_e[z, :ROWS], fy[z, ROWS : 2 * ROWS]], axis=0
        )
        wy = (wy + roll(wy, -1, 0))[: 3 * ROWS]
        wx = jnp.concatenate([fx[z, Y - ROWS :], fx_y[z], fx[z, :ROWS]], axis=0)
        wz = [
            jnp.concatenate([fz[i, Y - ROWS :], fz_y[i], fz[i, :ROWS]], axis=0) for i in (z, z + 1)
        ]
        scale = scale_of(tiles, wy + wx + roll(wx, -1, 1) + wz[0] + wz[1])
        dinv_e[z, :ROWS] = scale[2 * ROWS :]
        dinv_e[z, ROWS : 2 * ROWS] = scale[:ROWS]
        dinv_e[z, 2 * ROWS :] = scale[ROWS : 2 * ROWS]


def beyond(g, z):
    return z + DEPTH if z < DEPTH else z - g.Z + 3 * DEPTH


def either(top, high, low):
    return (high if top else low) if isinstance(top, bool) else jnp.where(top, high, low)


def halo_at(top, d):
    return either(top, 3 * DEPTH + d, DEPTH - 1 - d)


def face_at(top, d):
    return either(top, DEPTH + d, DEPTH - 1 - d)


def scale_at(top, d):
    return either(top, DEPTH + 1 + d, DEPTH - 2 - d)


def on_sides(g, zi, act):
    if g.zsides == 1:
        act(zi == 0)
    else:
        pl.when(zi < g.nz - 1)(functools.partial(act, True))
        pl.when(zi > 0)(functools.partial(act, False))


def on_ends(g, zi, act):
    if g.zsides == 1:
        act(zi != 0)
    else:
        pl.when(zi == g.nz - 1)(functools.partial(act, True))
        pl.when(zi == 0)(functools.partial(act, False))


def own_weights(refs):
    fz, fz_y, fx, fx_y, fy, fy_e = refs
    return Rows(fz, fz_y, 0, 0), Rows(fx, fx_y, 0, 0), Rows(fy, fy_e, 1, 0)


def halo_kernel(g, *refs):
    own_k = Fields(*refs[:3])
    fz, fx, fy = own_weights(refs[3:9])
    n = 9
    near = refs[n : n + g.zsides]
    n += g.zsides
    deep = refs[n : n + g.zsides]
    n += g.zsides
    relay = refs[n : n + g.zsides]
    n += g.zsides
    n += 1
    ph, sh, hz, hy, hx, hd, token = refs[n : n + 7]
    kh = refs[n + 7]
    token[...] = jnp.zeros((ROWS, LANES), F32)
    zi, yi, xi = g.where()
    Z, Y, X = g.Z, g.Y, g.X
    parts = X // LANES
    rest = DEPTH - 1
    zero = jnp.zeros((g.YE, g.XE), F32)

    def own_faces(z):
        wy, wx = fy[z], fx[z]
        return wy + roll(wy, -1, 0) + wx + roll(wx, -1, 1)

    def fill(top):
        def received(bufs, at):
            if len(bufs) == 1:
                return bufs[0][at]
            return jnp.where((zi % 2 == 0) == top, bufs[0][at], bufs[1][at])

        count = relay_tiles() * parts
        tiles = [received(relay, i) for i in range(relay_blocks(g))]
        strip = jnp.concatenate(tiles[count:], axis=0)
        packed = jnp.concatenate(
            [
                jnp.concatenate(tiles[i : i + parts], axis=1)
                for i in range(0, count, parts)
            ],
            axis=0,
        )
        start = 0
        for q, out in enumerate((ph, kh, sh)):
            for d in range(DEPTH if q < 2 else rest):
                at = halo_at(top, d)
                layer = either(top, d, rest - d)
                if q == 2:
                    plane = received(deep, 2 * rest + either(top, d, rest - 1 - d))
                elif d == 0:
                    plane = received(near, q)
                else:
                    plane = received(deep, q * rest + either(top, d - 1, rest - d))
                out[at, :Y, :X] = plane
                used = relay_rows(q, d)
                if used:
                    rows = [packed[start : start + used], packed[start + used : start + 2 * used]]
                    if 2 * used < ROWS:
                        rows.insert(1, jnp.zeros((ROWS - 2 * used, X), F32))
                    out[at, Y:, :X] = jnp.concatenate(rows, axis=0)
                    start += 2 * used
                else:
                    out[at, Y:, :X] = jnp.zeros((ROWS, X), F32)
                hi = turn(strip, -(q * DEPTH + layer) * DEPTH)
                lo = turn(strip, -((3 + q) * DEPTH + layer) * DEPTH - DEPTH)
                out[at, :, X:] = strip_tile(hi, lo)
        z = either(top, Z - 1, 0)
        kz = own_k[z]
        beyond_k = kh[halo_at(top, 0)]
        outer = face(beyond_k, kz)
        hz[face_at(top, 0)] = outer
        inner = fz[either(top, Z - 1, 1)]
        hd[scale_at(top, -1)] = scale_of(kz, own_faces(z) + inner + outer)
        for d in range(DEPTH - 1):
            inner = outer
            kz = beyond_k
            beyond_k = kh[halo_at(top, d + 1)]
            outer = face(beyond_k, kz)
            hz[face_at(top, d + 1)] = outer
            wy, wx, total = side_faces(kz)
            hy[halo_at(top, d)] = wy
            hx[halo_at(top, d)] = wx
            hd[scale_at(top, d)] = scale_of(kz, total + inner + outer)

    def end(top):
        z = either(top, Z - 1, 0)
        kz = own_k[z]
        ph[halo_at(top, 0)] = zero
        hz[face_at(top, 0)] = kz
        hd[scale_at(top, -1)] = scale_of(kz, own_faces(z) + fz[either(top, Z - 1, 1)] + kz)

    on_sides(g, zi, fill)
    on_ends(g, zi, end)


def turn(values, shift):
    if isinstance(shift, int):
        return roll(values, shift, 1)
    return pltpu.roll(values, lax.rem(shift + 8 * LANES, LANES), 1)


def sweep_kernel(g, sweep, inside, *refs):
    refs = list(refs)
    Z = g.Z
    final = sweep == SWEEPS
    own_s = Fields(*refs[:3])
    fz, fx, fy = own_weights(refs[3:9])
    dinv = Rows(refs[9], refs[10], 1, 1)
    n = 11
    if sweep == 1:
        v = Fields(*refs[n : n + 3])
        n += 3
    else:
        v = refs[n]
        n += 1
    if not inside:
        vh, sh, hz, hy, hx, hd = refs[n : n + 6]
        n += 6
    out = refs[-2]
    refs[-1][...] = jnp.zeros((ROWS, LANES), F32)
    zi, yi, xi = g.where()
    reach = SWEEPS - sweep

    def update(vz, low, high, source, z_low, z_high, wy, wx, scale):
        total = source + z_low * low + z_high * high
        total = total + wy * roll(vz, 1, 0) + roll(wy * vz, -1, 0)
        total = total + wx * roll(vz, 1, 1) + roll(wx * vz, -1, 1)
        return (1.0 - OMEGA) * vz + scale * total

    if inside:

        for z in range(sweep, Z - sweep):
            new = update(
                v[z], v[z - 1], v[z + 1], own_s[z], fz[z], fz[z + 1], fy[z], fx[z], dinv[z]
            )
            if final:
                out[z] = new[: g.Y, : g.X]
            else:
                out[z] = new
        return

    def v_at(z):
        return v[z] if sweep - 1 <= z <= Z - sweep else vh[beyond(g, z)]

    def z_face(z):
        return fz[z] if 1 <= z < Z else hz[face_at(z >= Z, 0)]

    def own_edge(z):
        new = update(
            v_at(z),
            v_at(z - 1),
            v_at(z + 1),
            own_s[z],
            z_face(z),
            z_face(z + 1),
            fy[z],
            fx[z],
            dinv[z] if 0 < z < Z - 1 else hd[scale_at(z > 0, -1)],
        )
        if final:
            out[beyond(g, z) - DEPTH] = new[: g.Y, : g.X]
        else:
            out[beyond(g, z)] = new

    def halo(top):
        inner = v[either(top, Z - 1, 0)] if sweep == 1 else vh[halo_at(top, -1)]
        vz = vh[halo_at(top, 0)]
        for d in range(reach):
            at = halo_at(top, d)
            outer = vh[halo_at(top, d + 1)]
            z_inner, z_outer = hz[face_at(top, d)], hz[face_at(top, d + 1)]
            out[at] = update(
                vz, inner, outer, sh[at], z_inner, z_outer, hy[at], hx[at], hd[scale_at(top, d)]
            )
            inner, vz = vz, outer

    def clear(top):
        out[halo_at(top, 0)] = jnp.zeros((g.YE, g.XE), F32)

    for z in range(sweep):
        own_edge(z)
        own_edge(Z - 1 - z)
    if final:
        return
    on_sides(g, zi, halo)
    on_ends(g, zi, clear)


def solve_kernel(g, gathered, fine, edges, out):
    zi, yi, xi = g.where()
    per = LANES // g.cx
    group = lane_of((ROWS, LANES)) // g.cx

    order = g.steps()

    def relative(a, b, c):
        apart = {
            "gx": jnp.bitwise_xor(a, zi),
            "gy": jnp.bitwise_xor(b, yi),
            "gz": jnp.bitwise_xor(c, xi),
        }
        at = 0
        for number, (axis, bit) in enumerate(order):
            at = at + (1 << number) * ((apart[axis] & bit) // bit)
        return at

    layers = g.nz * g.cz
    height = g.ny * g.cy
    fields = []
    for q in range(5):
        planes = []
        for layer in range(layers):
            a, cz = divmod(layer, g.cz)
            m = q * g.cz + cz
            tiles = []
            for b in range(g.ny):
                value = gathered[relative(a, b, 0), m // per]
                for c in range(1, g.nx):
                    value = jnp.where(
                        group == (m % per + c) % per, gathered[relative(a, b, c), m // per], value
                    )
                tiles.append(roll(value, -(m % per) * g.cx, 1))
            planes.append(jnp.concatenate(tiles, axis=0))
        fields.append(planes)
    rhs, diagonal, wz, wy, wx = fields
    shape = (height, LANES)
    zero = jnp.zeros(shape, F32)
    wz = [zero] + wz[1:]
    wy = [jnp.where(row_of(shape) == 0, 0.0, w) for w in wy]
    wx = [jnp.where(lane_of(shape) == 0, 0.0, w) for w in wx]
    scale = [OMEGA_COARSE / d for d in diagonal]

    def flux(e):
        result = []
        for i in range(layers):
            total = wy[i] * roll(e[i], 1, 0) + roll(wy[i] * e[i], -1, 0)
            total = total + wx[i] * roll(e[i], 1, 1) + roll(wx[i] * e[i], -1, 1)
            if i > 0:
                total = total + wz[i] * e[i - 1]
            if i < layers - 1:
                total = total + wz[i + 1] * e[i + 1]
            result.append(total)
        return result

    e = [sc * r for sc, r in zip(scale, rhs)]
    for _ in range(COARSE_SWEEPS - 1):
        f = flux(e)
        e = [(1.0 - OMEGA_COARSE) * e[i] + scale[i] * (rhs[i] + f[i]) for i in range(layers)]
    f = flux(e)
    left = zero
    total = zero
    for i in range(layers):
        left = left + (rhs[i] - diagonal[i] * e[i] + f[i])
        total = total + diagonal[i]
    shift = jnp.sum(left) / jnp.sum(total)

    own = []
    for cz in range(g.cz):
        mine = jnp.zeros((ROWS, LANES), F32)
        for a in range(g.nz):
            for b in range(g.ny):
                here = (zi == a) & (yi == b)
                mine = jnp.where(here, e[a * g.cz + cz][b * ROWS : (b + 1) * ROWS], mine)
        own.append(mine)
    onehot = (
        lax.broadcasted_iota(jnp.int32, (LANES, g.X), 0)
        == xi * g.cx + lax.broadcasted_iota(jnp.int32, (LANES, g.X), 1) // RATIO
    ).astype(jnp.bfloat16)
    wide = exact_dot(jnp.concatenate(own, axis=0), onehot) + shift
    for cz in range(g.cz):
        block = wide[cz * ROWS : (cz + 1) * ROWS]
        spread = jnp.broadcast_to(block[:, None, :], (g.cy, RATIO, g.X)).reshape(g.Y, g.X)
        for z in range(cz * RATIO, (cz + 1) * RATIO):
            if DEPTH <= z < g.Z - DEPTH:
                out[z] = fine[z] + spread
            else:
                out[z] = edges[beyond(g, z) - DEPTH] + spread


def merge_kernel(cells, got, token, out):
    count = cells.shape[0]
    out[:count] = cells[...]
    out[count:] = got[...]


def merge(cells, got, token):
    shape = (2 * cells.shape[0],) + cells.shape[1:]
    (out,) = run(merge_kernel, [shape], [cells, got, token], us=0.05, name="merge")
    return out


def exchange(bufs, axis, count, beside=None):
    got = [lax.ppermute(bufs[0], axis, pairs(count, 0))]
    if len(bufs) > 1:
        if beside is None:
            got.append(lax.ppermute(bufs[1], axis, pairs(count, 1)))
        else:
            perm = spread_pairs(count, lax.axis_size(beside))
            got.append(lax.ppermute(bufs[1], (axis, beside), perm))
    return got


def shards(pressure_start, source, permeability):
    g = Grid(pressure_start.shape)
    Z, Y, X = g.Z, g.Y, g.X
    tile = (ROWS, LANES)
    x_shape = (g.blocks, Y, LANES)
    y_shape = (3 * Z // 2 + 1, ROWS, X)
    sums_shape = (5, g.cz, ROWS, X)
    main = (Z, Y, g.XE)
    nr = relay_blocks(g)

    sent = run(
        functools.partial(pack_kernel, g),
        [(Z, Y, X)] * 3
        + [(2, Y, X)] * g.zsides
        + [x_shape] * g.xsides
        + [(2, Z, X)] * g.ysides,
        [pressure_start, permeability, source],
        scratch=[pltpu.SemaphoreType.DMA((3 + 2 * g.zsides,))],
        name="pack_faces",
        far=True,
    )
    sent = list(sent)
    (p, k, s), near, sent = sent[:3], sent[3 : 3 + g.zsides], sent[3 + g.zsides :]
    x_sent, row_sent = sent[: g.xsides], sent[g.xsides :]
    near_got = exchange(near, "gx", g.nz, "gz")
    x_got = exchange(x_sent, "gz", g.nx)
    row_got = exchange(row_sent, "gy", g.ny, "gz")
    sums, token_l = run(
        functools.partial(local_kernel, g),
        [sums_shape, tile],
        [p, k, s],
        us=US["local"],
        name="local_sums",
    )
    cells, token = run(
        functools.partial(restrict_kernel, g),
        [(1, coarse_blocks(g)) + tile, tile],
        [p, k, sums] + near_got + row_got + row_sent + x_got + x_sent,
        us=US["restrict"],
        name="restrict",
    )
    y_sent = run(
        functools.partial(pack_rows_kernel, g),
        [y_shape] * g.ysides,
        [p, k, s] + x_got + near_got + [token],
        us=US["rows"],
        name="pack_rows",
    )
    y_got = exchange(y_sent, "gy", g.ny, "gz")
    xp, xk, xs, token = run(
        functools.partial(side_kernel, g),
        [(Z, Y, LANES)] * 3 + [tile],
        x_got + [y_sent[0]],
        scratch=[pltpu.VMEM(x_shape, F32)] * 2,
        us=US["side"],
        name="side",
    )
    deep = run(
        functools.partial(deep_kernel, g),
        [(3 * (DEPTH - 1), Y, X)] * g.zsides,
        [p, k, s, token_l] + near_got + row_got + x_got,
        us=0.1,
        name="pack_deep",
    )
    deep_got = exchange(deep, "gx", g.nz, "gz")
    fz, fy, fx, dinv, token_w = run(
        functools.partial(weights_kernel, g),
        [main] * 4 + [tile],
        [k, xk, token],
        us=US["weights"],
        name="weights",
    )
    rows = (Z, ROWS, g.XE)
    halo_scratch = [pltpu.VMEM(y_shape, F32)] * 2 + [pltpu.VMEM((g.blocks, g.YE, LANES), F32)] * 2
    extended = run(
        functools.partial(extend_kernel, g),
        [rows] * 5 + [(Z, 2 * ROWS, g.XE), (Z, 3 * ROWS, g.XE), tile] + [(nr,) + tile] * g.zsides,
        [k, xk, fz, fy, fx] + list(y_got) + x_got + [token_w],
        scratch=halo_scratch,
        us=US["extend"],
        name="extend",
    )
    yp, yk, ys, fz_y, fx_y, fy_e, dinv_e, token = extended[:8]
    relay = exchange(extended[8:], "gx", g.nz, "gz")
    weights = [fz, fz_y, fx, fx_y, fy, fy_e]
    common = [s, xs, ys] + weights + [dinv, dinv_e]
    own = (Z, g.YE, g.XE)
    far = (4 * DEPTH, g.YE, g.XE)
    far8 = (2 * DEPTH, g.YE, g.XE)
    inner, tokens = [[p, xp, yp]], []
    for sweep in range(1, SWEEPS + 1):
        v, token = run(
            functools.partial(sweep_kernel, g, sweep, True),
            [(Z, Y, X) if sweep == SWEEPS else own, tile],
            common + inner[-1] + (relay[:1] if sweep == 3 else []),
            us=US["sweep"] * (Z - 2 * sweep) / Z,
            name=f"inner_{sweep}",
        )
        inner.append([v])
        tokens.append(token)
    vh, sh, hz, hy, hx, hd, token = run(
        functools.partial(halo_kernel, g),
        [far, far, far8, far, far, far8, tile],
        [k, xk, yk] + weights + near_got + deep_got + relay + [tokens[2]],
        scratch=[pltpu.VMEM(far, F32)],
        us=US["halo"],
        name="halo",
    )
    for sweep in range(1, SWEEPS + 1):
        final = sweep == SWEEPS
        vh, token = run(
            functools.partial(sweep_kernel, g, sweep, False),
            [(2 * DEPTH, Y, X) if final else far, tile],
            common + inner[sweep - 1] + [vh, sh, hz, hy, hx, hd],
            us=US["outer"],
            name=f"outer_{sweep}",
        )
        tokens.append(token)
    steps = g.steps()
    plan = [0, 1, 3, 5, 6]
    for number, (axis, bit) in enumerate(steps):
        got = lax.ppermute(cells, axis, flips(lax.axis_size(axis), bit))
        cells = merge(cells, got, tokens[plan[max(0, number - len(steps) + len(plan))]])
    (out,) = run(
        functools.partial(solve_kernel, g),
        [(Z, Y, X)],
        [cells, v, vh],
        us=US["solve"],
        name="solve",
        spaces=[jax.ShapeDtypeStruct((Z, Y, X), F32)],
    )
    return out


def solution(mesh):
    return jax.shard_map(
        shards,
        mesh=mesh,
        in_specs=(P("gx", "gy", "gz"), P("gx", "gy", "gz"), P("gx", "gy", "gz")),
        out_specs=P("gx", "gy", "gz"),
        check_vma=False,
    )
```

```python
import functools

import jax
import jax.numpy as jnp
from jax import lax
from jax.experimental import pallas as pl
from jax.experimental.pallas import tpu as pltpu
from jax.sharding import PartitionSpec as P

RATIO = 8
SWEEPS = 4
COARSE_SWEEPS = 8
OMEGA = 0.8
OMEGA_COARSE = 0.8

LANES = 128
ROWS = 8
DEPTH = SWEEPS
SLOTS = LANES // DEPTH
F32 = jnp.float32
VMEM_LIMIT = 14 * 1024 * 1024
PLAN = ["W", "I1", "I4", "O2", "O3"]
US = dict(local=1.2, rows=0.1, side=0.8, weights=3.2, restrict=0.6, extend=1.0, halo=1.4, outer=0.8, sweep=2.2, solve=2.2)


def pairs(count, odd):
    start = 1 if odd else 0
    out = []
    for low in range(start, count + start - 1, 2):
        high = (low + 1) % count
        out += [(low, high), (high, low)]
    return out


def spread_pairs(outer, inner):
    out = []
    for i in range(outer):
        for j in range(inner):
            if i in (0, outer - 1):
                target = i * inner + (j ^ 1)
            else:
                target = (i + 1 if i % 2 else i - 1) * inner + j
            out.append((i * inner + j, target))
    return out


def flips(count, bit):
    return [(i, i ^ bit) for i in range(count)]


def on_chip(value):
    return pltpu.with_memory_space_constraint(value, pltpu.VMEM)


def run(kernel, outs, args, scratch=(), us=1.0, name=None, spaces=None, far=False, aliases=None):
    whole = pl.BlockSpec(memory_space=pltpu.VMEM)
    shapes = [pltpu.VMEM(shape, F32) for shape in outs] if spaces is None else spaces
    return pl.pallas_call(
        kernel,
        out_shape=shapes,
        in_specs=[pl.BlockSpec(memory_space=pltpu.HBM) if far else whole] * len(args),
        out_specs=[whole] * len(outs),
        scratch_shapes=list(scratch),
        input_output_aliases=aliases or {},
        compiler_params=pltpu.CompilerParams(vmem_limit_bytes=VMEM_LIMIT),
        cost_estimate=pl.CostEstimate(
            flops=1000, bytes_accessed=int(us * 3_500_000), transcendentals=0
        ),
        name=name,
    )(*[pltpu.with_memory_space_constraint(a, pltpu.HBM) if far else on_chip(a) for a in args])


def lane_of(shape):
    return lax.broadcasted_iota(jnp.int32, shape, len(shape) - 1)


def row_of(shape):
    return lax.broadcasted_iota(jnp.int32, shape, len(shape) - 2)


def roll(values, shift, axis):
    size = values.shape[axis]
    if isinstance(shift, int):
        shift = shift % size
        if shift == 0:
            return values
    return pltpu.roll(values, shift, axis)


def face(one, other):
    half = jnp.where(jnp.minimum(one, other) > 0.0, 0.5, 1.0)
    return half * (one + other)


def group_rows(values):
    rows, width = values.shape
    return values.reshape(rows // RATIO, RATIO, width).sum(axis=1)


def split3(values):
    a = values.astype(jnp.bfloat16)
    rest = values - a.astype(F32)
    b = rest.astype(jnp.bfloat16)
    c = (rest - b.astype(F32)).astype(jnp.bfloat16)
    return jnp.concatenate([a, b, c], axis=0)


def exact_dot(values, onehot):
    rows = values.shape[0]
    out = jnp.dot(split3(values), onehot, preferred_element_type=F32)
    return out[:rows] + out[rows : 2 * rows] + out[2 * rows :]


class Grid:
    def __init__(self, shape):
        self.Z, self.Y, self.X = shape
        self.nz, self.ny, self.nx = (lax.axis_size("gx"), lax.axis_size("gy"), lax.axis_size("gz"))
        self.cz, self.cy, self.cx = (n // RATIO for n in shape)
        self.blocks = -(-3 * self.Z // SLOTS)
        self.XE = self.X + LANES
        self.YE = self.Y + ROWS
        self.ZE = self.Z + 2 * DEPTH
        self.zsides = 1 if self.nz == 2 else 2
        self.ysides = 1 if self.ny == 2 else 2
        self.xsides = 1 if self.nx == 2 else 2
        assert 2 * DEPTH == ROWS and 2 * self.Z <= SLOTS and self.Z % 2 == 0
        assert self.blocks * LANES <= self.X and self.cy == ROWS
        assert self.cx * self.nx == LANES

    def where(self):
        return lax.axis_index("gx"), lax.axis_index("gy"), lax.axis_index("gz")

    def steps(self):
        bits = [("gz", 1 << i) for i in reversed(range(1, self.nx.bit_length() - 1))]
        bits += [("gy", 1 << i) for i in reversed(range(self.ny.bit_length() - 1))]
        bits += [("gx", 1 << i) for i in reversed(range(self.nz.bit_length() - 1))]
        return bits + [("gz", 1)]

    def slot(self, q, z):
        index = q * self.Z + z
        return index // SLOTS, (index % SLOTS) * DEPTH


def pack_kernel(g, *refs):
    src = refs[:3]
    fields = refs[3:6]
    n = 6
    near = refs[n : n + g.zsides]
    n += g.zsides
    x_out = refs[n : n + g.xsides]
    n += g.xsides
    y_out = refs[n : n + g.ysides]
    sems = refs[n + g.ysides]
    zi, yi, xi = g.where()
    copies = []

    def send(q, at, size, out, place):
        source = src[q].at[pl.ds(at, size)]
        target = out.at[pl.ds(place, size)]
        copies.append(pltpu.make_async_copy(source, target, sems.at[3 + len(copies)]))

    for side in range(g.zsides):
        high = (zi % 2) == side
        for q in range(2):
            send(q, jnp.where(high, g.Z - 1, 0), 1, near[side], q)
    loads = [pltpu.make_async_copy(src[q], fields[q], sems.at[q]) for q in range(3)]
    for copy in loads + copies:
        copy.start()
    lane = lane_of((g.Y, LANES))
    packs = [[jnp.zeros((g.Y, LANES), F32) for _ in range(g.blocks)] for _ in range(2)]
    for q in range(3):
        loads[q].wait()
        for z in range(g.Z):
            block, at = g.slot(q, z)
            pack = packs[(at // DEPTH) % 2]
            both = jnp.where(
                lane < LANES // 2, fields[q][z, :, :LANES], fields[q][z, :, g.X - LANES :]
            )
            keep = (lane + (LANES + DEPTH - at)) % LANES < 2 * DEPTH
            pack[block] = jnp.where(keep, roll(both, at, 1), pack[block])
        if q < 2:
            for at in range(0, g.Z, ROWS):
                layers = range(at, at + ROWS)
                hi = jnp.concatenate([fields[q][z, g.Y - 1 :, :] for z in layers], axis=0)
                lo = jnp.concatenate([fields[q][z, :1, :] for z in layers], axis=0)
                for side, out in enumerate(y_out):
                    out[q, at : at + ROWS] = jnp.where((yi % 2) == side, hi, lo)
    even = (xi % 2) == 0
    first_half = lane % (2 * DEPTH) < DEPTH
    for block in range(g.blocks):
        lo = jnp.where(first_half, packs[0][block], packs[1][block])
        hi = roll(jnp.where(first_half, packs[1][block], packs[0][block]), DEPTH, 1)
        for side, out in enumerate(x_out):
            out[block] = jnp.where(even == (side == 0), hi, lo)
    for copy in copies:
        copy.wait()


def pick(first, second, even, inside):
    if second is None:
        return jnp.where(even & inside, first, 0.0)
    return jnp.where(inside, jnp.where(even, first, second), 0.0)


def from_high(index, count, bufs, view):
    even = (index % 2) == 0
    second = view(bufs[1]) if len(bufs) > 1 else None
    return pick(view(bufs[0]), second, even, index < count - 1)


def from_low(index, count, bufs, view):
    odd = (index % 2) == 1
    second = view(bufs[1]) if len(bufs) > 1 else None
    return pick(view(bufs[0]), second, odd, index > 0)


def pack_rows_kernel(g, *refs):
    src = refs[:3]
    x_in = refs[3 : 3 + g.xsides]
    y_out = refs[len(refs) - g.ysides :]
    zi, yi, xi = g.where()
    half = g.Z // 2
    last = g.Y - ROWS
    for side, out in enumerate(y_out):
        high = (yi % 2) == side

        def fill(top, out=out):
            for q in range(3):
                for pair in range(half):
                    a, b = src[q][2 * pair], src[q][2 * pair + 1]
                    if top:
                        part = jnp.concatenate([a[g.Y - DEPTH :], b[g.Y - DEPTH :]], axis=0)
                    else:
                        part = jnp.concatenate([a[:DEPTH], b[:DEPTH]], axis=0)
                    out[q * half + pair] = part
            rows = slice(g.Y - DEPTH, g.Y) if top else slice(0, DEPTH)
            for block in range(g.blocks):
                hi = from_high(xi, g.nx, x_in, lambda r: r[block, rows, :])
                lo = from_low(xi, g.nx, x_in, lambda r: r[block, rows, :])
                out[3 * half, :, block * LANES : (block + 1) * LANES] = jnp.concatenate(
                    [hi, lo], axis=0
                )

        pl.when(high)(functools.partial(fill, True))
        pl.when(jnp.logical_not(high))(functools.partial(fill, False))


def gather_rows(g, yi, y_in, hy, ly):
    hy[...] = from_high(yi, g.ny, y_in, lambda r: r[...])
    ly[...] = from_low(yi, g.ny, y_in, lambda r: r[...])


def gather_strips(g, xi, x_in, hy, ly, xh, xl):
    half = g.Z // 2
    for block in range(g.blocks):
        lanes = slice(block * LANES, (block + 1) * LANES)
        xh[block, : g.Y] = from_high(xi, g.nx, x_in, lambda r: r[block])
        xl[block, : g.Y] = from_low(xi, g.nx, x_in, lambda r: r[block])
        top, low = hy[3 * half, :, lanes], ly[3 * half, :, lanes]
        xh[block, g.Y :] = jnp.concatenate([top[:DEPTH], low[:DEPTH]], axis=0)
        xl[block, g.Y :] = jnp.concatenate([top[DEPTH:], low[DEPTH:]], axis=0)


def row_halo(g, hy, ly, q, z):
    half = g.Z // 2
    at = (z % 2) * DEPTH
    block = q * half + z // 2
    return jnp.concatenate([hy[block, at : at + DEPTH], ly[block, at : at + DEPTH]], axis=0)


def deep_kernel(g, p, k, s, *refs):
    deep = refs[len(refs) - g.zsides :]
    rest = DEPTH - 1
    zi = g.where()[0]
    for side in range(g.zsides):
        high = (zi % 2) == side
        for q, src in enumerate((p, k, s)):
            first = jnp.where(high, g.Z - rest if q == 2 else g.Z - DEPTH, 0 if q == 2 else 1)
            deep[side][q * rest : (q + 1) * rest] = src[pl.ds(first, rest)]


def local_kernel(g, p, k, s, out, token):
    token[...] = jnp.zeros((ROWS, LANES), F32)
    Z, Y, X = g.Z, g.Y, g.X
    zero = jnp.zeros((Y, X), F32)
    none = jnp.zeros((ROWS, X), F32)
    flux_z, weight_z = [none], [none]
    for layer in range(RATIO, Z, RATIO):
        w = 0.5 * (k[layer] + k[layer - 1])
        weight_z.append(group_rows(w))
        flux_z.append(group_rows(w * (p[layer] - p[layer - 1])))
    weight_z.append(none)
    flux_z.append(none)
    inner_x = (lane_of((ROWS, X)) % RATIO == 0) & (lane_of((ROWS, X)) > 0)
    first_y = row_of((Y, X)) % RATIO == 0
    row8 = row_of((ROWS, X))
    for cz in range(g.cz):
        acc_s = acc_wx = acc_fx = acc_wy = acc_fy = zero
        for z in range(cz * RATIO, (cz + 1) * RATIO):
            pz, kz = p[z], k[z]
            acc_s = acc_s + s[z]
            w = kz + roll(kz, 1, 1)
            acc_wx = acc_wx + w
            acc_fx = acc_fx + w * (pz - roll(pz, 1, 1))
            w = kz + roll(kz, 1, 0)
            acc_wy = acc_wy + w
            acc_fy = acc_fy + w * (pz - roll(pz, 1, 0))
        weight_x = jnp.where(inner_x, 0.5 * group_rows(acc_wx), 0.0)
        flux_x = jnp.where(inner_x, 0.5 * group_rows(acc_fx), 0.0)
        weight_y, flux_y = (
            jnp.where(row8 > 0, 0.5 * group_rows(jnp.where(first_y, acc, 0.0)), 0.0)
            for acc in (acc_wy, acc_fy)
        )
        out[0, cz] = (
            group_rows(acc_s)
            - (flux_z[cz] - flux_z[cz + 1])
            - (flux_y - roll(flux_y, -1, 0))
            - (flux_x - roll(flux_x, -1, 1))
        )
        out[1, cz] = (
            weight_z[cz]
            + weight_z[cz + 1]
            + weight_y
            + roll(weight_y, -1, 0)
            + weight_x
            + roll(weight_x, -1, 1)
        )
        out[2, cz] = weight_z[cz]
        out[3, cz] = weight_y
        out[4, cz] = weight_x


def side_kernel(g, *refs):
    x_in = refs[: g.xsides]
    xp, xk, xs, token, xh, xl = refs[g.xsides + 1 :]
    xi = g.where()[2]
    Z = g.Z
    token[...] = jnp.zeros((ROWS, LANES), F32)
    for block in range(g.blocks):
        xh[block] = from_high(xi, g.nx, x_in, lambda r: r[block])
        xl[block] = from_low(xi, g.nx, x_in, lambda r: r[block])

    for q, dst in enumerate((xp, xk, xs)):
        for z in range(Z):
            block, at = g.slot(q, z)
            hi = roll(xh[block], -at, 1)
            lo = roll(xl[block], -at - DEPTH, 1)
            dst[z] = strip_tile(hi, lo)


def weights_kernel(g, k, xk, after, fz, fy, fx, dinv, token):
    token[...] = jnp.zeros((ROWS, LANES), F32)
    Z = g.Z

    def k_at(z):
        return jnp.concatenate([k[z], xk[z]], axis=1)

    fy[0], fx[0], _ = side_faces(k_at(0))
    below = face(k_at(1), k_at(0))
    fz[1] = below
    for z in range(1, Z - 1):
        kz = k_at(z)
        above = face(k_at(z + 1), kz)
        fz[z + 1] = above
        wy, wx, total = side_faces(kz)
        fy[z] = wy
        fx[z] = wx
        dinv[z] = scale_of(kz, total + below + above)
        below = above
    fy[Z - 1], fx[Z - 1], _ = side_faces(k_at(Z - 1))


def own_sides(bufs, even, view):
    if len(bufs) == 1:
        return view(bufs[0]), view(bufs[0])
    first, second = view(bufs[0]), view(bufs[1])
    return jnp.where(even, first, second), jnp.where(even, second, first)


def side_weights_kernel(g, *refs):
    k, x_in = refs[0], refs[1 : 1 + g.xsides + 1]
    xp, xk, xs, fz, fy, fx, dinv, token, xh, xl = refs[2 + g.xsides :]
    side_kernel(g, *x_in, xp, xk, xs, token, xh, xl)
    weights_kernel(g, k, xk, token, fz, fy, fx, dinv, token)


def restrict_kernel(g, *refs):
    p, k, sums = refs[:3]
    n = 3
    near = refs[n : n + g.zsides]
    n += g.zsides
    y_in = refs[n : n + g.ysides]
    n += g.ysides
    y_own = refs[n : n + g.ysides]
    n += g.ysides
    x_in = refs[n : n + g.xsides]
    n += g.xsides
    x_own = refs[n : n + g.xsides]
    n += g.xsides
    out, token = refs[n:]
    token[...] = jnp.zeros((ROWS, LANES), F32)
    zi, yi, xi = g.where()
    Z, Y, X = g.Z, g.Y, g.X

    p0, k0 = (from_low(zi, g.nz, near, lambda r, q=q: r[q]) for q in range(2))
    w = face(k0, k[0])
    low_wz, low_fz = group_rows(w), group_rows(w * (p[0] - p0))
    p1, k1 = (from_high(zi, g.nz, near, lambda r, q=q: r[q]) for q in range(2))
    w = face(k[Z - 1], k1)
    top_wz, top_fz = group_rows(w), group_rows(w * (p1 - p[Z - 1]))

    (p_hi, p_lo), (k_hi, k_lo) = (
        own_sides(y_own, (yi % 2) == 0, lambda r, q=q: r[q]) for q in range(2)
    )
    p0, k0 = (from_low(yi, g.ny, y_in, lambda r, q=q: r[q]) for q in range(2))
    low_wy = face(k0, k_lo)
    low_fy = low_wy * (p_lo - p0)
    p1, k1 = (from_high(yi, g.ny, y_in, lambda r, q=q: r[q]) for q in range(2))
    top_wy = face(k_hi, k1)
    top_fy = top_wy * (p1 - p_hi)

    lane = lane_of((Y, LANES))
    own_hi, own_lo = own_sides(x_own, (xi % 2) == 0, lambda r: r[0])
    next_hi = from_high(xi, g.nx, x_in, lambda r: r[0])
    next_lo = from_low(xi, g.nx, x_in, lambda r: r[0])

    def side_sums(own, other, lane_in, flip):
        wk = face(roll(own, -Z * DEPTH, 1), roll(other, -Z * DEPTH, 1))
        diff = (other - own) if flip else (own - other)
        keep = (lane % DEPTH == lane_in) & (lane < Z * DEPTH)
        w = jnp.where(keep, wk, 0.0)
        result = []
        for value in (w, w * diff):
            total = group_rows(value)
            step = DEPTH
            while step < RATIO * DEPTH:
                total = total + roll(total, -step, 1)
                step *= 2
            result.append(total)
        return result

    low_wx, low_fx = side_sums(own_lo, roll(next_lo, -(DEPTH - 1), 1), 0, False)
    top_wx, top_fx = side_sums(own_hi, roll(next_hi, DEPTH - 1, 1), DEPTH - 1, True)
    lane8 = lane_of((ROWS, X))
    row8 = row_of((ROWS, X))

    def widen(value, at, cell):
        moved = roll(value, (at % LANES) - cell, 1)
        wide = jnp.concatenate([moved] * (X // LANES), axis=1)
        return jnp.where(lane8 == at, wide, 0.0)

    def at_row(row, values, cz):
        total = values[cz * RATIO : (cz + 1) * RATIO].sum(axis=0, keepdims=True)
        return jnp.where(row8 == row, jnp.broadcast_to(total, (ROWS, X)), 0.0)

    items = []
    for cz in range(g.cz):
        cell = cz * RATIO * DEPTH
        x_low = widen(low_wx, 0, cell)
        y_low = at_row(0, low_wy, cz)
        rhs = sums[0, cz] - at_row(0, low_fy, cz) + at_row(g.cy - 1, top_fy, cz)
        rhs = rhs - widen(low_fx, 0, cell) + widen(top_fx, X - 1, cell + DEPTH - 1)
        diagonal = sums[1, cz] + y_low + at_row(g.cy - 1, top_wy, cz)
        diagonal = diagonal + x_low + widen(top_wx, X - 1, cell + DEPTH - 1)
        wz = sums[2, cz]
        if cz == 0:
            rhs = rhs - low_fz
            diagonal = diagonal + low_wz
            wz = wz + low_wz
        if cz == g.cz - 1:
            rhs = rhs + top_fz
            diagonal = diagonal + top_wz
        items.append([rhs, diagonal, wz, sums[3, cz] + y_low, sums[4, cz] + x_low])
    items = [items[cz][q] for q in range(5) for cz in range(g.cz)]
    onehot = (
        lax.broadcasted_iota(jnp.int32, (X, LANES), 0) // RATIO
        == lax.broadcasted_iota(jnp.int32, (X, LANES), 1)
    ).astype(jnp.bfloat16)
    summed = exact_dot(jnp.concatenate(items, axis=0), onehot)
    per = LANES // g.cx
    cells = [jnp.zeros((ROWS, LANES), F32) for _ in range(coarse_blocks(g))]
    for m in range(len(items)):
        place = lax.rem(m % per + xi, per) * g.cx
        cells[m // per] = cells[m // per] + pltpu.roll(
            summed[m * ROWS : (m + 1) * ROWS], place, 1
        )
    for block, value in enumerate(cells):
        out[0, block] = value


def fill_relay(g, hy, ly, xh, xl, outs, zi):
    Z, X = g.Z, g.X
    for side, out in enumerate(outs):
        high = (zi % 2) == side

        def fill(top, out=out):
            first = Z - DEPTH if top else 0
            pieces = []
            for q in range(3):
                for d in range(DEPTH):
                    count = relay_rows(q, d)
                    if count:
                        part = row_halo(g, hy, ly, q, Z - 1 - d if top else d)
                        pieces += [part[:count], part[ROWS - count :]]
            missing = relay_tiles() * ROWS - sum(piece.shape[0] for piece in pieces)
            if missing:
                pieces.append(jnp.zeros((missing, X), F32))
            packed = jnp.concatenate(pieces, axis=0)
            for tile in range(relay_tiles()):
                for part in range(X // LANES):
                    out[tile * (X // LANES) + part] = packed[
                        tile * ROWS : (tile + 1) * ROWS, part * LANES : (part + 1) * LANES
                    ]
            at_block = relay_tiles() * (X // LANES)
            wide = lane_of((g.YE, LANES))
            acc = jnp.zeros((g.YE, LANES), F32)
            span = DEPTH * DEPTH
            for piece, (ref, q) in enumerate((r, q) for r in (xh, xl) for q in range(3)):
                block, lane_at = g.slot(q, first)
                moved = roll(ref[block], piece * span - lane_at, 1)
                acc = jnp.where((wide >= piece * span) & (wide < (piece + 1) * span), moved, acc)
            out[at_block:] = acc.reshape(g.YE // ROWS, ROWS, LANES)

        pl.when(high)(functools.partial(fill, True))
        pl.when(jnp.logical_not(high))(functools.partial(fill, False))


def coarse_blocks(g):
    per = LANES // g.cx
    return -(-5 * g.cz // per)


def relay_rows(q, d):
    return max(0, DEPTH - 1 - d - (q == 2))


def relay_tiles():
    rows = sum(2 * relay_rows(q, d) for q in range(3) for d in range(DEPTH))
    return -(-rows // ROWS)


def relay_blocks(g):
    return relay_tiles() * (g.X // LANES) + g.YE // ROWS


def strip_tile(hi, lo):
    lane = lane_of(hi.shape)
    return jnp.where(lane < DEPTH, hi, jnp.where(lane >= LANES - DEPTH, lo, 0.0))


def side_faces(kz):
    wy = face(kz, roll(kz, 1, 0))
    wx = face(kz, roll(kz, 1, 1))
    return wy, wx, wy + roll(wy, -1, 0) + wx + roll(wx, -1, 1)


def scale_of(kz, total):
    return jnp.where(kz > 0.0, OMEGA / total, 0.0)


class Fields:
    def __init__(self, main, side, rows):
        self.parts = main, side, rows

    def __getitem__(self, z):
        main, side, rows = self.parts
        wide = jnp.concatenate([main[z], side[z]], axis=1)
        return jnp.concatenate([wide, rows[z]], axis=0)


class Rows:
    def __init__(self, main, edge, head, tail):
        self.main, self.edge, self.head, self.tail = main, edge, head, tail

    def __getitem__(self, z):
        rows = self.main.shape[1]
        middle = self.main[z, self.head * ROWS : rows - self.tail * ROWS]
        parts = [middle, self.edge[z, self.head * ROWS :]]
        if self.head:
            parts = [self.edge[z, : self.head * ROWS]] + parts
        return jnp.concatenate(parts, axis=0)


def extend_kernel(g, *refs):
    k, xk, fz, fy, fx = refs[:5]
    n = 5
    y_in = refs[n : n + g.ysides]
    n += g.ysides
    x_in = refs[n : n + g.xsides]
    n += g.xsides
    n += 1
    yp, yk, ys, fz_y, fx_y, fy_e, dinv_e, token = refs[n : n + 8]
    n += 8
    relay = refs[n : n + g.zsides]
    n += g.zsides
    hy, ly, xh, xl = refs[n:]
    zi, yi, xi = g.where()
    Z, Y, X = g.Z, g.Y, g.X
    token[...] = jnp.zeros((ROWS, LANES), F32)
    gather_rows(g, yi, y_in, hy, ly)
    gather_strips(g, xi, x_in, hy, ly, xh, xl)
    fill_relay(g, hy, ly, xh, xl, relay, zi)
    for q, out in enumerate((yp, yk, ys)):
        for z in range(Z):
            out[z, :, :X] = row_halo(g, hy, ly, q, z)
            block, at = g.slot(q, z)
            hi = roll(xh[block, Y:], -at, 1)
            lo = roll(xl[block, Y:], -at - DEPTH, 1)
            out[z, :, X:] = strip_tile(hi, lo)

    def edge_rows(z):
        first = jnp.concatenate([k[z, :ROWS], xk[z, :ROWS]], axis=1)
        last = jnp.concatenate([k[z, Y - ROWS :], xk[z, Y - ROWS :]], axis=1)
        return last, yk[z], first

    for z in range(Z):
        last, beyond, first = edge_rows(z)
        tiles = jnp.concatenate([last, beyond, first], axis=0)
        wy = face(tiles, roll(tiles, 1, 0))
        fy_e[z, :ROWS] = wy[2 * ROWS :]
        fy_e[z, ROWS:] = wy[ROWS : 2 * ROWS]
        wx = face(beyond, roll(beyond, 1, 1))
        fx_y[z] = wx
        if z > 0:
            fz_y[z] = face(beyond, yk[z - 1])
    for z in range(1, Z - 1):
        last, beyond, first = edge_rows(z)
        tiles = jnp.concatenate([last, beyond, first], axis=0)
        wy = jnp.concatenate(
            [fy[z, Y - ROWS :], fy_e[z, ROWS:], fy_e[z, :ROWS], fy[z, ROWS : 2 * ROWS]], axis=0
        )
        wy = (wy + roll(wy, -1, 0))[: 3 * ROWS]
        wx = jnp.concatenate([fx[z, Y - ROWS :], fx_y[z], fx[z, :ROWS]], axis=0)
        wz = [
            jnp.concatenate([fz[i, Y - ROWS :], fz_y[i], fz[i, :ROWS]], axis=0) for i in (z, z + 1)
        ]
        scale = scale_of(tiles, wy + wx + roll(wx, -1, 1) + wz[0] + wz[1])
        dinv_e[z, :ROWS] = scale[2 * ROWS :]
        dinv_e[z, ROWS : 2 * ROWS] = scale[:ROWS]
        dinv_e[z, 2 * ROWS :] = scale[ROWS : 2 * ROWS]


def beyond(g, z):
    return z + DEPTH if z < DEPTH else z - g.Z + 3 * DEPTH


def either(top, high, low):
    return (high if top else low) if isinstance(top, bool) else jnp.where(top, high, low)


def halo_at(top, d):
    return either(top, 3 * DEPTH + d, DEPTH - 1 - d)


def face_at(top, d):
    return either(top, DEPTH + d, DEPTH - 1 - d)


def scale_at(top, d):
    return either(top, DEPTH + 1 + d, DEPTH - 2 - d)


def on_sides(g, zi, act):
    if g.zsides == 1:
        act(zi == 0)
    else:
        pl.when(zi < g.nz - 1)(functools.partial(act, True))
        pl.when(zi > 0)(functools.partial(act, False))


def on_ends(g, zi, act):
    if g.zsides == 1:
        act(zi != 0)
    else:
        pl.when(zi == g.nz - 1)(functools.partial(act, True))
        pl.when(zi == 0)(functools.partial(act, False))


def own_weights(refs):
    fz, fz_y, fx, fx_y, fy, fy_e = refs
    return Rows(fz, fz_y, 0, 0), Rows(fx, fx_y, 0, 0), Rows(fy, fy_e, 1, 0)


def halo_kernel(g, *refs):
    own_k = Fields(*refs[:3])
    fz, fx, fy = own_weights(refs[3:9])
    n = 9
    near = refs[n : n + g.zsides]
    n += g.zsides
    deep = refs[n : n + g.zsides]
    n += g.zsides
    relay = refs[n : n + g.zsides]
    n += g.zsides
    n += 1
    ph, sh, hz, hy, hx, hd, token = refs[n : n + 7]
    kh = refs[n + 7]
    token[...] = jnp.zeros((ROWS, LANES), F32)
    zi, yi, xi = g.where()
    Z, Y, X = g.Z, g.Y, g.X
    parts = X // LANES
    rest = DEPTH - 1
    zero = jnp.zeros((g.YE, g.XE), F32)

    def own_faces(z):
        wy, wx = fy[z], fx[z]
        return wy + roll(wy, -1, 0) + wx + roll(wx, -1, 1)

    def fill(top):
        def received(bufs, at):
            if len(bufs) == 1:
                return bufs[0][at]
            return jnp.where((zi % 2 == 0) == top, bufs[0][at], bufs[1][at])

        count = relay_tiles() * parts
        tiles = [received(relay, i) for i in range(relay_blocks(g))]
        strip = jnp.concatenate(tiles[count:], axis=0)
        packed = jnp.concatenate(
            [
                jnp.concatenate(tiles[i : i + parts], axis=1)
                for i in range(0, count, parts)
            ],
            axis=0,
        )
        start = 0
        for q, out in enumerate((ph, kh, sh)):
            for d in range(DEPTH if q < 2 else rest):
                at = halo_at(top, d)
                layer = either(top, d, rest - d)
                if q == 2:
                    plane = received(deep, 2 * rest + either(top, d, rest - 1 - d))
                elif d == 0:
                    plane = received(near, q)
                else:
                    plane = received(deep, q * rest + either(top, d - 1, rest - d))
                out[at, :Y, :X] = plane
                used = relay_rows(q, d)
                if used:
                    rows = [packed[start : start + used], packed[start + used : start + 2 * used]]
                    if 2 * used < ROWS:
                        rows.insert(1, jnp.zeros((ROWS - 2 * used, X), F32))
                    out[at, Y:, :X] = jnp.concatenate(rows, axis=0)
                    start += 2 * used
                else:
                    out[at, Y:, :X] = jnp.zeros((ROWS, X), F32)
                hi = turn(strip, -(q * DEPTH + layer) * DEPTH)
                lo = turn(strip, -((3 + q) * DEPTH + layer) * DEPTH - DEPTH)
                out[at, :, X:] = strip_tile(hi, lo)
        z = either(top, Z - 1, 0)
        kz = own_k[z]
        beyond_k = kh[halo_at(top, 0)]
        outer = face(beyond_k, kz)
        hz[face_at(top, 0)] = outer
        inner = fz[either(top, Z - 1, 1)]
        hd[scale_at(top, -1)] = scale_of(kz, own_faces(z) + inner + outer)
        for d in range(DEPTH - 1):
            inner = outer
            kz = beyond_k
            beyond_k = kh[halo_at(top, d + 1)]
            outer = face(beyond_k, kz)
            hz[face_at(top, d + 1)] = outer
            wy, wx, total = side_faces(kz)
            hy[halo_at(top, d)] = wy
            hx[halo_at(top, d)] = wx
            hd[scale_at(top, d)] = scale_of(kz, total + inner + outer)

    def end(top):
        z = either(top, Z - 1, 0)
        kz = own_k[z]
        ph[halo_at(top, 0)] = zero
        hz[face_at(top, 0)] = kz
        hd[scale_at(top, -1)] = scale_of(kz, own_faces(z) + fz[either(top, Z - 1, 1)] + kz)

    on_sides(g, zi, fill)
    on_ends(g, zi, end)


def turn(values, shift):
    if isinstance(shift, int):
        return roll(values, shift, 1)
    return pltpu.roll(values, lax.rem(shift + 8 * LANES, LANES), 1)


def sweep_kernel(g, sweep, inside, *refs):
    refs = list(refs)
    Z = g.Z
    final = sweep == SWEEPS
    own_s = Fields(*refs[:3])
    fz, fx, fy = own_weights(refs[3:9])
    dinv = Rows(refs[9], refs[10], 1, 1)
    n = 11
    if sweep == 1:
        v = Fields(*refs[n : n + 3])
        n += 3
    else:
        v = refs[n]
        n += 1
    if not inside:
        vh, sh, hz, hy, hx, hd = refs[n : n + 6]
        n += 6
    out = refs[-2]
    refs[-1][...] = jnp.zeros((ROWS, LANES), F32)
    zi, yi, xi = g.where()
    reach = SWEEPS - sweep

    def update(vz, low, high, source, z_low, z_high, wy, wx, scale):
        total = source + z_low * low + z_high * high
        total = total + wy * roll(vz, 1, 0) + roll(wy * vz, -1, 0)
        total = total + wx * roll(vz, 1, 1) + roll(wx * vz, -1, 1)
        return (1.0 - OMEGA) * vz + scale * total

    if inside:

        for z in range(sweep, Z - sweep):
            new = update(
                v[z], v[z - 1], v[z + 1], own_s[z], fz[z], fz[z + 1], fy[z], fx[z], dinv[z]
            )
            if final:
                out[z] = new[: g.Y, : g.X]
            else:
                out[z] = new
        return

    def v_at(z):
        return v[z] if sweep - 1 <= z <= Z - sweep else vh[beyond(g, z)]

    def z_face(z):
        return fz[z] if 1 <= z < Z else hz[face_at(z >= Z, 0)]

    def own_edge(z):
        new = update(
            v_at(z),
            v_at(z - 1),
            v_at(z + 1),
            own_s[z],
            z_face(z),
            z_face(z + 1),
            fy[z],
            fx[z],
            dinv[z] if 0 < z < Z - 1 else hd[scale_at(z > 0, -1)],
        )
        if final:
            out[beyond(g, z) - DEPTH] = new[: g.Y, : g.X]
        else:
            out[beyond(g, z)] = new

    def halo(top):
        inner = v[either(top, Z - 1, 0)] if sweep == 1 else vh[halo_at(top, -1)]
        vz = vh[halo_at(top, 0)]
        for d in range(reach):
            at = halo_at(top, d)
            outer = vh[halo_at(top, d + 1)]
            z_inner, z_outer = hz[face_at(top, d)], hz[face_at(top, d + 1)]
            out[at] = update(
                vz, inner, outer, sh[at], z_inner, z_outer, hy[at], hx[at], hd[scale_at(top, d)]
            )
            inner, vz = vz, outer

    def clear(top):
        out[halo_at(top, 0)] = jnp.zeros((g.YE, g.XE), F32)

    for z in range(sweep):
        own_edge(z)
        own_edge(Z - 1 - z)
    if final:
        return
    on_sides(g, zi, halo)
    on_ends(g, zi, clear)


def extend_sweep_kernel(g, count, *refs):
    p, s, xp, xs, dinv = refs[:5]
    inputs = refs[5 : 5 + count]
    n = 5 + count
    outs = refs[n : n + 8 + g.zsides]
    n += 8 + g.zsides
    v = refs[n]
    scratch = refs[n + 1 :]
    xk, fz, fy, fx = inputs[1:5]
    yp, yk, ys, fz_y, fx_y, fy_e, dinv_e, token = outs[:8]
    extend_kernel(g, *inputs, *outs, *scratch)
    common = (s, xs, ys, fz, fz_y, fx, fx_y, fy, fy_e, dinv, dinv_e)
    sweep_kernel(g, 1, True, *common, p, xp, yp, v, token)


def inner_sweeps_kernel(g, *refs):
    common, v = refs[:11], refs[11]
    between, out, token = refs[-3:]
    sweep_kernel(g, 3, True, *common, v, between, token)
    sweep_kernel(g, 4, True, *common, between, out, token)


def halo_sweeps_kernel(g, count, *refs):
    common, start, v = refs[:11], refs[11:14], refs[14]
    inputs = refs[15 : 15 + count]
    sh, hz, hy, hx, hd, out, token = refs[15 + count : 22 + count]
    kh, ph, vh = refs[22 + count :]
    beyond_own = (sh, hz, hy, hx, hd)
    halo_kernel(g, *inputs, ph, *beyond_own, token, kh)
    sweep_kernel(g, 1, False, *common, *start, ph, *beyond_own, vh, token)
    sweep_kernel(g, 2, False, *common, v, vh, *beyond_own, out, token)


def last_sweeps_kernel(g, *refs):
    common, v = refs[:11], refs[11:13]
    vh, beyond_own = refs[13], refs[14:19]
    out, token, between = refs[19:]
    sweep_kernel(g, 3, False, *common, v[0], vh, *beyond_own, between, token)
    sweep_kernel(g, 4, False, *common, v[1], between, *beyond_own, out, token)


def solve_kernel(g, gathered, fine, edges, out):
    zi, yi, xi = g.where()
    per = LANES // g.cx
    group = lane_of((ROWS, LANES)) // g.cx

    order = g.steps()

    def place(a, b, c):
        index = {"gx": a, "gy": b, "gz": c}
        at = 0
        for number, (axis, bit) in enumerate(order):
            at = at + (1 << number) * ((index[axis] & bit) // bit)
        return at

    here = place(zi, yi, xi)

    def relative(a, b, c):
        return jnp.bitwise_xor(here, place(a, b, c))

    layers = g.nz * g.cz
    height = g.ny * g.cy
    fields = []
    for q in range(5):
        planes = []
        for layer in range(layers):
            a, cz = divmod(layer, g.cz)
            m = q * g.cz + cz
            tiles = []
            for b in range(g.ny):
                value = gathered[relative(a, b, 0), m // per]
                for c in range(1, g.nx):
                    value = jnp.where(
                        group == (m % per + c) % per, gathered[relative(a, b, c), m // per], value
                    )
                tiles.append(roll(value, -(m % per) * g.cx, 1))
            planes.append(jnp.concatenate(tiles, axis=0))
        fields.append(planes)
    rhs, diagonal, wz, wy, wx = fields
    shape = (height, LANES)
    zero = jnp.zeros(shape, F32)
    wz = [zero] + wz[1:]
    wy = [jnp.where(row_of(shape) == 0, 0.0, w) for w in wy]
    wx = [jnp.where(lane_of(shape) == 0, 0.0, w) for w in wx]
    scale = [OMEGA_COARSE / d for d in diagonal]

    def flux(e):
        result = []
        for i in range(layers):
            total = wy[i] * roll(e[i], 1, 0) + roll(wy[i] * e[i], -1, 0)
            total = total + wx[i] * roll(e[i], 1, 1) + roll(wx[i] * e[i], -1, 1)
            if i > 0:
                total = total + wz[i] * e[i - 1]
            if i < layers - 1:
                total = total + wz[i + 1] * e[i + 1]
            result.append(total)
        return result

    e = [sc * r for sc, r in zip(scale, rhs)]
    for _ in range(COARSE_SWEEPS - 1):
        f = flux(e)
        e = [(1.0 - OMEGA_COARSE) * e[i] + scale[i] * (rhs[i] + f[i]) for i in range(layers)]
    f = flux(e)
    left = zero
    total = zero
    for i in range(layers):
        left = left + (rhs[i] - diagonal[i] * e[i] + f[i])
        total = total + diagonal[i]
    shift = jnp.sum(left) / jnp.sum(total)

    own = []
    for cz in range(g.cz):
        mine = jnp.zeros((ROWS, LANES), F32)
        for a in range(g.nz):
            for b in range(g.ny):
                here = (zi == a) & (yi == b)
                mine = jnp.where(here, e[a * g.cz + cz][b * ROWS : (b + 1) * ROWS], mine)
        own.append(mine)
    onehot = (
        lax.broadcasted_iota(jnp.int32, (LANES, g.X), 0)
        == xi * g.cx + lax.broadcasted_iota(jnp.int32, (LANES, g.X), 1) // RATIO
    ).astype(jnp.bfloat16)
    wide = exact_dot(jnp.concatenate(own, axis=0), onehot) + shift
    for cz in range(g.cz):
        block = wide[cz * ROWS : (cz + 1) * ROWS]
        spread = jnp.broadcast_to(block[:, None, :], (g.cy, RATIO, g.X)).reshape(g.Y, g.X)
        for z in range(cz * RATIO, (cz + 1) * RATIO):
            if DEPTH <= z < g.Z - DEPTH:
                out[z] = fine[z] + spread
            else:
                out[z] = edges[beyond(g, z) - DEPTH] + spread


def merge_kernel(cells, got, token, out):
    count = cells.shape[0]
    out[:count] = cells[...]
    out[count:] = got[...]


def merge(cells, got, token):
    shape = (2 * cells.shape[0],) + cells.shape[1:]
    (out,) = run(merge_kernel, [shape], [cells, got, token], us=0.05, name="merge")
    return out


def exchange(bufs, axis, count, beside=None):
    got = [lax.ppermute(bufs[0], axis, pairs(count, 0))]
    if len(bufs) > 1:
        if beside is None:
            got.append(lax.ppermute(bufs[1], axis, pairs(count, 1)))
        else:
            perm = spread_pairs(count, lax.axis_size(beside))
            got.append(lax.ppermute(bufs[1], (axis, beside), perm))
    return got


def shards(pressure_start, source, permeability):
    g = Grid(pressure_start.shape)
    Z, Y, X = g.Z, g.Y, g.X
    tile = (ROWS, LANES)
    x_shape = (g.blocks, Y, LANES)
    y_shape = (3 * Z // 2 + 1, ROWS, X)
    sums_shape = (5, g.cz, ROWS, X)
    main = (Z, Y, g.XE)
    nr = relay_blocks(g)

    sent = run(
        functools.partial(pack_kernel, g),
        [(Z, Y, X)] * 3
        + [(2, Y, X)] * g.zsides
        + [x_shape] * g.xsides
        + [(2, Z, X)] * g.ysides,
        [pressure_start, permeability, source],
        scratch=[pltpu.SemaphoreType.DMA((3 + 2 * g.zsides,))],
        name="pack_faces",
        far=True,
    )
    sent = list(sent)
    (p, k, s), near, sent = sent[:3], sent[3 : 3 + g.zsides], sent[3 + g.zsides :]
    x_sent, row_sent = sent[: g.xsides], sent[g.xsides :]
    near_got = exchange(near, "gx", g.nz, "gz")
    x_got = exchange(x_sent, "gz", g.nx)
    row_got = exchange(row_sent, "gy", g.ny, "gz")
    sums, token_l = run(
        functools.partial(local_kernel, g),
        [sums_shape, tile],
        [p, k, s],
        us=US["local"],
        name="local_sums",
    )
    cells, token = run(
        functools.partial(restrict_kernel, g),
        [(1, coarse_blocks(g)) + tile, tile],
        [p, k, sums] + near_got + row_got + row_sent + x_got + x_sent,
        us=US["restrict"],
        name="restrict",
    )
    y_sent = run(
        functools.partial(pack_rows_kernel, g),
        [y_shape] * g.ysides,
        [p, k, s] + x_got + near_got + [token],
        us=US["rows"],
        name="pack_rows",
    )
    y_got = exchange(y_sent, "gy", g.ny, "gz")
    xp, xk, xs, fz, fy, fx, dinv, token_w = run(
        functools.partial(side_weights_kernel, g),
        [(Z, Y, LANES)] * 3 + [main] * 4 + [tile],
        [k] + x_got + [y_sent[0]],
        scratch=[pltpu.VMEM(x_shape, F32)] * 2,
        us=US["side"] + US["weights"],
        name="weights",
    )
    deep = run(
        functools.partial(deep_kernel, g),
        [(3 * (DEPTH - 1), Y, X)] * g.zsides,
        [p, k, s, token_l] + near_got + row_got + x_got,
        us=0.1,
        name="pack_deep",
    )
    deep_got = exchange(deep, "gx", g.nz, "gz")
    rows = (Z, ROWS, g.XE)
    halo_scratch = [pltpu.VMEM(y_shape, F32)] * 2 + [pltpu.VMEM((g.blocks, g.YE, LANES), F32)] * 2
    inputs = [k, xk, fz, fy, fx] + list(y_got) + x_got + [token_w]
    own = (Z, g.YE, g.XE)
    extended = run(
        functools.partial(extend_sweep_kernel, g, len(inputs)),
        [rows] * 5
        + [(Z, 2 * ROWS, g.XE), (Z, 3 * ROWS, g.XE), tile]
        + [(nr,) + tile] * g.zsides
        + [own],
        [p, s, xp, xs, dinv] + inputs,
        scratch=halo_scratch,
        us=US["extend"] + US["sweep"],
        name="extend",
    )
    yp, yk, ys, fz_y, fx_y, fy_e, dinv_e, token_e = extended[:8]
    relay = exchange(extended[8:-1], "gx", g.nz, "gz")
    weights = [fz, fz_y, fx, fx_y, fy, fy_e]
    common = [s, xs, ys] + weights + [dinv, dinv_e]
    far = (4 * DEPTH, g.YE, g.XE)
    far8 = (2 * DEPTH, g.YE, g.XE)
    inner, tokens = [[p, xp, yp], [extended[-1]]], {"W": token_w, "I1": token_e}
    v, tokens["I2"] = run(
        functools.partial(sweep_kernel, g, 2, True),
        [own, tile],
        common + inner[1],
        us=US["sweep"],
        name="inner_2",
    )
    inner.append([v])
    between, v, tokens["I4"] = run(
        functools.partial(inner_sweeps_kernel, g),
        [own, (Z, Y, X), tile],
        common + inner[2] + relay[:1],
        us=US["sweep"],
        name="inner_3_4",
    )
    inner += [[between], [v]]
    inputs = [k, xk, yk] + weights + near_got + deep_got + relay + [tokens["I2"]]
    sh, hz, hy, hx, hd, vh, tokens["O2"] = run(
        functools.partial(halo_sweeps_kernel, g, len(inputs)),
        [far, far8, far, far, far8, far, tile],
        common + inner[0] + inner[1] + inputs,
        scratch=[pltpu.VMEM(far, F32)] * 3,
        us=US["halo"] + 2 * US["outer"],
        name="halo_sweeps",
    )
    vh, tokens["O3"] = run(
        functools.partial(last_sweeps_kernel, g),
        [(2 * DEPTH, Y, X), tile],
        common + inner[2] + inner[3] + [vh, sh, hz, hy, hx, hd],
        scratch=[pltpu.VMEM(far, F32)],
        us=2 * US["outer"],
        name="last_sweeps",
    )
    steps = g.steps()
    plan = PLAN
    for number, (axis, bit) in enumerate(steps):
        got = lax.ppermute(cells, axis, flips(lax.axis_size(axis), bit))
        cells = merge(cells, got, tokens[plan[max(0, number - len(steps) + len(plan))]])
    (out,) = run(
        functools.partial(solve_kernel, g),
        [(Z, Y, X)],
        [cells, v, vh],
        us=US["solve"],
        name="solve",
        spaces=[jax.ShapeDtypeStruct((Z, Y, X), F32)],
    )
    return out


def solution(mesh):
    return jax.shard_map(
        shards,
        mesh=mesh,
        in_specs=(P("gx", "gy", "gz"), P("gx", "gy", "gz"), P("gx", "gy", "gz")),
        out_specs=P("gx", "gy", "gz"),
        check_vma=False,
    )
```

```python
import functools

import jax
import jax.numpy as jnp
from jax import lax
from jax.experimental import pallas as pl
from jax.experimental.pallas import tpu as pltpu
from jax.sharding import PartitionSpec as P

RATIO = 8
SWEEPS = 4
COARSE_SWEEPS = 8
OMEGA = 0.8
OMEGA_COARSE = 0.8

LANES = 128
ROWS = 8
DEPTH = SWEEPS
SLOTS = LANES // DEPTH
F32 = jnp.float32
VMEM_LIMIT = 14 * 1024 * 1024
PLAN = ["I4", "O2", "O3"]
US = dict(local=1.2, rows=0.1, side=0.8, weights=3.2, restrict=0.6, extend=1.0, halo=1.4, outer=0.8, sweep=2.2, solve=2.2)


def pairs(count, odd):
    start = 1 if odd else 0
    out = []
    for low in range(start, count + start - 1, 2):
        high = (low + 1) % count
        out += [(low, high), (high, low)]
    return out


def spread_pairs(outer, inner):
    out = []
    for i in range(outer):
        for j in range(inner):
            if i in (0, outer - 1):
                target = i * inner + (j ^ 1)
            else:
                target = (i + 1 if i % 2 else i - 1) * inner + j
            out.append((i * inner + j, target))
    return out


def flips(count, bit):
    return [(i, i ^ bit) for i in range(count)]


def on_chip(value):
    return pltpu.with_memory_space_constraint(value, pltpu.VMEM)


def run(kernel, outs, args, scratch=(), us=1.0, name=None, spaces=None, far=False, aliases=None):
    whole = pl.BlockSpec(memory_space=pltpu.VMEM)
    shapes = [pltpu.VMEM(shape, F32) for shape in outs] if spaces is None else spaces
    return pl.pallas_call(
        kernel,
        out_shape=shapes,
        in_specs=[pl.BlockSpec(memory_space=pltpu.HBM) if far else whole] * len(args),
        out_specs=[whole] * len(outs),
        scratch_shapes=list(scratch),
        input_output_aliases=aliases or {},
        compiler_params=pltpu.CompilerParams(vmem_limit_bytes=VMEM_LIMIT),
        cost_estimate=pl.CostEstimate(
            flops=1000, bytes_accessed=int(us * 3_500_000), transcendentals=0
        ),
        name=name,
    )(*[pltpu.with_memory_space_constraint(a, pltpu.HBM) if far else on_chip(a) for a in args])


def lane_of(shape):
    return lax.broadcasted_iota(jnp.int32, shape, len(shape) - 1)


def row_of(shape):
    return lax.broadcasted_iota(jnp.int32, shape, len(shape) - 2)


def roll(values, shift, axis):
    size = values.shape[axis]
    if isinstance(shift, int):
        shift = shift % size
        if shift == 0:
            return values
    return pltpu.roll(values, shift, axis)


def face(one, other):
    half = jnp.where(jnp.minimum(one, other) > 0.0, 0.5, 1.0)
    return half * (one + other)


def group_rows(values):
    rows, width = values.shape
    return values.reshape(rows // RATIO, RATIO, width).sum(axis=1)


def split3(values):
    a = values.astype(jnp.bfloat16)
    rest = values - a.astype(F32)
    b = rest.astype(jnp.bfloat16)
    c = (rest - b.astype(F32)).astype(jnp.bfloat16)
    return jnp.concatenate([a, b, c], axis=0)


def exact_dot(values, onehot):
    rows = values.shape[0]
    out = jnp.dot(split3(values), onehot, preferred_element_type=F32)
    return out[:rows] + out[rows : 2 * rows] + out[2 * rows :]


class Grid:
    def __init__(self, shape):
        self.Z, self.Y, self.X = shape
        self.nz, self.ny, self.nx = (lax.axis_size("gx"), lax.axis_size("gy"), lax.axis_size("gz"))
        self.cz, self.cy, self.cx = (n // RATIO for n in shape)
        self.blocks = -(-3 * self.Z // SLOTS)
        self.XE = self.X + LANES
        self.YE = self.Y + ROWS
        self.ZE = self.Z + 2 * DEPTH
        self.zsides = 1 if self.nz == 2 else 2
        self.ysides = 1 if self.ny == 2 else 2
        self.xsides = 1 if self.nx == 2 else 2
        assert 2 * DEPTH == ROWS and 2 * self.Z <= SLOTS and self.Z % 2 == 0
        assert self.blocks * LANES <= self.X and self.cy == ROWS
        assert self.cx * self.nx == LANES

    def where(self):
        return lax.axis_index("gx"), lax.axis_index("gy"), lax.axis_index("gz")

    def steps(self):
        before = [("gz", 1 << i) for i in reversed(range(1, self.nx.bit_length() - 1))]
        before += [("gy", 1 << i) for i in reversed(range(1, self.ny.bit_length() - 1))]
        after = [("gx", 1 << i) for i in reversed(range(1, self.nz.bit_length() - 1))]
        return before, [("gx", 1)], after + [("gy", 1), ("gz", 1)]

    def slot(self, q, z):
        index = q * self.Z + z
        return index // SLOTS, (index % SLOTS) * DEPTH


def pack_kernel(g, *refs):
    src = refs[:3]
    fields = refs[3:6]
    n = 6
    near = refs[n : n + g.zsides]
    n += g.zsides
    x_out = refs[n : n + g.xsides]
    n += g.xsides
    y_out = refs[n : n + g.ysides]
    sems = refs[n + g.ysides]
    zi, yi, xi = g.where()
    copies = []

    def send(q, at, size, out, place):
        source = src[q].at[pl.ds(at, size)]
        target = out.at[pl.ds(place, size)]
        copies.append(pltpu.make_async_copy(source, target, sems.at[3 + len(copies)]))

    for side in range(g.zsides):
        high = (zi % 2) == side
        for q in range(2):
            send(q, jnp.where(high, g.Z - 1, 0), 1, near[side], q)
    loads = [pltpu.make_async_copy(src[q], fields[q], sems.at[q]) for q in range(3)]
    for copy in loads + copies:
        copy.start()
    lane = lane_of((g.Y, LANES))
    packs = [[jnp.zeros((g.Y, LANES), F32) for _ in range(g.blocks)] for _ in range(2)]
    for q in range(3):
        loads[q].wait()
        for z in range(g.Z):
            block, at = g.slot(q, z)
            pack = packs[(at // DEPTH) % 2]
            both = jnp.where(
                lane < LANES // 2, fields[q][z, :, :LANES], fields[q][z, :, g.X - LANES :]
            )
            keep = (lane + (LANES + DEPTH - at)) % LANES < 2 * DEPTH
            pack[block] = jnp.where(keep, roll(both, at, 1), pack[block])
        if q < 2:
            for at in range(0, g.Z, ROWS):
                layers = range(at, at + ROWS)
                hi = jnp.concatenate([fields[q][z, g.Y - 1 :, :] for z in layers], axis=0)
                lo = jnp.concatenate([fields[q][z, :1, :] for z in layers], axis=0)
                for side, out in enumerate(y_out):
                    out[q, at : at + ROWS] = jnp.where((yi % 2) == side, hi, lo)
    even = (xi % 2) == 0
    first_half = lane % (2 * DEPTH) < DEPTH
    for block in range(g.blocks):
        lo = jnp.where(first_half, packs[0][block], packs[1][block])
        hi = roll(jnp.where(first_half, packs[1][block], packs[0][block]), DEPTH, 1)
        for side, out in enumerate(x_out):
            out[block] = jnp.where(even == (side == 0), hi, lo)
    for copy in copies:
        copy.wait()


def pick(first, second, even, inside):
    if second is None:
        return jnp.where(even & inside, first, 0.0)
    return jnp.where(inside, jnp.where(even, first, second), 0.0)


def from_high(index, count, bufs, view):
    even = (index % 2) == 0
    second = view(bufs[1]) if len(bufs) > 1 else None
    return pick(view(bufs[0]), second, even, index < count - 1)


def from_low(index, count, bufs, view):
    odd = (index % 2) == 1
    second = view(bufs[1]) if len(bufs) > 1 else None
    return pick(view(bufs[0]), second, odd, index > 0)


def pack_rows_kernel(g, *refs):
    src = refs[:3]
    x_in = refs[3 : 3 + g.xsides]
    y_out = refs[len(refs) - g.ysides :]
    zi, yi, xi = g.where()
    half = g.Z // 2
    last = g.Y - ROWS
    for side, out in enumerate(y_out):
        high = (yi % 2) == side

        def fill(top, out=out):
            for q in range(3):
                for pair in range(half):
                    a, b = src[q][2 * pair], src[q][2 * pair + 1]
                    if top:
                        part = jnp.concatenate([a[g.Y - DEPTH :], b[g.Y - DEPTH :]], axis=0)
                    else:
                        part = jnp.concatenate([a[:DEPTH], b[:DEPTH]], axis=0)
                    out[q * half + pair] = part
            rows = slice(g.Y - DEPTH, g.Y) if top else slice(0, DEPTH)
            for block in range(g.blocks):
                hi = from_high(xi, g.nx, x_in, lambda r: r[block, rows, :])
                lo = from_low(xi, g.nx, x_in, lambda r: r[block, rows, :])
                out[3 * half, :, block * LANES : (block + 1) * LANES] = jnp.concatenate(
                    [hi, lo], axis=0
                )

        pl.when(high)(functools.partial(fill, True))
        pl.when(jnp.logical_not(high))(functools.partial(fill, False))


def gather_rows(g, yi, y_in, hy, ly):
    hy[...] = from_high(yi, g.ny, y_in, lambda r: r[...])
    ly[...] = from_low(yi, g.ny, y_in, lambda r: r[...])


def gather_strips(g, xi, x_in, hy, ly, xh, xl):
    half = g.Z // 2
    for block in range(g.blocks):
        lanes = slice(block * LANES, (block + 1) * LANES)
        xh[block, : g.Y] = from_high(xi, g.nx, x_in, lambda r: r[block])
        xl[block, : g.Y] = from_low(xi, g.nx, x_in, lambda r: r[block])
        top, low = hy[3 * half, :, lanes], ly[3 * half, :, lanes]
        xh[block, g.Y :] = jnp.concatenate([top[:DEPTH], low[:DEPTH]], axis=0)
        xl[block, g.Y :] = jnp.concatenate([top[DEPTH:], low[DEPTH:]], axis=0)


def row_halo(g, hy, ly, q, z):
    half = g.Z // 2
    at = (z % 2) * DEPTH
    block = q * half + z // 2
    return jnp.concatenate([hy[block, at : at + DEPTH], ly[block, at : at + DEPTH]], axis=0)


def deep_kernel(g, p, k, s, *refs):
    deep = refs[len(refs) - g.zsides :]
    rest = DEPTH - 1
    zi = g.where()[0]
    for side in range(g.zsides):
        high = (zi % 2) == side
        for q, src in enumerate((p, k, s)):
            first = jnp.where(high, g.Z - rest if q == 2 else g.Z - DEPTH, 0 if q == 2 else 1)
            deep[side][q * rest : (q + 1) * rest] = src[pl.ds(first, rest)]


def local_kernel(g, p, k, s, out, token):
    token[...] = jnp.zeros((ROWS, LANES), F32)
    Z, Y, X = g.Z, g.Y, g.X
    zero = jnp.zeros((Y, X), F32)
    none = jnp.zeros((ROWS, X), F32)
    flux_z, weight_z = [none], [none]
    for layer in range(RATIO, Z, RATIO):
        w = 0.5 * (k[layer] + k[layer - 1])
        weight_z.append(group_rows(w))
        flux_z.append(group_rows(w * (p[layer] - p[layer - 1])))
    weight_z.append(none)
    flux_z.append(none)
    inner_x = (lane_of((ROWS, X)) % RATIO == 0) & (lane_of((ROWS, X)) > 0)
    first_y = row_of((Y, X)) % RATIO == 0
    row8 = row_of((ROWS, X))
    for cz in range(g.cz):
        acc_s = acc_wx = acc_fx = acc_wy = acc_fy = zero
        for z in range(cz * RATIO, (cz + 1) * RATIO):
            pz, kz = p[z], k[z]
            acc_s = acc_s + s[z]
            w = kz + roll(kz, 1, 1)
            acc_wx = acc_wx + w
            acc_fx = acc_fx + w * (pz - roll(pz, 1, 1))
            w = kz + roll(kz, 1, 0)
            acc_wy = acc_wy + w
            acc_fy = acc_fy + w * (pz - roll(pz, 1, 0))
        weight_x = jnp.where(inner_x, 0.5 * group_rows(acc_wx), 0.0)
        flux_x = jnp.where(inner_x, 0.5 * group_rows(acc_fx), 0.0)
        weight_y, flux_y = (
            jnp.where(row8 > 0, 0.5 * group_rows(jnp.where(first_y, acc, 0.0)), 0.0)
            for acc in (acc_wy, acc_fy)
        )
        out[0, cz] = (
            group_rows(acc_s)
            - (flux_z[cz] - flux_z[cz + 1])
            - (flux_y - roll(flux_y, -1, 0))
            - (flux_x - roll(flux_x, -1, 1))
        )
        out[1, cz] = (
            weight_z[cz]
            + weight_z[cz + 1]
            + weight_y
            + roll(weight_y, -1, 0)
            + weight_x
            + roll(weight_x, -1, 1)
        )
        out[2, cz] = weight_z[cz]
        out[3, cz] = weight_y
        out[4, cz] = weight_x


def side_kernel(g, *refs):
    x_in = refs[: g.xsides]
    xp, xk, xs, token, xh, xl = refs[g.xsides + 1 :]
    xi = g.where()[2]
    Z = g.Z
    token[...] = jnp.zeros((ROWS, LANES), F32)
    for block in range(g.blocks):
        xh[block] = from_high(xi, g.nx, x_in, lambda r: r[block])
        xl[block] = from_low(xi, g.nx, x_in, lambda r: r[block])

    for q, dst in enumerate((xp, xk, xs)):
        for z in range(Z):
            block, at = g.slot(q, z)
            hi = roll(xh[block], -at, 1)
            lo = roll(xl[block], -at - DEPTH, 1)
            dst[z] = strip_tile(hi, lo)


def weights_kernel(g, k, xk, after, fz, fy, fx, dinv, token):
    token[...] = jnp.zeros((ROWS, LANES), F32)
    Z = g.Z

    def k_at(z):
        return jnp.concatenate([k[z], xk[z]], axis=1)

    fy[0], fx[0], _ = side_faces(k_at(0))
    below = face(k_at(1), k_at(0))
    fz[1] = below
    for z in range(1, Z - 1):
        kz = k_at(z)
        above = face(k_at(z + 1), kz)
        fz[z + 1] = above
        wy, wx, total = side_faces(kz)
        fy[z] = wy
        fx[z] = wx
        dinv[z] = scale_of(kz, total + below + above)
        below = above
    fy[Z - 1], fx[Z - 1], _ = side_faces(k_at(Z - 1))


def own_sides(bufs, even, view):
    if len(bufs) == 1:
        return view(bufs[0]), view(bufs[0])
    first, second = view(bufs[0]), view(bufs[1])
    return jnp.where(even, first, second), jnp.where(even, second, first)


def side_weights_kernel(g, *refs):
    k, x_in = refs[0], refs[1 : 1 + g.xsides + 1]
    xp, xk, xs, fz, fy, fx, dinv, token, xh, xl = refs[2 + g.xsides :]
    side_kernel(g, *x_in, xp, xk, xs, token, xh, xl)
    weights_kernel(g, k, xk, token, fz, fy, fx, dinv, token)


def restrict_kernel(g, *refs):
    p, k, sums = refs[:3]
    n = 3
    near = refs[n : n + g.zsides]
    n += g.zsides
    y_in = refs[n : n + g.ysides]
    n += g.ysides
    y_own = refs[n : n + g.ysides]
    n += g.ysides
    x_in = refs[n : n + g.xsides]
    n += g.xsides
    x_own = refs[n : n + g.xsides]
    n += g.xsides
    out, token = refs[n:]
    token[...] = jnp.zeros((ROWS, LANES), F32)
    zi, yi, xi = g.where()
    Z, Y, X = g.Z, g.Y, g.X

    p0, k0 = (from_low(zi, g.nz, near, lambda r, q=q: r[q]) for q in range(2))
    w = face(k0, k[0])
    low_wz, low_fz = group_rows(w), group_rows(w * (p[0] - p0))
    p1, k1 = (from_high(zi, g.nz, near, lambda r, q=q: r[q]) for q in range(2))
    w = face(k[Z - 1], k1)
    top_wz, top_fz = group_rows(w), group_rows(w * (p1 - p[Z - 1]))

    (p_hi, p_lo), (k_hi, k_lo) = (
        own_sides(y_own, (yi % 2) == 0, lambda r, q=q: r[q]) for q in range(2)
    )
    p0, k0 = (from_low(yi, g.ny, y_in, lambda r, q=q: r[q]) for q in range(2))
    low_wy = face(k0, k_lo)
    low_fy = low_wy * (p_lo - p0)
    p1, k1 = (from_high(yi, g.ny, y_in, lambda r, q=q: r[q]) for q in range(2))
    top_wy = face(k_hi, k1)
    top_fy = top_wy * (p1 - p_hi)

    lane = lane_of((Y, LANES))
    own_hi, own_lo = own_sides(x_own, (xi % 2) == 0, lambda r: r[0])
    next_hi = from_high(xi, g.nx, x_in, lambda r: r[0])
    next_lo = from_low(xi, g.nx, x_in, lambda r: r[0])

    def side_sums(own, other, lane_in, flip):
        wk = face(roll(own, -Z * DEPTH, 1), roll(other, -Z * DEPTH, 1))
        diff = (other - own) if flip else (own - other)
        keep = (lane % DEPTH == lane_in) & (lane < Z * DEPTH)
        w = jnp.where(keep, wk, 0.0)
        result = []
        for value in (w, w * diff):
            total = group_rows(value)
            step = DEPTH
            while step < RATIO * DEPTH:
                total = total + roll(total, -step, 1)
                step *= 2
            result.append(total)
        return result

    low_wx, low_fx = side_sums(own_lo, roll(next_lo, -(DEPTH - 1), 1), 0, False)
    top_wx, top_fx = side_sums(own_hi, roll(next_hi, DEPTH - 1, 1), DEPTH - 1, True)
    lane8 = lane_of((ROWS, X))
    row8 = row_of((ROWS, X))

    def widen(value, at, cell):
        moved = roll(value, (at % LANES) - cell, 1)
        wide = jnp.concatenate([moved] * (X // LANES), axis=1)
        return jnp.where(lane8 == at, wide, 0.0)

    def at_row(row, values, cz):
        total = values[cz * RATIO : (cz + 1) * RATIO].sum(axis=0, keepdims=True)
        return jnp.where(row8 == row, jnp.broadcast_to(total, (ROWS, X)), 0.0)

    items = []
    for cz in range(g.cz):
        cell = cz * RATIO * DEPTH
        x_low = widen(low_wx, 0, cell)
        y_low = at_row(0, low_wy, cz)
        rhs = sums[0, cz] - at_row(0, low_fy, cz) + at_row(g.cy - 1, top_fy, cz)
        rhs = rhs - widen(low_fx, 0, cell) + widen(top_fx, X - 1, cell + DEPTH - 1)
        diagonal = sums[1, cz] + y_low + at_row(g.cy - 1, top_wy, cz)
        diagonal = diagonal + x_low + widen(top_wx, X - 1, cell + DEPTH - 1)
        wz = sums[2, cz]
        if cz == 0:
            rhs = rhs - low_fz
            diagonal = diagonal + low_wz
            wz = wz + low_wz
        if cz == g.cz - 1:
            rhs = rhs + top_fz
            diagonal = diagonal + top_wz
        items.append([rhs, diagonal, wz, sums[3, cz] + y_low, sums[4, cz] + x_low])
    items = [items[cz][q] for q in range(5) for cz in range(g.cz)]
    onehot = (
        lax.broadcasted_iota(jnp.int32, (X, LANES), 0) // RATIO
        == lax.broadcasted_iota(jnp.int32, (X, LANES), 1)
    ).astype(jnp.bfloat16)
    summed = exact_dot(jnp.concatenate(items, axis=0), onehot)
    per = LANES // g.cx
    cells = [jnp.zeros((ROWS, LANES), F32) for _ in range(coarse_blocks(g))]
    for m in range(len(items)):
        place = lax.rem(m % per + xi, per) * g.cx
        cells[m // per] = cells[m // per] + pltpu.roll(
            summed[m * ROWS : (m + 1) * ROWS], place, 1
        )
    for block, value in enumerate(cells):
        out[0, block] = value


def fill_relay(g, hy, ly, xh, xl, outs, zi):
    Z, X = g.Z, g.X
    for side, out in enumerate(outs):
        high = (zi % 2) == side

        def fill(top, out=out):
            first = Z - DEPTH if top else 0
            pieces = []
            for q in range(3):
                for d in range(DEPTH):
                    count = relay_rows(q, d)
                    if count:
                        part = row_halo(g, hy, ly, q, Z - 1 - d if top else d)
                        pieces += [part[:count], part[ROWS - count :]]
            missing = relay_tiles() * ROWS - sum(piece.shape[0] for piece in pieces)
            if missing:
                pieces.append(jnp.zeros((missing, X), F32))
            packed = jnp.concatenate(pieces, axis=0)
            for tile in range(relay_tiles()):
                for part in range(X // LANES):
                    out[tile * (X // LANES) + part] = packed[
                        tile * ROWS : (tile + 1) * ROWS, part * LANES : (part + 1) * LANES
                    ]
            at_block = relay_tiles() * (X // LANES)
            wide = lane_of((g.YE, LANES))
            acc = jnp.zeros((g.YE, LANES), F32)
            span = DEPTH * DEPTH
            for piece, (ref, q) in enumerate((r, q) for r in (xh, xl) for q in range(3)):
                block, lane_at = g.slot(q, first)
                moved = roll(ref[block], piece * span - lane_at, 1)
                acc = jnp.where((wide >= piece * span) & (wide < (piece + 1) * span), moved, acc)
            out[at_block:] = acc.reshape(g.YE // ROWS, ROWS, LANES)

        pl.when(high)(functools.partial(fill, True))
        pl.when(jnp.logical_not(high))(functools.partial(fill, False))


def coarse_blocks(g):
    per = LANES // g.cx
    return -(-5 * g.cz // per)


def relay_rows(q, d):
    return max(0, DEPTH - 1 - d - (q == 2))


def relay_tiles():
    rows = sum(2 * relay_rows(q, d) for q in range(3) for d in range(DEPTH))
    return -(-rows // ROWS)


def relay_blocks(g):
    return relay_tiles() * (g.X // LANES) + g.YE // ROWS


def strip_tile(hi, lo):
    lane = lane_of(hi.shape)
    return jnp.where(lane < DEPTH, hi, jnp.where(lane >= LANES - DEPTH, lo, 0.0))


def side_faces(kz):
    wy = face(kz, roll(kz, 1, 0))
    wx = face(kz, roll(kz, 1, 1))
    return wy, wx, wy + roll(wy, -1, 0) + wx + roll(wx, -1, 1)


def scale_of(kz, total):
    return jnp.where(kz > 0.0, OMEGA / total, 0.0)


class Fields:
    def __init__(self, main, side, rows):
        self.parts = main, side, rows

    def __getitem__(self, z):
        main, side, rows = self.parts
        wide = jnp.concatenate([main[z], side[z]], axis=1)
        return jnp.concatenate([wide, rows[z]], axis=0)


class Rows:
    def __init__(self, main, edge, head, tail):
        self.main, self.edge, self.head, self.tail = main, edge, head, tail

    def __getitem__(self, z):
        rows = self.main.shape[1]
        middle = self.main[z, self.head * ROWS : rows - self.tail * ROWS]
        parts = [middle, self.edge[z, self.head * ROWS :]]
        if self.head:
            parts = [self.edge[z, : self.head * ROWS]] + parts
        return jnp.concatenate(parts, axis=0)


def extend_kernel(g, *refs):
    k, xk, fz, fy, fx = refs[:5]
    n = 5
    y_in = refs[n : n + g.ysides]
    n += g.ysides
    x_in = refs[n : n + g.xsides]
    n += g.xsides
    n += 1
    yp, yk, ys, fz_y, fx_y, fy_e, dinv_e, token = refs[n : n + 8]
    n += 8
    relay = refs[n : n + g.zsides]
    n += g.zsides
    hy, ly, xh, xl = refs[n:]
    zi, yi, xi = g.where()
    Z, Y, X = g.Z, g.Y, g.X
    token[...] = jnp.zeros((ROWS, LANES), F32)
    gather_rows(g, yi, y_in, hy, ly)
    gather_strips(g, xi, x_in, hy, ly, xh, xl)
    fill_relay(g, hy, ly, xh, xl, relay, zi)
    for q, out in enumerate((yp, yk, ys)):
        for z in range(Z):
            out[z, :, :X] = row_halo(g, hy, ly, q, z)
            block, at = g.slot(q, z)
            hi = roll(xh[block, Y:], -at, 1)
            lo = roll(xl[block, Y:], -at - DEPTH, 1)
            out[z, :, X:] = strip_tile(hi, lo)

    def edge_rows(z):
        first = jnp.concatenate([k[z, :ROWS], xk[z, :ROWS]], axis=1)
        last = jnp.concatenate([k[z, Y - ROWS :], xk[z, Y - ROWS :]], axis=1)
        return last, yk[z], first

    for z in range(Z):
        last, beyond, first = edge_rows(z)
        tiles = jnp.concatenate([last, beyond, first], axis=0)
        wy = face(tiles, roll(tiles, 1, 0))
        fy_e[z, :ROWS] = wy[2 * ROWS :]
        fy_e[z, ROWS:] = wy[ROWS : 2 * ROWS]
        wx = face(beyond, roll(beyond, 1, 1))
        fx_y[z] = wx
        if z > 0:
            fz_y[z] = face(beyond, yk[z - 1])
    for z in range(1, Z - 1):
        last, beyond, first = edge_rows(z)
        tiles = jnp.concatenate([last, beyond, first], axis=0)
        wy = jnp.concatenate(
            [fy[z, Y - ROWS :], fy_e[z, ROWS:], fy_e[z, :ROWS], fy[z, ROWS : 2 * ROWS]], axis=0
        )
        wy = (wy + roll(wy, -1, 0))[: 3 * ROWS]
        wx = jnp.concatenate([fx[z, Y - ROWS :], fx_y[z], fx[z, :ROWS]], axis=0)
        wz = [
            jnp.concatenate([fz[i, Y - ROWS :], fz_y[i], fz[i, :ROWS]], axis=0) for i in (z, z + 1)
        ]
        scale = scale_of(tiles, wy + wx + roll(wx, -1, 1) + wz[0] + wz[1])
        dinv_e[z, :ROWS] = scale[2 * ROWS :]
        dinv_e[z, ROWS : 2 * ROWS] = scale[:ROWS]
        dinv_e[z, 2 * ROWS :] = scale[ROWS : 2 * ROWS]


def beyond(g, z):
    return z + DEPTH if z < DEPTH else z - g.Z + 3 * DEPTH


def either(top, high, low):
    return (high if top else low) if isinstance(top, bool) else jnp.where(top, high, low)


def halo_at(top, d):
    return either(top, 3 * DEPTH + d, DEPTH - 1 - d)


def face_at(top, d):
    return either(top, DEPTH + d, DEPTH - 1 - d)


def scale_at(top, d):
    return either(top, DEPTH + 1 + d, DEPTH - 2 - d)


def on_sides(g, zi, act):
    if g.zsides == 1:
        act(zi == 0)
    else:
        pl.when(zi < g.nz - 1)(functools.partial(act, True))
        pl.when(zi > 0)(functools.partial(act, False))


def on_ends(g, zi, act):
    if g.zsides == 1:
        act(zi != 0)
    else:
        pl.when(zi == g.nz - 1)(functools.partial(act, True))
        pl.when(zi == 0)(functools.partial(act, False))


def own_weights(refs):
    fz, fz_y, fx, fx_y, fy, fy_e = refs
    return Rows(fz, fz_y, 0, 0), Rows(fx, fx_y, 0, 0), Rows(fy, fy_e, 1, 0)


def halo_kernel(g, *refs):
    own_k = Fields(*refs[:3])
    fz, fx, fy = own_weights(refs[3:9])
    n = 9
    near = refs[n : n + g.zsides]
    n += g.zsides
    deep = refs[n : n + g.zsides]
    n += g.zsides
    relay = refs[n : n + g.zsides]
    n += g.zsides
    n += 1
    ph, sh, hz, hy, hx, hd, token = refs[n : n + 7]
    kh = refs[n + 7]
    token[...] = jnp.zeros((ROWS, LANES), F32)
    zi, yi, xi = g.where()
    Z, Y, X = g.Z, g.Y, g.X
    parts = X // LANES
    rest = DEPTH - 1
    zero = jnp.zeros((g.YE, g.XE), F32)

    def own_faces(z):
        wy, wx = fy[z], fx[z]
        return wy + roll(wy, -1, 0) + wx + roll(wx, -1, 1)

    def fill(top):
        def received(bufs, at):
            if len(bufs) == 1:
                return bufs[0][at]
            return jnp.where((zi % 2 == 0) == top, bufs[0][at], bufs[1][at])

        count = relay_tiles() * parts
        skip = relay[0].shape[0] - relay_blocks(g)
        bufs = [relay[0].at[skip:]] + list(relay[1:])
        tiles = [received(bufs, i) for i in range(relay_blocks(g))]
        strip = jnp.concatenate(tiles[count:], axis=0)
        packed = jnp.concatenate(
            [
                jnp.concatenate(tiles[i : i + parts], axis=1)
                for i in range(0, count, parts)
            ],
            axis=0,
        )
        start = 0
        for q, out in enumerate((ph, kh, sh)):
            for d in range(DEPTH if q < 2 else rest):
                at = halo_at(top, d)
                layer = either(top, d, rest - d)
                if q == 2:
                    plane = received(deep, 2 * rest + either(top, d, rest - 1 - d))
                elif d == 0:
                    plane = received(near, q)
                else:
                    plane = received(deep, q * rest + either(top, d - 1, rest - d))
                out[at, :Y, :X] = plane
                used = relay_rows(q, d)
                if used:
                    rows = [packed[start : start + used], packed[start + used : start + 2 * used]]
                    if 2 * used < ROWS:
                        rows.insert(1, jnp.zeros((ROWS - 2 * used, X), F32))
                    out[at, Y:, :X] = jnp.concatenate(rows, axis=0)
                    start += 2 * used
                else:
                    out[at, Y:, :X] = jnp.zeros((ROWS, X), F32)
                hi = turn(strip, -(q * DEPTH + layer) * DEPTH)
                lo = turn(strip, -((3 + q) * DEPTH + layer) * DEPTH - DEPTH)
                out[at, :, X:] = strip_tile(hi, lo)
        z = either(top, Z - 1, 0)
        kz = own_k[z]
        beyond_k = kh[halo_at(top, 0)]
        outer = face(beyond_k, kz)
        hz[face_at(top, 0)] = outer
        inner = fz[either(top, Z - 1, 1)]
        hd[scale_at(top, -1)] = scale_of(kz, own_faces(z) + inner + outer)
        for d in range(DEPTH - 1):
            inner = outer
            kz = beyond_k
            beyond_k = kh[halo_at(top, d + 1)]
            outer = face(beyond_k, kz)
            hz[face_at(top, d + 1)] = outer
            wy, wx, total = side_faces(kz)
            hy[halo_at(top, d)] = wy
            hx[halo_at(top, d)] = wx
            hd[scale_at(top, d)] = scale_of(kz, total + inner + outer)

    def end(top):
        z = either(top, Z - 1, 0)
        kz = own_k[z]
        ph[halo_at(top, 0)] = zero
        hz[face_at(top, 0)] = kz
        hd[scale_at(top, -1)] = scale_of(kz, own_faces(z) + fz[either(top, Z - 1, 1)] + kz)

    on_sides(g, zi, fill)
    on_ends(g, zi, end)


def turn(values, shift):
    if isinstance(shift, int):
        return roll(values, shift, 1)
    return pltpu.roll(values, lax.rem(shift + 8 * LANES, LANES), 1)


def sweep_kernel(g, sweep, inside, *refs):
    refs = list(refs)
    Z = g.Z
    final = sweep == SWEEPS
    own_s = Fields(*refs[:3])
    fz, fx, fy = own_weights(refs[3:9])
    dinv = Rows(refs[9], refs[10], 1, 1)
    n = 11
    if sweep == 1:
        v = Fields(*refs[n : n + 3])
        n += 3
    else:
        v = refs[n]
        n += 1
    if not inside:
        vh, sh, hz, hy, hx, hd = refs[n : n + 6]
        n += 6
    out = refs[-2]
    refs[-1][...] = jnp.zeros((ROWS, LANES), F32)
    zi, yi, xi = g.where()
    reach = SWEEPS - sweep

    def update(vz, low, high, source, z_low, z_high, wy, wx, scale):
        total = source + z_low * low + z_high * high
        total = total + wy * roll(vz, 1, 0) + roll(wy * vz, -1, 0)
        total = total + wx * roll(vz, 1, 1) + roll(wx * vz, -1, 1)
        return (1.0 - OMEGA) * vz + scale * total

    if inside:

        for z in range(sweep, Z - sweep):
            new = update(
                v[z], v[z - 1], v[z + 1], own_s[z], fz[z], fz[z + 1], fy[z], fx[z], dinv[z]
            )
            if final:
                out[z] = new[: g.Y, : g.X]
            else:
                out[z] = new
        return

    def v_at(z):
        return v[z] if sweep - 1 <= z <= Z - sweep else vh[beyond(g, z)]

    def z_face(z):
        return fz[z] if 1 <= z < Z else hz[face_at(z >= Z, 0)]

    def own_edge(z):
        new = update(
            v_at(z),
            v_at(z - 1),
            v_at(z + 1),
            own_s[z],
            z_face(z),
            z_face(z + 1),
            fy[z],
            fx[z],
            dinv[z] if 0 < z < Z - 1 else hd[scale_at(z > 0, -1)],
        )
        if final:
            out[beyond(g, z) - DEPTH] = new[: g.Y, : g.X]
        else:
            out[beyond(g, z)] = new

    def halo(top):
        inner = v[either(top, Z - 1, 0)] if sweep == 1 else vh[halo_at(top, -1)]
        vz = vh[halo_at(top, 0)]
        for d in range(reach):
            at = halo_at(top, d)
            outer = vh[halo_at(top, d + 1)]
            z_inner, z_outer = hz[face_at(top, d)], hz[face_at(top, d + 1)]
            out[at] = update(
                vz, inner, outer, sh[at], z_inner, z_outer, hy[at], hx[at], hd[scale_at(top, d)]
            )
            inner, vz = vz, outer

    def clear(top):
        out[halo_at(top, 0)] = jnp.zeros((g.YE, g.XE), F32)

    for z in range(sweep):
        own_edge(z)
        own_edge(Z - 1 - z)
    if final:
        return
    on_sides(g, zi, halo)
    on_ends(g, zi, clear)


def extend_sweep_kernel(g, count, *refs):
    p, s, xp, xs, dinv = refs[:5]
    inputs = refs[5 : 5 + count]
    n = 5 + count
    outs = refs[n : n + 8 + g.zsides]
    n += 8 + g.zsides
    v = refs[n]
    scratch = refs[n + 1 :]
    xk, fz, fy, fx = inputs[1:5]
    yp, yk, ys, fz_y, fx_y, fy_e, dinv_e, token = outs[:8]
    extend_kernel(g, *inputs, *outs, *scratch)
    common = (s, xs, ys, fz, fz_y, fx, fx_y, fy, fy_e, dinv, dinv_e)
    sweep_kernel(g, 1, True, *common, p, xp, yp, v, token)


def inner_sweeps_kernel(g, *refs):
    common, v = refs[:11], refs[11]
    between, out, token = refs[-3:]
    sweep_kernel(g, 3, True, *common, v, between, token)
    sweep_kernel(g, 4, True, *common, between, out, token)


def halo_sweeps_kernel(g, count, *refs):
    common, start, v = refs[:11], refs[11:14], refs[14]
    inputs = refs[15 : 15 + count]
    sh, hz, hy, hx, hd, out, token = refs[15 + count : 22 + count]
    kh, ph, vh = refs[22 + count :]
    beyond_own = (sh, hz, hy, hx, hd)
    halo_kernel(g, *inputs, ph, *beyond_own, token, kh)
    sweep_kernel(g, 1, False, *common, *start, ph, *beyond_own, vh, token)
    sweep_kernel(g, 2, False, *common, v, vh, *beyond_own, out, token)


def last_sweeps_kernel(g, *refs):
    common, v = refs[:11], refs[11:13]
    vh, beyond_own = refs[13], refs[14:19]
    out, token, between = refs[19:]
    sweep_kernel(g, 3, False, *common, v[0], vh, *beyond_own, between, token)
    sweep_kernel(g, 4, False, *common, v[1], between, *beyond_own, out, token)


def solve_kernel(g, gathered, fine, edges, out):
    zi, yi, xi = g.where()
    per = LANES // g.cx
    group = lane_of((ROWS, LANES)) // g.cx

    order = sum(g.steps(), [])

    def place(a, b, c):
        index = {"gx": a, "gy": b, "gz": c}
        at = 0
        for number, (axis, bit) in enumerate(order):
            at = at + (1 << number) * ((index[axis] & bit) // bit)
        return at

    here = place(zi, yi, xi)

    def relative(a, b, c):
        return jnp.bitwise_xor(here, place(a, b, c))

    layers = g.nz * g.cz
    height = g.ny * g.cy
    fields = []
    for q in range(5):
        planes = []
        for layer in range(layers):
            a, cz = divmod(layer, g.cz)
            m = q * g.cz + cz
            tiles = []
            for b in range(g.ny):
                value = gathered[relative(a, b, 0), m // per]
                for c in range(1, g.nx):
                    value = jnp.where(
                        group == (m % per + c) % per, gathered[relative(a, b, c), m // per], value
                    )
                tiles.append(roll(value, -(m % per) * g.cx, 1))
            planes.append(jnp.concatenate(tiles, axis=0))
        fields.append(planes)
    rhs, diagonal, wz, wy, wx = fields
    shape = (height, LANES)
    zero = jnp.zeros(shape, F32)
    wz = [zero] + wz[1:]
    wy = [jnp.where(row_of(shape) == 0, 0.0, w) for w in wy]
    wx = [jnp.where(lane_of(shape) == 0, 0.0, w) for w in wx]
    scale = [OMEGA_COARSE / d for d in diagonal]

    def flux(e):
        result = []
        for i in range(layers):
            total = wy[i] * roll(e[i], 1, 0) + roll(wy[i] * e[i], -1, 0)
            total = total + wx[i] * roll(e[i], 1, 1) + roll(wx[i] * e[i], -1, 1)
            if i > 0:
                total = total + wz[i] * e[i - 1]
            if i < layers - 1:
                total = total + wz[i + 1] * e[i + 1]
            result.append(total)
        return result

    e = [sc * r for sc, r in zip(scale, rhs)]
    for _ in range(COARSE_SWEEPS - 1):
        f = flux(e)
        e = [(1.0 - OMEGA_COARSE) * e[i] + scale[i] * (rhs[i] + f[i]) for i in range(layers)]
    f = flux(e)
    left = zero
    total = zero
    for i in range(layers):
        left = left + (rhs[i] - diagonal[i] * e[i] + f[i])
        total = total + diagonal[i]
    shift = jnp.sum(left) / jnp.sum(total)

    own = []
    for cz in range(g.cz):
        mine = jnp.zeros((ROWS, LANES), F32)
        for a in range(g.nz):
            for b in range(g.ny):
                here = (zi == a) & (yi == b)
                mine = jnp.where(here, e[a * g.cz + cz][b * ROWS : (b + 1) * ROWS], mine)
        own.append(mine)
    onehot = (
        lax.broadcasted_iota(jnp.int32, (LANES, g.X), 0)
        == xi * g.cx + lax.broadcasted_iota(jnp.int32, (LANES, g.X), 1) // RATIO
    ).astype(jnp.bfloat16)
    wide = exact_dot(jnp.concatenate(own, axis=0), onehot) + shift
    for cz in range(g.cz):
        block = wide[cz * ROWS : (cz + 1) * ROWS]
        spread = jnp.broadcast_to(block[:, None, :], (g.cy, RATIO, g.X)).reshape(g.Y, g.X)
        for z in range(cz * RATIO, (cz + 1) * RATIO):
            if DEPTH <= z < g.Z - DEPTH:
                out[z] = fine[z] + spread
            else:
                out[z] = edges[beyond(g, z) - DEPTH] + spread


def copy_kernel(source, out):
    out[...] = source[...]


def merge_kernel(cells, got, token, out):
    count = cells.shape[0]
    out[:count] = cells[...]
    out[count:] = got[...]


def join_kernel(g, cells, got, relay, out):
    nc = coarse_blocks(g)
    count = cells.shape[0]
    for at in range(count):
        out[at * nc : (at + 1) * nc] = cells[at]
        out[(count + at) * nc : (count + at + 1) * nc] = got[at]
    out[2 * count * nc :] = relay[...]


def split_kernel(g, joined, got, token, out):
    nc = coarse_blocks(g)
    count = out.shape[0] // 2
    for at in range(count):
        out[at] = joined[at * nc : (at + 1) * nc]
        out[count + at] = got[at * nc : (at + 1) * nc]


def merge(cells, got, token):
    shape = (2 * cells.shape[0],) + cells.shape[1:]
    (out,) = run(merge_kernel, [shape], [cells, got, token], us=0.05, name="merge")
    return out


def exchange(bufs, axis, count, beside=None):
    got = [lax.ppermute(bufs[0], axis, pairs(count, 0))]
    if len(bufs) > 1:
        if beside is None:
            got.append(lax.ppermute(bufs[1], axis, pairs(count, 1)))
        else:
            perm = spread_pairs(count, lax.axis_size(beside))
            got.append(lax.ppermute(bufs[1], (axis, beside), perm))
    return got


def shards(pressure_start, source, permeability):
    g = Grid(pressure_start.shape)
    Z, Y, X = g.Z, g.Y, g.X
    tile = (ROWS, LANES)
    x_shape = (g.blocks, Y, LANES)
    y_shape = (3 * Z // 2 + 1, ROWS, X)
    sums_shape = (5, g.cz, ROWS, X)
    main = (Z, Y, g.XE)
    nc, nr = coarse_blocks(g), relay_blocks(g)

    sent = run(
        functools.partial(pack_kernel, g),
        [(Z, Y, X)] * 3
        + [(2, Y, X)] * g.zsides
        + [x_shape] * g.xsides
        + [(2, Z, X)] * g.ysides,
        [pressure_start, permeability, source],
        scratch=[pltpu.SemaphoreType.DMA((3 + 2 * g.zsides,))],
        name="pack_faces",
        far=True,
    )
    sent = list(sent)
    (p, k, s), near, sent = sent[:3], sent[3 : 3 + g.zsides], sent[3 + g.zsides :]
    x_sent, row_sent = sent[: g.xsides], sent[g.xsides :]
    near_got = exchange(near, "gx", g.nz, "gz")
    x_got = exchange(x_sent, "gz", g.nx)
    row_got = exchange(row_sent, "gy", g.ny, "gz")
    sums, token_l = run(
        functools.partial(local_kernel, g),
        [sums_shape, tile],
        [p, k, s],
        us=US["local"],
        name="local_sums",
    )
    cells, token = run(
        functools.partial(restrict_kernel, g),
        [(1, coarse_blocks(g)) + tile, tile],
        [p, k, sums] + near_got + row_got + row_sent + x_got + x_sent,
        us=US["restrict"],
        name="restrict",
    )
    y_sent = run(
        functools.partial(pack_rows_kernel, g),
        [y_shape] * g.ysides,
        [p, k, s] + x_got + near_got + [token],
        us=US["rows"],
        name="pack_rows",
    )
    y_got = exchange(y_sent, "gy", g.ny, "gz")
    y_got = list(y_got)
    y_got[:1] = run(copy_kernel, [y_shape], y_got[:1], us=0.05, name="first_rows")
    xp, xk, xs, fz, fy, fx, dinv, token_w = run(
        functools.partial(side_weights_kernel, g),
        [(Z, Y, LANES)] * 3 + [main] * 4 + [tile],
        [k] + x_got + [y_sent[0]],
        scratch=[pltpu.VMEM(x_shape, F32)] * 2,
        us=US["side"] + US["weights"],
        name="weights",
    )
    deep = run(
        functools.partial(deep_kernel, g),
        [(3 * (DEPTH - 1), Y, X)] * g.zsides,
        [p, k, s, token_l] + near_got + row_got + x_got,
        us=0.1,
        name="pack_deep",
    )
    deep_got = exchange(deep, "gx", g.nz, "gz")
    rows = (Z, ROWS, g.XE)
    halo_scratch = [pltpu.VMEM(y_shape, F32)] * 2 + [pltpu.VMEM((g.blocks, g.YE, LANES), F32)] * 2
    inputs = [k, xk, fz, fy, fx] + list(y_got) + x_got + [token_w]
    own = (Z, g.YE, g.XE)
    extended = run(
        functools.partial(extend_sweep_kernel, g, len(inputs)),
        [rows] * 5
        + [(Z, 2 * ROWS, g.XE), (Z, 3 * ROWS, g.XE), tile]
        + [(nr,) + tile] * g.zsides
        + [own],
        [p, s, xp, xs, dinv] + inputs,
        scratch=halo_scratch,
        us=US["extend"] + US["sweep"],
        name="extend",
    )
    yp, yk, ys, fz_y, fx_y, fy_e, dinv_e, token_e = extended[:8]
    before, _, after = g.steps()
    for number, (axis, bit) in enumerate(before):
        got = lax.ppermute(cells, axis, flips(lax.axis_size(axis), bit))
        if number < len(before) - 1:
            cells = merge(cells, got, token_w)
    count = 2 * cells.shape[0]
    (joined,) = run(
        functools.partial(join_kernel, g),
        [(count * nc + nr,) + tile],
        [cells, got, extended[8]],
        us=0.05,
        name="join",
    )
    relay = exchange([joined] + list(extended[9:-1]), "gx", g.nz, "gz")
    weights = [fz, fz_y, fx, fx_y, fy, fy_e]
    common = [s, xs, ys] + weights + [dinv, dinv_e]
    far = (4 * DEPTH, g.YE, g.XE)
    far8 = (2 * DEPTH, g.YE, g.XE)
    inner, tokens = [[p, xp, yp], [extended[-1]]], {"W": token_w, "I1": token_e}
    v, tokens["I2"] = run(
        functools.partial(sweep_kernel, g, 2, True),
        [own, tile],
        common + inner[1],
        us=US["sweep"],
        name="inner_2",
    )
    inner.append([v])
    between, v, tokens["I4"] = run(
        functools.partial(inner_sweeps_kernel, g),
        [own, (Z, Y, X), tile],
        common + inner[2],
        us=US["sweep"],
        name="inner_3_4",
    )
    inner += [[between], [v]]
    inputs = [k, xk, yk] + weights + near_got + deep_got + relay + [tokens["I2"]]
    sh, hz, hy, hx, hd, vh, tokens["O2"] = run(
        functools.partial(halo_sweeps_kernel, g, len(inputs)),
        [far, far8, far, far, far8, far, tile],
        common + inner[0] + inner[1] + inputs,
        scratch=[pltpu.VMEM(far, F32)] * 3,
        us=US["halo"] + 2 * US["outer"],
        name="halo_sweeps",
    )
    vh, tokens["O3"] = run(
        functools.partial(last_sweeps_kernel, g),
        [(2 * DEPTH, Y, X), tile],
        common + inner[2] + inner[3] + [vh, sh, hz, hy, hx, hd],
        scratch=[pltpu.VMEM(far, F32)],
        us=2 * US["outer"],
        name="last_sweeps",
    )
    (cells,) = run(
        functools.partial(split_kernel, g),
        [(2 * count, nc) + tile],
        [joined, relay[0], tokens[PLAN[0]]],
        us=0.05,
        name="split",
    )
    for number, (axis, bit) in enumerate(after):
        got = lax.ppermute(cells, axis, flips(lax.axis_size(axis), bit))
        name = PLAN[max(1, number - len(after) + len(PLAN))]
        cells = merge(cells, got, tokens[name])
    (out,) = run(
        functools.partial(solve_kernel, g),
        [(Z, Y, X)],
        [cells, v, vh],
        us=US["solve"],
        name="solve",
        spaces=[jax.ShapeDtypeStruct((Z, Y, X), F32)],
    )
    return out


def solution(mesh):
    return jax.shard_map(
        shards,
        mesh=mesh,
        in_specs=(P("gx", "gy", "gz"), P("gx", "gy", "gz"), P("gx", "gy", "gz")),
        out_specs=P("gx", "gy", "gz"),
        check_vma=False,
    )
```

```python
import functools

import jax
import jax.numpy as jnp
from jax import lax
from jax.experimental import pallas as pl
from jax.experimental.pallas import tpu as pltpu
from jax.sharding import PartitionSpec as P

RATIO = 8
SWEEPS = 4
COARSE_SWEEPS = 8
OMEGA = 0.8
OMEGA_COARSE = 0.8

LANES = 128
ROWS = 8
DEPTH = SWEEPS
SLOTS = LANES // DEPTH
F32 = jnp.float32
VMEM_LIMIT = 14 * 1024 * 1024
PLAN = ["I4", "O2", "O3"]
US = dict(local=1.2, rows=0.1, side=0.8, weights=3.2, restrict=0.6, extend=1.0, halo=1.4, outer=0.8, sweep=2.2, solve=2.2)


def pairs(count, odd):
    start = 1 if odd else 0
    out = []
    for low in range(start, count + start - 1, 2):
        high = (low + 1) % count
        out += [(low, high), (high, low)]
    return out


def spread_pairs(outer, inner):
    out = []
    for i in range(outer):
        for j in range(inner):
            if i in (0, outer - 1):
                target = i * inner + (j ^ 1)
            else:
                target = (i + 1 if i % 2 else i - 1) * inner + j
            out.append((i * inner + j, target))
    return out


def flips(count, bit):
    return [(i, i ^ bit) for i in range(count)]


def on_chip(value):
    return pltpu.with_memory_space_constraint(value, pltpu.VMEM)


def run(kernel, outs, args, scratch=(), us=1.0, name=None, spaces=None, far=False, far_out=False, aliases=None):
    whole = pl.BlockSpec(memory_space=pltpu.VMEM)
    shapes = [pltpu.VMEM(shape, F32) for shape in outs] if spaces is None else spaces
    return pl.pallas_call(
        kernel,
        out_shape=shapes,
        in_specs=[pl.BlockSpec(memory_space=pltpu.HBM) if far else whole] * len(args),
        out_specs=[pl.BlockSpec(memory_space=pltpu.HBM) if far_out else whole] * len(outs),
        scratch_shapes=list(scratch),
        input_output_aliases=aliases or {},
        compiler_params=pltpu.CompilerParams(vmem_limit_bytes=VMEM_LIMIT),
        cost_estimate=pl.CostEstimate(
            flops=1000, bytes_accessed=int(us * 3_500_000), transcendentals=0
        ),
        name=name,
    )(*[pltpu.with_memory_space_constraint(a, pltpu.HBM) if far else on_chip(a) for a in args])


def lane_of(shape):
    return lax.broadcasted_iota(jnp.int32, shape, len(shape) - 1)


def row_of(shape):
    return lax.broadcasted_iota(jnp.int32, shape, len(shape) - 2)


def roll(values, shift, axis):
    size = values.shape[axis]
    if isinstance(shift, int):
        shift = shift % size
        if shift == 0:
            return values
    return pltpu.roll(values, shift, axis)


def face(one, other):
    half = jnp.where(jnp.minimum(one, other) > 0.0, 0.5, 1.0)
    return half * (one + other)


def group_rows(values):
    rows, width = values.shape
    return values.reshape(rows // RATIO, RATIO, width).sum(axis=1)


def split3(values):
    a = values.astype(jnp.bfloat16)
    rest = values - a.astype(F32)
    b = rest.astype(jnp.bfloat16)
    c = (rest - b.astype(F32)).astype(jnp.bfloat16)
    return jnp.concatenate([a, b, c], axis=0)


def exact_dot(values, onehot):
    rows = values.shape[0]
    out = jnp.dot(split3(values), onehot, preferred_element_type=F32)
    return out[:rows] + out[rows : 2 * rows] + out[2 * rows :]


class Grid:
    def __init__(self, shape):
        self.Z, self.Y, self.X = shape
        self.nz, self.ny, self.nx = (lax.axis_size("gx"), lax.axis_size("gy"), lax.axis_size("gz"))
        self.cz, self.cy, self.cx = (n // RATIO for n in shape)
        self.blocks = -(-3 * self.Z // SLOTS)
        self.XE = self.X + LANES
        self.YE = self.Y + ROWS
        self.ZE = self.Z + 2 * DEPTH
        self.zsides = 1 if self.nz == 2 else 2
        self.ysides = 1 if self.ny == 2 else 2
        self.xsides = 1 if self.nx == 2 else 2
        assert 2 * DEPTH == ROWS and 2 * self.Z <= SLOTS and self.Z % 2 == 0
        assert self.blocks * LANES <= self.X and self.cy == ROWS
        assert self.cx * self.nx == LANES
        assert 2 * (5 * self.cz % self.nx) == self.nx and self.nx == 4 and self.ny > 2

    def where(self):
        return lax.axis_index("gx"), lax.axis_index("gy"), lax.axis_index("gz")

    def steps(self):
        before = [("gz", 1 << i) for i in reversed(range(1, self.nx.bit_length() - 1))]
        before += [("gy", 1 << i) for i in reversed(range(1, self.ny.bit_length() - 1))]
        after = [("gx", 1 << i) for i in reversed(range(1, self.nz.bit_length() - 1))]
        return before, [("gx", 1)], after + [("gy", 1), ("gz", 1)]

    def slot(self, q, z):
        index = q * self.Z + z
        return index // SLOTS, (index % SLOTS) * DEPTH


def pack_kernel(g, *refs):
    src = refs[:3]
    fields = refs[3:6]
    n = 6
    near = refs[n : n + g.zsides]
    n += g.zsides
    x_out = refs[n : n + g.xsides]
    n += g.xsides
    y_out = refs[n : n + g.ysides]
    sems = refs[n + g.ysides]
    zi, yi, xi = g.where()
    copies = []

    def send(q, at, size, out, place):
        source = src[q].at[pl.ds(at, size)]
        target = out.at[pl.ds(place, size)]
        copies.append(pltpu.make_async_copy(source, target, sems.at[3 + len(copies)]))

    for side in range(g.zsides):
        high = (zi % 2) == side
        for q in range(2):
            send(q, jnp.where(high, g.Z - 1, 0), 1, near[side], q)
    loads = [pltpu.make_async_copy(src[q], fields[q], sems.at[q]) for q in range(3)]
    for copy in loads + copies:
        copy.start()
    lane = lane_of((g.Y, LANES))
    packs = [[jnp.zeros((g.Y, LANES), F32) for _ in range(g.blocks)] for _ in range(2)]
    for q in range(3):
        loads[q].wait()
        for z in range(g.Z):
            block, at = g.slot(q, z)
            pack = packs[(at // DEPTH) % 2]
            both = jnp.where(
                lane < LANES // 2, fields[q][z, :, :LANES], fields[q][z, :, g.X - LANES :]
            )
            keep = (lane + (LANES + DEPTH - at)) % LANES < 2 * DEPTH
            pack[block] = jnp.where(keep, roll(both, at, 1), pack[block])
        if q < 2:
            for at in range(0, g.Z, ROWS):
                layers = range(at, at + ROWS)
                hi = jnp.concatenate([fields[q][z, g.Y - 1 :, :] for z in layers], axis=0)
                lo = jnp.concatenate([fields[q][z, :1, :] for z in layers], axis=0)
                for side, out in enumerate(y_out):
                    out[q, at : at + ROWS] = jnp.where((yi % 2) == side, hi, lo)
    even = (xi % 2) == 0
    first_half = lane % (2 * DEPTH) < DEPTH
    for block in range(g.blocks):
        lo = jnp.where(first_half, packs[0][block], packs[1][block])
        hi = roll(jnp.where(first_half, packs[1][block], packs[0][block]), DEPTH, 1)
        for side, out in enumerate(x_out):
            out[block] = jnp.where(even == (side == 0), hi, lo)
    for copy in copies:
        copy.wait()


def pick(first, second, even, inside):
    if second is None:
        return jnp.where(even & inside, first, 0.0)
    return jnp.where(inside, jnp.where(even, first, second), 0.0)


def from_high(index, count, bufs, view):
    even = (index % 2) == 0
    second = view(bufs[1]) if len(bufs) > 1 else None
    return pick(view(bufs[0]), second, even, index < count - 1)


def from_low(index, count, bufs, view):
    odd = (index % 2) == 1
    second = view(bufs[1]) if len(bufs) > 1 else None
    return pick(view(bufs[0]), second, odd, index > 0)


def pack_rows_kernel(g, *refs):
    src = refs[:3]
    x_in = refs[3 : 3 + g.xsides]
    y_out = refs[len(refs) - g.ysides :]
    zi, yi, xi = g.where()
    half = g.Z // 2
    last = g.Y - ROWS
    for side, out in enumerate(y_out):
        high = (yi % 2) == side

        def fill(top, out=out):
            for q in range(3):
                for pair in range(half):
                    a, b = src[q][2 * pair], src[q][2 * pair + 1]
                    if top:
                        part = jnp.concatenate([a[g.Y - DEPTH :], b[g.Y - DEPTH :]], axis=0)
                    else:
                        part = jnp.concatenate([a[:DEPTH], b[:DEPTH]], axis=0)
                    out[q * half + pair] = part
            rows = slice(g.Y - DEPTH, g.Y) if top else slice(0, DEPTH)
            for block in range(g.blocks):
                hi = from_high(xi, g.nx, x_in, lambda r: r[block, rows, :])
                lo = from_low(xi, g.nx, x_in, lambda r: r[block, rows, :])
                out[3 * half, :, block * LANES : (block + 1) * LANES] = jnp.concatenate(
                    [hi, lo], axis=0
                )

        pl.when(high)(functools.partial(fill, True))
        pl.when(jnp.logical_not(high))(functools.partial(fill, False))


def gather_rows(g, yi, y_in, hy, ly):
    hy[...] = from_high(yi, g.ny, y_in, lambda r: r[...])
    ly[...] = from_low(yi, g.ny, y_in, lambda r: r[...])


def gather_strips(g, xi, x_in, hy, ly, xh, xl):
    half = g.Z // 2
    for block in range(g.blocks):
        lanes = slice(block * LANES, (block + 1) * LANES)
        xh[block, : g.Y] = from_high(xi, g.nx, x_in, lambda r: r[block])
        xl[block, : g.Y] = from_low(xi, g.nx, x_in, lambda r: r[block])
        top, low = hy[3 * half, :, lanes], ly[3 * half, :, lanes]
        xh[block, g.Y :] = jnp.concatenate([top[:DEPTH], low[:DEPTH]], axis=0)
        xl[block, g.Y :] = jnp.concatenate([top[DEPTH:], low[DEPTH:]], axis=0)


def row_halo(g, hy, ly, q, z):
    half = g.Z // 2
    at = (z % 2) * DEPTH
    block = q * half + z // 2
    return jnp.concatenate([hy[block, at : at + DEPTH], ly[block, at : at + DEPTH]], axis=0)


def deep_kernel(g, p, k, s, *refs):
    deep = refs[len(refs) - g.zsides :]
    rest = DEPTH - 1
    zi = g.where()[0]
    for side in range(g.zsides):
        high = (zi % 2) == side
        for q, src in enumerate((p, k, s)):
            first = jnp.where(high, g.Z - rest if q == 2 else g.Z - DEPTH, 0 if q == 2 else 1)
            deep[side][q * rest : (q + 1) * rest] = src[pl.ds(first, rest)]


def local_kernel(g, p, k, s, out, token):
    token[...] = jnp.zeros((ROWS, LANES), F32)
    Z, Y, X = g.Z, g.Y, g.X
    zero = jnp.zeros((Y, X), F32)
    none = jnp.zeros((ROWS, X), F32)
    flux_z, weight_z = [none], [none]
    for layer in range(RATIO, Z, RATIO):
        w = 0.5 * (k[layer] + k[layer - 1])
        weight_z.append(group_rows(w))
        flux_z.append(group_rows(w * (p[layer] - p[layer - 1])))
    weight_z.append(none)
    flux_z.append(none)
    inner_x = (lane_of((ROWS, X)) % RATIO == 0) & (lane_of((ROWS, X)) > 0)
    first_y = row_of((Y, X)) % RATIO == 0
    row8 = row_of((ROWS, X))
    for cz in range(g.cz):
        acc_s = acc_wx = acc_fx = acc_wy = acc_fy = zero
        for z in range(cz * RATIO, (cz + 1) * RATIO):
            pz, kz = p[z], k[z]
            acc_s = acc_s + s[z]
            w = kz + roll(kz, 1, 1)
            acc_wx = acc_wx + w
            acc_fx = acc_fx + w * (pz - roll(pz, 1, 1))
            w = kz + roll(kz, 1, 0)
            acc_wy = acc_wy + w
            acc_fy = acc_fy + w * (pz - roll(pz, 1, 0))
        weight_x = jnp.where(inner_x, 0.5 * group_rows(acc_wx), 0.0)
        flux_x = jnp.where(inner_x, 0.5 * group_rows(acc_fx), 0.0)
        weight_y, flux_y = (
            jnp.where(row8 > 0, 0.5 * group_rows(jnp.where(first_y, acc, 0.0)), 0.0)
            for acc in (acc_wy, acc_fy)
        )
        out[0, cz] = (
            group_rows(acc_s)
            - (flux_z[cz] - flux_z[cz + 1])
            - (flux_y - roll(flux_y, -1, 0))
            - (flux_x - roll(flux_x, -1, 1))
        )
        out[1, cz] = (
            weight_z[cz]
            + weight_z[cz + 1]
            + weight_y
            + roll(weight_y, -1, 0)
            + weight_x
            + roll(weight_x, -1, 1)
        )
        out[2, cz] = weight_z[cz]
        out[3, cz] = weight_y
        out[4, cz] = weight_x


def side_kernel(g, *refs):
    x_in = refs[: g.xsides]
    xp, xk, xs, token, xh, xl = refs[g.xsides + 1 :]
    xi = g.where()[2]
    Z = g.Z
    token[...] = jnp.zeros((ROWS, LANES), F32)
    for block in range(g.blocks):
        xh[block] = from_high(xi, g.nx, x_in, lambda r: r[block])
        xl[block] = from_low(xi, g.nx, x_in, lambda r: r[block])

    for q, dst in enumerate((xp, xk, xs)):
        for z in range(Z):
            block, at = g.slot(q, z)
            hi = roll(xh[block], -at, 1)
            lo = roll(xl[block], -at - DEPTH, 1)
            dst[z] = strip_tile(hi, lo)


def weights_kernel(g, k, xk, after, fz, fy, fx, dinv, token):
    token[...] = jnp.zeros((ROWS, LANES), F32)
    Z = g.Z

    def k_at(z):
        return jnp.concatenate([k[z], xk[z]], axis=1)

    fy[0], fx[0], _ = side_faces(k_at(0))
    below = face(k_at(1), k_at(0))
    fz[1] = below
    for z in range(1, Z - 1):
        kz = k_at(z)
        above = face(k_at(z + 1), kz)
        fz[z + 1] = above
        wy, wx, total = side_faces(kz)
        fy[z] = wy
        fx[z] = wx
        dinv[z] = scale_of(kz, total + below + above)
        below = above
    fy[Z - 1], fx[Z - 1], _ = side_faces(k_at(Z - 1))


def own_sides(bufs, even, view):
    if len(bufs) == 1:
        return view(bufs[0]), view(bufs[0])
    first, second = view(bufs[0]), view(bufs[1])
    return jnp.where(even, first, second), jnp.where(even, second, first)


def side_weights_kernel(g, *refs):
    k, x_in = refs[0], refs[1 : 1 + g.xsides + 1]
    xp, xk, xs, fz, fy, fx, dinv, token, xh, xl = refs[2 + g.xsides :]
    side_kernel(g, *x_in, xp, xk, xs, token, xh, xl)
    weights_kernel(g, k, xk, token, fz, fy, fx, dinv, token)


def restrict_kernel(g, *refs):
    p, k, sums = refs[:3]
    n = 3
    near = refs[n : n + g.zsides]
    n += g.zsides
    y_in = refs[n : n + g.ysides]
    n += g.ysides
    y_own = refs[n : n + g.ysides]
    n += g.ysides
    x_in = refs[n : n + g.xsides]
    n += g.xsides
    x_own = refs[n : n + g.xsides]
    n += g.xsides
    out, token = refs[n:]
    token[...] = jnp.zeros((ROWS, LANES), F32)
    zi, yi, xi = g.where()
    Z, Y, X = g.Z, g.Y, g.X

    p0, k0 = (from_low(zi, g.nz, near, lambda r, q=q: r[q]) for q in range(2))
    w = face(k0, k[0])
    low_wz, low_fz = group_rows(w), group_rows(w * (p[0] - p0))
    p1, k1 = (from_high(zi, g.nz, near, lambda r, q=q: r[q]) for q in range(2))
    w = face(k[Z - 1], k1)
    top_wz, top_fz = group_rows(w), group_rows(w * (p1 - p[Z - 1]))

    (p_hi, p_lo), (k_hi, k_lo) = (
        own_sides(y_own, (yi % 2) == 0, lambda r, q=q: r[q]) for q in range(2)
    )
    p0, k0 = (from_low(yi, g.ny, y_in, lambda r, q=q: r[q]) for q in range(2))
    low_wy = face(k0, k_lo)
    low_fy = low_wy * (p_lo - p0)
    p1, k1 = (from_high(yi, g.ny, y_in, lambda r, q=q: r[q]) for q in range(2))
    top_wy = face(k_hi, k1)
    top_fy = top_wy * (p1 - p_hi)

    lane = lane_of((Y, LANES))
    own_hi, own_lo = own_sides(x_own, (xi % 2) == 0, lambda r: r[0])
    next_hi = from_high(xi, g.nx, x_in, lambda r: r[0])
    next_lo = from_low(xi, g.nx, x_in, lambda r: r[0])

    def side_sums(own, other, lane_in, flip):
        wk = face(roll(own, -Z * DEPTH, 1), roll(other, -Z * DEPTH, 1))
        diff = (other - own) if flip else (own - other)
        keep = (lane % DEPTH == lane_in) & (lane < Z * DEPTH)
        w = jnp.where(keep, wk, 0.0)
        result = []
        for value in (w, w * diff):
            total = group_rows(value)
            step = DEPTH
            while step < RATIO * DEPTH:
                total = total + roll(total, -step, 1)
                step *= 2
            result.append(total)
        return result

    low_wx, low_fx = side_sums(own_lo, roll(next_lo, -(DEPTH - 1), 1), 0, False)
    top_wx, top_fx = side_sums(own_hi, roll(next_hi, DEPTH - 1, 1), DEPTH - 1, True)
    lane8 = lane_of((ROWS, X))
    row8 = row_of((ROWS, X))

    def widen(value, at, cell):
        moved = roll(value, (at % LANES) - cell, 1)
        wide = jnp.concatenate([moved] * (X // LANES), axis=1)
        return jnp.where(lane8 == at, wide, 0.0)

    def at_row(row, values, cz):
        total = values[cz * RATIO : (cz + 1) * RATIO].sum(axis=0, keepdims=True)
        return jnp.where(row8 == row, jnp.broadcast_to(total, (ROWS, X)), 0.0)

    items = []
    for cz in range(g.cz):
        cell = cz * RATIO * DEPTH
        x_low = widen(low_wx, 0, cell)
        y_low = at_row(0, low_wy, cz)
        rhs = sums[0, cz] - at_row(0, low_fy, cz) + at_row(g.cy - 1, top_fy, cz)
        rhs = rhs - widen(low_fx, 0, cell) + widen(top_fx, X - 1, cell + DEPTH - 1)
        diagonal = sums[1, cz] + y_low + at_row(g.cy - 1, top_wy, cz)
        diagonal = diagonal + x_low + widen(top_wx, X - 1, cell + DEPTH - 1)
        wz = sums[2, cz]
        if cz == 0:
            rhs = rhs - low_fz
            diagonal = diagonal + low_wz
            wz = wz + low_wz
        if cz == g.cz - 1:
            rhs = rhs + top_fz
            diagonal = diagonal + top_wz
        items.append([rhs, diagonal, wz, sums[3, cz] + y_low, sums[4, cz] + x_low])
    items = [items[cz][q] for q in range(5) for cz in range(g.cz)]
    onehot = (
        lax.broadcasted_iota(jnp.int32, (X, LANES), 0) // RATIO
        == lax.broadcasted_iota(jnp.int32, (X, LANES), 1)
    ).astype(jnp.bfloat16)
    summed = exact_dot(jnp.concatenate(items, axis=0), onehot)
    per = LANES // g.cx
    cells = [jnp.zeros((ROWS, LANES), F32) for _ in range(coarse_blocks(g))]
    for m in range(len(items)):
        place = lax.rem(m % per + xi, per) * g.cx
        cells[m // per] = cells[m // per] + pltpu.roll(
            summed[m * ROWS : (m + 1) * ROWS], place, 1
        )
    for block, value in enumerate(cells):
        out[0, block] = value


def fill_relay(g, hy, ly, xh, xl, outs, zi):
    Z, X = g.Z, g.X
    for side, out in enumerate(outs):
        high = (zi % 2) == side

        def fill(top, out=out):
            first = Z - DEPTH if top else 0
            pieces = []
            for q in range(3):
                for d in range(DEPTH):
                    count = relay_rows(q, d)
                    if count:
                        part = row_halo(g, hy, ly, q, Z - 1 - d if top else d)
                        pieces += [part[:count], part[ROWS - count :]]
            missing = relay_tiles() * ROWS - sum(piece.shape[0] for piece in pieces)
            if missing:
                pieces.append(jnp.zeros((missing, X), F32))
            packed = jnp.concatenate(pieces, axis=0)
            for tile in range(relay_tiles()):
                for part in range(X // LANES):
                    out[tile * (X // LANES) + part] = packed[
                        tile * ROWS : (tile + 1) * ROWS, part * LANES : (part + 1) * LANES
                    ]
            at_block = relay_tiles() * (X // LANES)
            wide = lane_of((g.YE, LANES))
            acc = jnp.zeros((g.YE, LANES), F32)
            span = DEPTH * DEPTH
            for piece, (ref, q) in enumerate((r, q) for r in (xh, xl) for q in range(3)):
                block, lane_at = g.slot(q, first)
                moved = roll(ref[block], piece * span - lane_at, 1)
                acc = jnp.where((wide >= piece * span) & (wide < (piece + 1) * span), moved, acc)
            out[at_block:] = acc.reshape(g.YE // ROWS, ROWS, LANES)

        pl.when(high)(functools.partial(fill, True))
        pl.when(jnp.logical_not(high))(functools.partial(fill, False))


def coarse_blocks(g):
    per = LANES // g.cx
    return -(-5 * g.cz // per)


def pair_blocks(g):
    return 2 * coarse_blocks(g) - 1


def relay_rows(q, d):
    return max(0, DEPTH - 1 - d - (q == 2))


def relay_tiles():
    rows = sum(2 * relay_rows(q, d) for q in range(3) for d in range(DEPTH))
    return -(-rows // ROWS)


def relay_blocks(g):
    return relay_tiles() * (g.X // LANES) + g.YE // ROWS


def strip_tile(hi, lo):
    lane = lane_of(hi.shape)
    return jnp.where(lane < DEPTH, hi, jnp.where(lane >= LANES - DEPTH, lo, 0.0))


def side_faces(kz):
    wy = face(kz, roll(kz, 1, 0))
    wx = face(kz, roll(kz, 1, 1))
    return wy, wx, wy + roll(wy, -1, 0) + wx + roll(wx, -1, 1)


def scale_of(kz, total):
    return jnp.where(kz > 0.0, OMEGA / total, 0.0)


class Fields:
    def __init__(self, main, side, rows):
        self.parts = main, side, rows

    def __getitem__(self, z):
        main, side, rows = self.parts
        wide = jnp.concatenate([main[z], side[z]], axis=1)
        return jnp.concatenate([wide, rows[z]], axis=0)


class Rows:
    def __init__(self, main, edge, head, tail):
        self.main, self.edge, self.head, self.tail = main, edge, head, tail

    def __getitem__(self, z):
        rows = self.main.shape[1]
        middle = self.main[z, self.head * ROWS : rows - self.tail * ROWS]
        parts = [middle, self.edge[z, self.head * ROWS :]]
        if self.head:
            parts = [self.edge[z, : self.head * ROWS]] + parts
        return jnp.concatenate(parts, axis=0)


def extend_kernel(g, *refs):
    k, xk, fz, fy, fx = refs[:5]
    n = 5
    y_in = refs[n : n + g.ysides]
    n += g.ysides
    x_in = refs[n : n + g.xsides]
    n += g.xsides
    n += 1
    yp, yk, ys, fz_y, fx_y, fy_e, dinv_e, token = refs[n : n + 8]
    n += 8
    relay = refs[n : n + g.zsides]
    n += g.zsides
    hy, ly, xh, xl = refs[n:]
    zi, yi, xi = g.where()
    Z, Y, X = g.Z, g.Y, g.X
    token[...] = jnp.zeros((ROWS, LANES), F32)
    gather_rows(g, yi, y_in, hy, ly)
    gather_strips(g, xi, x_in, hy, ly, xh, xl)
    fill_relay(g, hy, ly, xh, xl, relay, zi)
    for q, out in enumerate((yp, yk, ys)):
        for z in range(Z):
            out[z, :, :X] = row_halo(g, hy, ly, q, z)
            block, at = g.slot(q, z)
            hi = roll(xh[block, Y:], -at, 1)
            lo = roll(xl[block, Y:], -at - DEPTH, 1)
            out[z, :, X:] = strip_tile(hi, lo)

    def edge_rows(z):
        first = jnp.concatenate([k[z, :ROWS], xk[z, :ROWS]], axis=1)
        last = jnp.concatenate([k[z, Y - ROWS :], xk[z, Y - ROWS :]], axis=1)
        return last, yk[z], first

    for z in range(Z):
        last, beyond, first = edge_rows(z)
        tiles = jnp.concatenate([last, beyond, first], axis=0)
        wy = face(tiles, roll(tiles, 1, 0))
        fy_e[z, :ROWS] = wy[2 * ROWS :]
        fy_e[z, ROWS:] = wy[ROWS : 2 * ROWS]
        wx = face(beyond, roll(beyond, 1, 1))
        fx_y[z] = wx
        if z > 0:
            fz_y[z] = face(beyond, yk[z - 1])
    for z in range(1, Z - 1):
        last, beyond, first = edge_rows(z)
        tiles = jnp.concatenate([last, beyond, first], axis=0)
        wy = jnp.concatenate(
            [fy[z, Y - ROWS :], fy_e[z, ROWS:], fy_e[z, :ROWS], fy[z, ROWS : 2 * ROWS]], axis=0
        )
        wy = (wy + roll(wy, -1, 0))[: 3 * ROWS]
        wx = jnp.concatenate([fx[z, Y - ROWS :], fx_y[z], fx[z, :ROWS]], axis=0)
        wz = [
            jnp.concatenate([fz[i, Y - ROWS :], fz_y[i], fz[i, :ROWS]], axis=0) for i in (z, z + 1)
        ]
        scale = scale_of(tiles, wy + wx + roll(wx, -1, 1) + wz[0] + wz[1])
        dinv_e[z, :ROWS] = scale[2 * ROWS :]
        dinv_e[z, ROWS : 2 * ROWS] = scale[:ROWS]
        dinv_e[z, 2 * ROWS :] = scale[ROWS : 2 * ROWS]


def beyond(g, z):
    return z + DEPTH if z < DEPTH else z - g.Z + 3 * DEPTH


def either(top, high, low):
    return (high if top else low) if isinstance(top, bool) else jnp.where(top, high, low)


def halo_at(top, d):
    return either(top, 3 * DEPTH + d, DEPTH - 1 - d)


def face_at(top, d):
    return either(top, DEPTH + d, DEPTH - 1 - d)


def scale_at(top, d):
    return either(top, DEPTH + 1 + d, DEPTH - 2 - d)


def on_sides(g, zi, act):
    if g.zsides == 1:
        act(zi == 0)
    else:
        pl.when(zi < g.nz - 1)(functools.partial(act, True))
        pl.when(zi > 0)(functools.partial(act, False))


def on_ends(g, zi, act):
    if g.zsides == 1:
        act(zi != 0)
    else:
        pl.when(zi == g.nz - 1)(functools.partial(act, True))
        pl.when(zi == 0)(functools.partial(act, False))


def own_weights(refs):
    fz, fz_y, fx, fx_y, fy, fy_e = refs
    return Rows(fz, fz_y, 0, 0), Rows(fx, fx_y, 0, 0), Rows(fy, fy_e, 1, 0)


def halo_kernel(g, *refs):
    own_k = Fields(*refs[:3])
    fz, fx, fy = own_weights(refs[3:9])
    n = 9
    near = refs[n : n + g.zsides]
    n += g.zsides
    deep = refs[n : n + g.zsides]
    n += g.zsides
    relay = refs[n : n + g.zsides]
    n += g.zsides
    n += 1
    ph, sh, hz, hy, hx, hd, token = refs[n : n + 7]
    kh = refs[n + 7]
    token[...] = jnp.zeros((ROWS, LANES), F32)
    zi, yi, xi = g.where()
    Z, Y, X = g.Z, g.Y, g.X
    parts = X // LANES
    rest = DEPTH - 1
    zero = jnp.zeros((g.YE, g.XE), F32)

    def own_faces(z):
        wy, wx = fy[z], fx[z]
        return wy + roll(wy, -1, 0) + wx + roll(wx, -1, 1)

    def fill(top):
        def received(bufs, at):
            if len(bufs) == 1:
                return bufs[0][at]
            return jnp.where((zi % 2 == 0) == top, bufs[0][at], bufs[1][at])

        count = relay_tiles() * parts
        skip = relay[0].shape[0] - relay_blocks(g)
        bufs = [relay[0].at[skip:]] + list(relay[1:])
        tiles = [received(bufs, i) for i in range(relay_blocks(g))]
        strip = jnp.concatenate(tiles[count:], axis=0)
        packed = jnp.concatenate(
            [
                jnp.concatenate(tiles[i : i + parts], axis=1)
                for i in range(0, count, parts)
            ],
            axis=0,
        )
        start = 0
        for q, out in enumerate((ph, kh, sh)):
            for d in range(DEPTH if q < 2 else rest):
                at = halo_at(top, d)
                layer = either(top, d, rest - d)
                if q == 2:
                    plane = received(deep, 2 * rest + either(top, d, rest - 1 - d))
                elif d == 0:
                    plane = received(near, q)
                else:
                    plane = received(deep, q * rest + either(top, d - 1, rest - d))
                out[at, :Y, :X] = plane
                used = relay_rows(q, d)
                if used:
                    rows = [packed[start : start + used], packed[start + used : start + 2 * used]]
                    if 2 * used < ROWS:
                        rows.insert(1, jnp.zeros((ROWS - 2 * used, X), F32))
                    out[at, Y:, :X] = jnp.concatenate(rows, axis=0)
                    start += 2 * used
                else:
                    out[at, Y:, :X] = jnp.zeros((ROWS, X), F32)
                hi = turn(strip, -(q * DEPTH + layer) * DEPTH)
                lo = turn(strip, -((3 + q) * DEPTH + layer) * DEPTH - DEPTH)
                out[at, :, X:] = strip_tile(hi, lo)
        z = either(top, Z - 1, 0)
        kz = own_k[z]
        beyond_k = kh[halo_at(top, 0)]
        outer = face(beyond_k, kz)
        hz[face_at(top, 0)] = outer
        inner = fz[either(top, Z - 1, 1)]
        hd[scale_at(top, -1)] = scale_of(kz, own_faces(z) + inner + outer)
        for d in range(DEPTH - 1):
            inner = outer
            kz = beyond_k
            beyond_k = kh[halo_at(top, d + 1)]
            outer = face(beyond_k, kz)
            hz[face_at(top, d + 1)] = outer
            wy, wx, total = side_faces(kz)
            hy[halo_at(top, d)] = wy
            hx[halo_at(top, d)] = wx
            hd[scale_at(top, d)] = scale_of(kz, total + inner + outer)

    def end(top):
        z = either(top, Z - 1, 0)
        kz = own_k[z]
        ph[halo_at(top, 0)] = zero
        hz[face_at(top, 0)] = kz
        hd[scale_at(top, -1)] = scale_of(kz, own_faces(z) + fz[either(top, Z - 1, 1)] + kz)

    on_sides(g, zi, fill)
    on_ends(g, zi, end)


def turn(values, shift):
    if isinstance(shift, int):
        return roll(values, shift, 1)
    return pltpu.roll(values, lax.rem(shift + 8 * LANES, LANES), 1)


def sweep_kernel(g, sweep, inside, *refs):
    refs = list(refs)
    Z = g.Z
    final = sweep == SWEEPS
    own_s = Fields(*refs[:3])
    fz, fx, fy = own_weights(refs[3:9])
    dinv = Rows(refs[9], refs[10], 1, 1)
    n = 11
    if sweep == 1:
        v = Fields(*refs[n : n + 3])
        n += 3
    else:
        v = refs[n]
        n += 1
    if not inside:
        vh, sh, hz, hy, hx, hd = refs[n : n + 6]
        n += 6
    out = refs[-2]
    refs[-1][...] = jnp.zeros((ROWS, LANES), F32)
    zi, yi, xi = g.where()
    reach = SWEEPS - sweep

    def update(vz, low, high, source, z_low, z_high, wy, wx, scale):
        total = source + z_low * low + z_high * high
        total = total + wy * roll(vz, 1, 0) + roll(wy * vz, -1, 0)
        total = total + wx * roll(vz, 1, 1) + roll(wx * vz, -1, 1)
        return (1.0 - OMEGA) * vz + scale * total

    if inside:

        for z in range(sweep, Z - sweep):
            new = update(
                v[z], v[z - 1], v[z + 1], own_s[z], fz[z], fz[z + 1], fy[z], fx[z], dinv[z]
            )
            if final:
                out[z] = new[: g.Y, : g.X]
            else:
                out[z] = new
        return

    def v_at(z):
        return v[z] if sweep - 1 <= z <= Z - sweep else vh[beyond(g, z)]

    def z_face(z):
        return fz[z] if 1 <= z < Z else hz[face_at(z >= Z, 0)]

    def own_edge(z):
        new = update(
            v_at(z),
            v_at(z - 1),
            v_at(z + 1),
            own_s[z],
            z_face(z),
            z_face(z + 1),
            fy[z],
            fx[z],
            dinv[z] if 0 < z < Z - 1 else hd[scale_at(z > 0, -1)],
        )
        if final:
            out[beyond(g, z) - DEPTH] = new[: g.Y, : g.X]
        else:
            out[beyond(g, z)] = new

    def halo(top):
        inner = v[either(top, Z - 1, 0)] if sweep == 1 else vh[halo_at(top, -1)]
        vz = vh[halo_at(top, 0)]
        for d in range(reach):
            at = halo_at(top, d)
            outer = vh[halo_at(top, d + 1)]
            z_inner, z_outer = hz[face_at(top, d)], hz[face_at(top, d + 1)]
            out[at] = update(
                vz, inner, outer, sh[at], z_inner, z_outer, hy[at], hx[at], hd[scale_at(top, d)]
            )
            inner, vz = vz, outer

    def clear(top):
        out[halo_at(top, 0)] = jnp.zeros((g.YE, g.XE), F32)

    for z in range(sweep):
        own_edge(z)
        own_edge(Z - 1 - z)
    if final:
        return
    on_sides(g, zi, halo)
    on_ends(g, zi, clear)


def extend_sweep_kernel(g, count, *refs):
    p, s, xp, xs, dinv = refs[:5]
    inputs = refs[5 : 5 + count]
    n = 5 + count
    outs = refs[n : n + 8 + g.zsides]
    n += 8 + g.zsides
    v = refs[n]
    scratch = refs[n + 1 :]
    xk, fz, fy, fx = inputs[1:5]
    yp, yk, ys, fz_y, fx_y, fy_e, dinv_e, token = outs[:8]
    extend_kernel(g, *inputs, *outs, *scratch)
    common = (s, xs, ys, fz, fz_y, fx, fx_y, fy, fy_e, dinv, dinv_e)
    sweep_kernel(g, 1, True, *common, p, xp, yp, v, token)


def inner_sweeps_kernel(g, *refs):
    common, v = refs[:11], refs[11]
    between, out, token = refs[-3:]
    sweep_kernel(g, 3, True, *common, v, between, token)
    sweep_kernel(g, 4, True, *common, between, out, token)


def halo_sweeps_kernel(g, count, *refs):
    common, start, v = refs[:11], refs[11:14], refs[14]
    inputs = refs[15 : 15 + count]
    sh, hz, hy, hx, hd, out, token = refs[15 + count : 22 + count]
    kh, ph, vh = refs[22 + count :]
    beyond_own = (sh, hz, hy, hx, hd)
    halo_kernel(g, *inputs, ph, *beyond_own, token, kh)
    sweep_kernel(g, 1, False, *common, *start, ph, *beyond_own, vh, token)
    sweep_kernel(g, 2, False, *common, v, vh, *beyond_own, out, token)


def last_sweeps_kernel(g, *refs):
    common, v = refs[:11], refs[11:13]
    vh, beyond_own = refs[13], refs[14:19]
    out, token, between = refs[19:]
    sweep_kernel(g, 3, False, *common, v[0], vh, *beyond_own, between, token)
    sweep_kernel(g, 4, False, *common, v[1], between, *beyond_own, out, token)


def solve_kernel(g, gathered, fine, edges, out, buffer, sems):
    zi, yi, xi = g.where()
    per = LANES // g.cx
    group = lane_of((ROWS, LANES)) // g.cx

    order = sum(g.steps(), [])

    def place(a, b, c):
        index = {"gx": a, "gy": b, "gz": c}
        at = 0
        for number, (axis, bit) in enumerate(order):
            at = at + (1 << number) * ((index[axis] & bit) // bit)
        return at

    here = place(zi, yi, xi)

    def relative(a, b, c):
        return jnp.bitwise_xor(here, place(a, b, c))

    last = coarse_blocks(g) - 1

    def block_of(at, block):
        return gathered[at >> 1, 2 * last if block == last else (at & 1) * last + block]

    layers = g.nz * g.cz
    height = g.ny * g.cy
    fields = []
    for q in range(5):
        planes = []
        for layer in range(layers):
            a, cz = divmod(layer, g.cz)
            m = q * g.cz + cz
            tiles = []
            for b in range(g.ny):
                value = block_of(relative(a, b, 0), m // per)
                for c in range(1, g.nx):
                    value = jnp.where(
                        group == (m % per + c) % per, block_of(relative(a, b, c), m // per), value
                    )
                tiles.append(roll(value, -(m % per) * g.cx, 1))
            planes.append(jnp.concatenate(tiles, axis=0))
        fields.append(planes)
    rhs, diagonal, wz, wy, wx = fields
    shape = (height, LANES)
    zero = jnp.zeros(shape, F32)
    wz = [zero] + wz[1:]
    wy = [jnp.where(row_of(shape) == 0, 0.0, w) for w in wy]
    wx = [jnp.where(lane_of(shape) == 0, 0.0, w) for w in wx]
    scale = [OMEGA_COARSE / d for d in diagonal]

    def flux(e):
        result = []
        for i in range(layers):
            total = wy[i] * roll(e[i], 1, 0) + roll(wy[i] * e[i], -1, 0)
            total = total + wx[i] * roll(e[i], 1, 1) + roll(wx[i] * e[i], -1, 1)
            if i > 0:
                total = total + wz[i] * e[i - 1]
            if i < layers - 1:
                total = total + wz[i + 1] * e[i + 1]
            result.append(total)
        return result

    start = [sc * r for sc, r in zip(scale, rhs)]
    below_y = [sc * w for sc, w in zip(scale, wy)]
    above_y = [sc * roll(w, -1, 0) for sc, w in zip(scale, wy)]
    below_x = [sc * w for sc, w in zip(scale, wx)]
    above_x = [sc * roll(w, -1, 1) for sc, w in zip(scale, wx)]
    below_z = [sc * w for sc, w in zip(scale, wz)]
    above_z = [sc * w for sc, w in zip(scale, wz[1:])]
    e = start
    for _ in range(COARSE_SWEEPS - 1):
        new = []
        for i in range(layers):
            total = start[i] + (1.0 - OMEGA_COARSE) * e[i]
            if i > 0:
                total = total + below_z[i] * e[i - 1]
            if i < layers - 1:
                total = total + above_z[i] * e[i + 1]
            total = total + below_y[i] * roll(e[i], 1, 0) + above_y[i] * roll(e[i], -1, 0)
            total = total + below_x[i] * roll(e[i], 1, 1) + above_x[i] * roll(e[i], -1, 1)
            new.append(total)
        e = new
    f = flux(e)
    left = zero
    total = zero
    for i in range(layers):
        left = left + (rhs[i] - diagonal[i] * e[i] + f[i])
        total = total + diagonal[i]
    shift = jnp.sum(left) / jnp.sum(total)

    own = []
    for cz in range(g.cz):
        mine = jnp.zeros((ROWS, LANES), F32)
        for a in range(g.nz):
            for b in range(g.ny):
                here = (zi == a) & (yi == b)
                mine = jnp.where(here, e[a * g.cz + cz][b * ROWS : (b + 1) * ROWS], mine)
        own.append(mine)
    onehot = (
        lax.broadcasted_iota(jnp.int32, (LANES, g.X), 0)
        == xi * g.cx + lax.broadcasted_iota(jnp.int32, (LANES, g.X), 1) // RATIO
    ).astype(jnp.bfloat16)
    wide = exact_dot(jnp.concatenate(own, axis=0), onehot) + shift
    copies = []
    for cz in range(g.cz):
        block = wide[cz * ROWS : (cz + 1) * ROWS]
        spread = jnp.broadcast_to(block[:, None, :], (g.cy, RATIO, g.X)).reshape(g.Y, g.X)
        for z in range(cz * RATIO, (cz + 1) * RATIO):
            if DEPTH <= z < g.Z - DEPTH:
                buffer[z] = fine[z] + spread
            else:
                buffer[z] = edges[beyond(g, z) - DEPTH] + spread
            if z % DEPTH == DEPTH - 1:
                part = pl.ds(z + 1 - DEPTH, DEPTH)
                copy = pltpu.make_async_copy(buffer.at[part], out.at[part], sems.at[z // DEPTH])
                copy.start()
                copies.append(copy)
    for copy in copies:
        copy.wait()


def copy_kernel(source, out):
    out[...] = source[...]


def merge_kernel(cells, got, token, out):
    count = cells.shape[0]
    out[:count] = cells[...]
    out[count:] = got[...]


def pair_kernel(g, cells, got, token, out):
    last = coarse_blocks(g) - 1
    for block in range(last):
        out[0, block] = cells[0, block]
        out[0, last + block] = got[0, block]
    out[0, 2 * last] = cells[0, last] + got[0, last]


def join_kernel(g, cells, got, relay, out):
    nc = pair_blocks(g)
    count = cells.shape[0]
    for at in range(count):
        out[at * nc : (at + 1) * nc] = cells[at]
        out[(count + at) * nc : (count + at + 1) * nc] = got[at]
    out[2 * count * nc :] = relay[...]


def split_kernel(g, joined, got, token, out):
    nc = pair_blocks(g)
    count = out.shape[0] // 2
    for at in range(count):
        out[at] = joined[at * nc : (at + 1) * nc]
        out[count + at] = got[at * nc : (at + 1) * nc]


def merge(cells, got, token):
    shape = (2 * cells.shape[0],) + cells.shape[1:]
    (out,) = run(merge_kernel, [shape], [cells, got, token], us=0.05, name="merge")
    return out


def exchange(bufs, axis, count, beside=None):
    got = [lax.ppermute(bufs[0], axis, pairs(count, 0))]
    if len(bufs) > 1:
        if beside is None:
            got.append(lax.ppermute(bufs[1], axis, pairs(count, 1)))
        else:
            perm = spread_pairs(count, lax.axis_size(beside))
            got.append(lax.ppermute(bufs[1], (axis, beside), perm))
    return got


def shards(pressure_start, source, permeability):
    g = Grid(pressure_start.shape)
    Z, Y, X = g.Z, g.Y, g.X
    tile = (ROWS, LANES)
    x_shape = (g.blocks, Y, LANES)
    y_shape = (3 * Z // 2 + 1, ROWS, X)
    sums_shape = (5, g.cz, ROWS, X)
    main = (Z, Y, g.XE)
    nc, nr = pair_blocks(g), relay_blocks(g)

    sent = run(
        functools.partial(pack_kernel, g),
        [(Z, Y, X)] * 3
        + [(2, Y, X)] * g.zsides
        + [x_shape] * g.xsides
        + [(2, Z, X)] * g.ysides,
        [pressure_start, permeability, source],
        scratch=[pltpu.SemaphoreType.DMA((3 + 2 * g.zsides,))],
        name="pack_faces",
        far=True,
    )
    sent = list(sent)
    (p, k, s), near, sent = sent[:3], sent[3 : 3 + g.zsides], sent[3 + g.zsides :]
    x_sent, row_sent = sent[: g.xsides], sent[g.xsides :]
    near_got = exchange(near, "gx", g.nz, "gz")
    x_got = exchange(x_sent, "gz", g.nx)
    row_got = exchange(row_sent, "gy", g.ny, "gz")
    sums, token_l = run(
        functools.partial(local_kernel, g),
        [sums_shape, tile],
        [p, k, s],
        us=US["local"],
        name="local_sums",
    )
    cells, token = run(
        functools.partial(restrict_kernel, g),
        [(1, coarse_blocks(g)) + tile, tile],
        [p, k, sums] + near_got + row_got + row_sent + x_got + x_sent,
        us=US["restrict"],
        name="restrict",
    )
    y_sent = run(
        functools.partial(pack_rows_kernel, g),
        [y_shape] * g.ysides,
        [p, k, s] + x_got + near_got + [token],
        us=US["rows"],
        name="pack_rows",
    )
    y_got = exchange(y_sent, "gy", g.ny, "gz")
    y_got = list(y_got)
    y_got[:1] = run(copy_kernel, [y_shape], y_got[:1], us=0.05, name="first_rows")
    xp, xk, xs, fz, fy, fx, dinv, token_w = run(
        functools.partial(side_weights_kernel, g),
        [(Z, Y, LANES)] * 3 + [main] * 4 + [tile],
        [k] + x_got + [y_sent[0]],
        scratch=[pltpu.VMEM(x_shape, F32)] * 2,
        us=US["side"] + US["weights"],
        name="weights",
    )
    deep = run(
        functools.partial(deep_kernel, g),
        [(3 * (DEPTH - 1), Y, X)] * g.zsides,
        [p, k, s, token_l] + near_got + row_got + x_got,
        us=0.1,
        name="pack_deep",
    )
    deep_got = exchange(deep, "gx", g.nz, "gz")
    rows = (Z, ROWS, g.XE)
    halo_scratch = [pltpu.VMEM(y_shape, F32)] * 2 + [pltpu.VMEM((g.blocks, g.YE, LANES), F32)] * 2
    inputs = [k, xk, fz, fy, fx] + list(y_got) + x_got + [token_w]
    own = (Z, g.YE, g.XE)
    extended = run(
        functools.partial(extend_sweep_kernel, g, len(inputs)),
        [rows] * 5
        + [(Z, 2 * ROWS, g.XE), (Z, 3 * ROWS, g.XE), tile]
        + [(nr,) + tile] * g.zsides
        + [own],
        [p, s, xp, xs, dinv] + inputs,
        scratch=halo_scratch,
        us=US["extend"] + US["sweep"],
        name="extend",
    )
    yp, yk, ys, fz_y, fx_y, fy_e, dinv_e, token_e = extended[:8]
    before, _, after = g.steps()
    for number, (axis, bit) in enumerate(before):
        got = lax.ppermute(cells, axis, flips(lax.axis_size(axis), bit))
        if number == 0:
            (cells,) = run(
                functools.partial(pair_kernel, g),
                [(1, nc) + tile],
                [cells, got, token_w],
                us=0.05,
                name="pair",
            )
    count = 2 * cells.shape[0]
    (joined,) = run(
        functools.partial(join_kernel, g),
        [(count * nc + nr,) + tile],
        [cells, got, extended[8]],
        us=0.05,
        name="join",
    )
    relay = exchange([joined] + list(extended[9:-1]), "gx", g.nz, "gz")
    weights = [fz, fz_y, fx, fx_y, fy, fy_e]
    common = [s, xs, ys] + weights + [dinv, dinv_e]
    far = (4 * DEPTH, g.YE, g.XE)
    far8 = (2 * DEPTH, g.YE, g.XE)
    inner, tokens = [[p, xp, yp], [extended[-1]]], {"W": token_w, "I1": token_e}
    v, tokens["I2"] = run(
        functools.partial(sweep_kernel, g, 2, True),
        [own, tile],
        common + inner[1],
        us=US["sweep"],
        name="inner_2",
    )
    inner.append([v])
    between, v, tokens["I4"] = run(
        functools.partial(inner_sweeps_kernel, g),
        [own, (Z, Y, X), tile],
        common + inner[2],
        us=US["sweep"],
        name="inner_3_4",
    )
    inner += [[between], [v]]
    inputs = [k, xk, yk] + weights + near_got + deep_got + relay + [tokens["I2"]]
    sh, hz, hy, hx, hd, vh, tokens["O2"] = run(
        functools.partial(halo_sweeps_kernel, g, len(inputs)),
        [far, far8, far, far, far8, far, tile],
        common + inner[0] + inner[1] + inputs,
        scratch=[pltpu.VMEM(far, F32)] * 3,
        us=US["halo"] + 2 * US["outer"],
        name="halo_sweeps",
    )
    vh, tokens["O3"] = run(
        functools.partial(last_sweeps_kernel, g),
        [(2 * DEPTH, Y, X), tile],
        common + inner[2] + inner[3] + [vh, sh, hz, hy, hx, hd],
        scratch=[pltpu.VMEM(far, F32)],
        us=2 * US["outer"],
        name="last_sweeps",
    )
    (cells,) = run(
        functools.partial(split_kernel, g),
        [(2 * count, nc) + tile],
        [joined, relay[0], tokens[PLAN[0]]],
        us=0.05,
        name="split",
    )
    for number, (axis, bit) in enumerate(after):
        got = lax.ppermute(cells, axis, flips(lax.axis_size(axis), bit))
        name = PLAN[max(1, number - len(after) + len(PLAN))]
        cells = merge(cells, got, tokens[name])
    (out,) = run(
        functools.partial(solve_kernel, g),
        [(Z, Y, X)],
        [cells, v, vh],
        us=US["solve"],
        scratch=[pltpu.VMEM((Z, Y, X), F32), pltpu.SemaphoreType.DMA((Z // DEPTH,))],
        name="solve",
        far_out=True,
        spaces=[jax.ShapeDtypeStruct((Z, Y, X), F32)],
    )
    return out


def solution(mesh):
    return jax.shard_map(
        shards,
        mesh=mesh,
        in_specs=(P("gx", "gy", "gz"), P("gx", "gy", "gz"), P("gx", "gy", "gz")),
        out_specs=P("gx", "gy", "gz"),
        check_vma=False,
    )
```

```python
import functools

import jax
import jax.numpy as jnp
from jax import lax
from jax.experimental import pallas as pl
from jax.experimental.pallas import tpu as pltpu
from jax.sharding import PartitionSpec as P

RATIO = 8
SWEEPS = 4
COARSE_SWEEPS = 8
OMEGA = 0.8
OMEGA_COARSE = 0.8

LANES = 128
ROWS = 8
DEPTH = SWEEPS
SLOTS = LANES // DEPTH
F32 = jnp.float32
VMEM_LIMIT = 14 * 1024 * 1024
PLAN = ["I4", "O2", "O3"]
US = dict(local=1.2, rows=0.1, side=0.8, weights=3.2, restrict=0.6, extend=1.0, halo=1.4, outer=0.8, sweep=2.2, solve=2.2)


def pairs(count, odd):
    start = 1 if odd else 0
    out = []
    for low in range(start, count + start - 1, 2):
        high = (low + 1) % count
        out += [(low, high), (high, low)]
    return out


def spread_pairs(outer, inner):
    out = []
    for i in range(outer):
        for j in range(inner):
            if i in (0, outer - 1):
                target = i * inner + (j ^ 1)
            else:
                target = (i + 1 if i % 2 else i - 1) * inner + j
            out.append((i * inner + j, target))
    return out


def flips(count, bit):
    return [(i, i ^ bit) for i in range(count)]


def on_chip(value):
    return pltpu.with_memory_space_constraint(value, pltpu.VMEM)


def run(kernel, outs, args, scratch=(), us=1.0, name=None, spaces=None, far=False, far_out=False, aliases=None):
    whole = pl.BlockSpec(memory_space=pltpu.VMEM)
    shapes = [pltpu.VMEM(shape, F32) for shape in outs] if spaces is None else spaces
    return pl.pallas_call(
        kernel,
        out_shape=shapes,
        in_specs=[pl.BlockSpec(memory_space=pltpu.HBM) if far else whole] * len(args),
        out_specs=[pl.BlockSpec(memory_space=pltpu.HBM) if far_out else whole] * len(outs),
        scratch_shapes=list(scratch),
        input_output_aliases=aliases or {},
        compiler_params=pltpu.CompilerParams(vmem_limit_bytes=VMEM_LIMIT),
        cost_estimate=pl.CostEstimate(
            flops=1000, bytes_accessed=int(us * 3_500_000), transcendentals=0
        ),
        name=name,
    )(*[pltpu.with_memory_space_constraint(a, pltpu.HBM) if far else on_chip(a) for a in args])


def lane_of(shape):
    return lax.broadcasted_iota(jnp.int32, shape, len(shape) - 1)


def row_of(shape):
    return lax.broadcasted_iota(jnp.int32, shape, len(shape) - 2)


def roll(values, shift, axis):
    size = values.shape[axis]
    if isinstance(shift, int):
        shift = shift % size
        if shift == 0:
            return values
    return pltpu.roll(values, shift, axis)


def face(one, other):
    half = jnp.where(jnp.minimum(one, other) > 0.0, 0.5, 1.0)
    return half * (one + other)


def group_rows(values):
    rows, width = values.shape
    return values.reshape(rows // RATIO, RATIO, width).sum(axis=1)


def split3(values):
    a = values.astype(jnp.bfloat16)
    rest = values - a.astype(F32)
    b = rest.astype(jnp.bfloat16)
    c = (rest - b.astype(F32)).astype(jnp.bfloat16)
    return jnp.concatenate([a, b, c], axis=0)


def exact_dot(values, onehot):
    rows = values.shape[0]
    out = jnp.dot(split3(values), onehot, preferred_element_type=F32)
    return out[:rows] + out[rows : 2 * rows] + out[2 * rows :]


class Grid:
    def __init__(self, shape):
        self.Z, self.Y, self.X = shape
        self.nz, self.ny, self.nx = (lax.axis_size("gx"), lax.axis_size("gy"), lax.axis_size("gz"))
        self.cz, self.cy, self.cx = (n // RATIO for n in shape)
        self.blocks = -(-3 * self.Z // SLOTS)
        self.XE = self.X + LANES
        self.YE = self.Y + ROWS
        self.ZE = self.Z + 2 * DEPTH
        self.zsides = 1 if self.nz == 2 else 2
        self.ysides = 1 if self.ny == 2 else 2
        self.xsides = 1 if self.nx == 2 else 2
        assert 2 * DEPTH == ROWS and 2 * self.Z <= SLOTS and self.Z % 2 == 0
        assert self.blocks * LANES <= self.X and self.cy == ROWS
        assert self.cx * self.nx == LANES
        assert 2 * (5 * self.cz % self.nx) == self.nx and self.nx == 4 and self.ny > 2

    def where(self):
        return lax.axis_index("gx"), lax.axis_index("gy"), lax.axis_index("gz")

    def steps(self):
        before = [("gz", 1 << i) for i in reversed(range(1, self.nx.bit_length() - 1))]
        before += [("gy", 1 << i) for i in reversed(range(1, self.ny.bit_length() - 1))]
        after = [("gx", 1 << i) for i in reversed(range(1, self.nz.bit_length() - 1))]
        return before, [("gx", 1)], after + [("gy", 1), ("gz", 1)]

    def slot(self, q, z):
        index = q * self.Z + z
        return index // SLOTS, (index % SLOTS) * DEPTH


def pack_kernel(g, *refs):
    src = refs[:3]
    fields = refs[3:6]
    n = 6
    near = refs[n : n + g.zsides]
    n += g.zsides
    x_out = refs[n : n + g.xsides]
    n += g.xsides
    y_out = refs[n : n + g.ysides]
    sems = refs[n + g.ysides]
    zi, yi, xi = g.where()
    loads = [pltpu.make_async_copy(src[q], fields[q], sems.at[q]) for q in range(3)]
    for copy in loads:
        copy.start()
    lane = lane_of((g.Y, LANES))
    packs = [[jnp.zeros((g.Y, LANES), F32) for _ in range(g.blocks)] for _ in range(2)]
    for q in range(3):
        loads[q].wait()
        if q < 2:
            for side, out in enumerate(near):
                out[q] = fields[q][jnp.where((zi % 2) == side, g.Z - 1, 0)]
        for z in range(g.Z):
            block, at = g.slot(q, z)
            pack = packs[(at // DEPTH) % 2]
            both = jnp.where(
                lane < LANES // 2, fields[q][z, :, :LANES], fields[q][z, :, g.X - LANES :]
            )
            keep = (lane + (LANES + DEPTH - at)) % LANES < 2 * DEPTH
            pack[block] = jnp.where(keep, roll(both, at, 1), pack[block])
        if q < 2:
            for at in range(0, g.Z, ROWS):
                layers = range(at, at + ROWS)
                hi = jnp.concatenate([fields[q][z, g.Y - 1 :, :] for z in layers], axis=0)
                lo = jnp.concatenate([fields[q][z, :1, :] for z in layers], axis=0)
                for side, out in enumerate(y_out):
                    out[q, at : at + ROWS] = jnp.where((yi % 2) == side, hi, lo)
    even = (xi % 2) == 0
    first_half = lane % (2 * DEPTH) < DEPTH
    for block in range(g.blocks):
        lo = jnp.where(first_half, packs[0][block], packs[1][block])
        hi = roll(jnp.where(first_half, packs[1][block], packs[0][block]), DEPTH, 1)
        for side, out in enumerate(x_out):
            out[block] = jnp.where(even == (side == 0), hi, lo)


def pick(first, second, even, inside):
    if second is None:
        return jnp.where(even & inside, first, 0.0)
    return jnp.where(inside, jnp.where(even, first, second), 0.0)


def from_high(index, count, bufs, view):
    even = (index % 2) == 0
    second = view(bufs[1]) if len(bufs) > 1 else None
    return pick(view(bufs[0]), second, even, index < count - 1)


def from_low(index, count, bufs, view):
    odd = (index % 2) == 1
    second = view(bufs[1]) if len(bufs) > 1 else None
    return pick(view(bufs[0]), second, odd, index > 0)


def pack_rows_kernel(g, *refs):
    src = refs[:3]
    x_in = refs[3 : 3 + g.xsides]
    y_out = refs[len(refs) - g.ysides :]
    zi, yi, xi = g.where()
    half = g.Z // 2
    last = g.Y - ROWS
    for side, out in enumerate(y_out):
        high = (yi % 2) == side

        def fill(top, out=out):
            for q in range(3):
                for pair in range(half):
                    a, b = src[q][2 * pair], src[q][2 * pair + 1]
                    if top:
                        part = jnp.concatenate([a[g.Y - DEPTH :], b[g.Y - DEPTH :]], axis=0)
                    else:
                        part = jnp.concatenate([a[:DEPTH], b[:DEPTH]], axis=0)
                    out[q * half + pair] = part
            rows = slice(g.Y - DEPTH, g.Y) if top else slice(0, DEPTH)
            for block in range(g.blocks):
                hi = from_high(xi, g.nx, x_in, lambda r: r[block, rows, :])
                lo = from_low(xi, g.nx, x_in, lambda r: r[block, rows, :])
                out[3 * half, :, block * LANES : (block + 1) * LANES] = jnp.concatenate(
                    [hi, lo], axis=0
                )

        pl.when(high)(functools.partial(fill, True))
        pl.when(jnp.logical_not(high))(functools.partial(fill, False))


def gather_rows(g, yi, y_in, hy, ly):
    hy[...] = from_high(yi, g.ny, y_in, lambda r: r[...])
    ly[...] = from_low(yi, g.ny, y_in, lambda r: r[...])


def gather_strips(g, xi, x_in, hy, ly, xh, xl):
    half = g.Z // 2
    for block in range(g.blocks):
        lanes = slice(block * LANES, (block + 1) * LANES)
        xh[block, : g.Y] = from_high(xi, g.nx, x_in, lambda r: r[block])
        xl[block, : g.Y] = from_low(xi, g.nx, x_in, lambda r: r[block])
        top, low = hy[3 * half, :, lanes], ly[3 * half, :, lanes]
        xh[block, g.Y :] = jnp.concatenate([top[:DEPTH], low[:DEPTH]], axis=0)
        xl[block, g.Y :] = jnp.concatenate([top[DEPTH:], low[DEPTH:]], axis=0)


def row_halo(g, hy, ly, q, z):
    half = g.Z // 2
    at = (z % 2) * DEPTH
    block = q * half + z // 2
    return jnp.concatenate([hy[block, at : at + DEPTH], ly[block, at : at + DEPTH]], axis=0)


def deep_kernel(g, p, k, s, *refs):
    deep = refs[len(refs) - g.zsides :]
    rest = DEPTH - 1
    zi = g.where()[0]
    for side in range(g.zsides):
        high = (zi % 2) == side
        for q, src in enumerate((p, k, s)):
            first = jnp.where(high, g.Z - rest if q == 2 else g.Z - DEPTH, 0 if q == 2 else 1)
            deep[side][q * rest : (q + 1) * rest] = src[pl.ds(first, rest)]


def local_kernel(g, p, k, s, out, token):
    token[...] = jnp.zeros((ROWS, LANES), F32)
    Z, Y, X = g.Z, g.Y, g.X
    zero = jnp.zeros((Y, X), F32)
    none = jnp.zeros((ROWS, X), F32)
    flux_z, weight_z = [none], [none]
    for layer in range(RATIO, Z, RATIO):
        w = 0.5 * (k[layer] + k[layer - 1])
        weight_z.append(group_rows(w))
        flux_z.append(group_rows(w * (p[layer] - p[layer - 1])))
    weight_z.append(none)
    flux_z.append(none)
    inner_x = (lane_of((ROWS, X)) % RATIO == 0) & (lane_of((ROWS, X)) > 0)
    first_y = row_of((Y, X)) % RATIO == 0
    row8 = row_of((ROWS, X))
    for cz in range(g.cz):
        acc_s = acc_wx = acc_fx = acc_wy = acc_fy = zero
        for z in range(cz * RATIO, (cz + 1) * RATIO):
            pz, kz = p[z], k[z]
            acc_s = acc_s + s[z]
            w = kz + roll(kz, 1, 1)
            acc_wx = acc_wx + w
            acc_fx = acc_fx + w * (pz - roll(pz, 1, 1))
            w = kz + roll(kz, 1, 0)
            acc_wy = acc_wy + w
            acc_fy = acc_fy + w * (pz - roll(pz, 1, 0))
        weight_x = jnp.where(inner_x, 0.5 * group_rows(acc_wx), 0.0)
        flux_x = jnp.where(inner_x, 0.5 * group_rows(acc_fx), 0.0)
        weight_y, flux_y = (
            jnp.where(row8 > 0, 0.5 * group_rows(jnp.where(first_y, acc, 0.0)), 0.0)
            for acc in (acc_wy, acc_fy)
        )
        out[0, cz] = (
            group_rows(acc_s)
            - (flux_z[cz] - flux_z[cz + 1])
            - (flux_y - roll(flux_y, -1, 0))
            - (flux_x - roll(flux_x, -1, 1))
        )
        out[1, cz] = (
            weight_z[cz]
            + weight_z[cz + 1]
            + weight_y
            + roll(weight_y, -1, 0)
            + weight_x
            + roll(weight_x, -1, 1)
        )
        out[2, cz] = weight_z[cz]
        out[3, cz] = weight_y
        out[4, cz] = weight_x


def side_kernel(g, *refs):
    x_in = refs[: g.xsides]
    xp, xk, xs, token, xh, xl = refs[g.xsides + 1 :]
    xi = g.where()[2]
    Z = g.Z
    token[...] = jnp.zeros((ROWS, LANES), F32)
    for block in range(g.blocks):
        xh[block] = from_high(xi, g.nx, x_in, lambda r: r[block])
        xl[block] = from_low(xi, g.nx, x_in, lambda r: r[block])

    for q, dst in enumerate((xp, xk, xs)):
        for z in range(Z):
            block, at = g.slot(q, z)
            hi = roll(xh[block], -at, 1)
            lo = roll(xl[block], -at - DEPTH, 1)
            dst[z] = strip_tile(hi, lo)


def weights_kernel(g, k, xk, after, fz, fy, fx, dinv, token):
    token[...] = jnp.zeros((ROWS, LANES), F32)
    Z = g.Z

    def k_at(z):
        return jnp.concatenate([k[z], xk[z]], axis=1)

    fy[0], fx[0], _ = side_faces(k_at(0))
    below = face(k_at(1), k_at(0))
    fz[1] = below
    for z in range(1, Z - 1):
        kz = k_at(z)
        above = face(k_at(z + 1), kz)
        fz[z + 1] = above
        wy, wx, total = side_faces(kz)
        fy[z] = wy
        fx[z] = wx
        dinv[z] = scale_of(kz, total + below + above)
        below = above
    fy[Z - 1], fx[Z - 1], _ = side_faces(k_at(Z - 1))


def own_sides(bufs, even, view):
    if len(bufs) == 1:
        return view(bufs[0]), view(bufs[0])
    first, second = view(bufs[0]), view(bufs[1])
    return jnp.where(even, first, second), jnp.where(even, second, first)


def side_weights_kernel(g, *refs):
    k, x_in = refs[0], refs[1 : 1 + g.xsides + 1]
    xp, xk, xs, fz, fy, fx, dinv, token, xh, xl = refs[2 + g.xsides :]
    side_kernel(g, *x_in, xp, xk, xs, token, xh, xl)
    weights_kernel(g, k, xk, token, fz, fy, fx, dinv, token)


def restrict_kernel(g, *refs):
    p, k, sums = refs[:3]
    n = 3
    near = refs[n : n + g.zsides]
    n += g.zsides
    y_in = refs[n : n + g.ysides]
    n += g.ysides
    y_own = refs[n : n + g.ysides]
    n += g.ysides
    x_in = refs[n : n + g.xsides]
    n += g.xsides
    x_own = refs[n : n + g.xsides]
    n += g.xsides
    out, token = refs[n:]
    token[...] = jnp.zeros((ROWS, LANES), F32)
    zi, yi, xi = g.where()
    Z, Y, X = g.Z, g.Y, g.X

    p0, k0 = (from_low(zi, g.nz, near, lambda r, q=q: r[q]) for q in range(2))
    w = face(k0, k[0])
    low_wz, low_fz = group_rows(w), group_rows(w * (p[0] - p0))
    p1, k1 = (from_high(zi, g.nz, near, lambda r, q=q: r[q]) for q in range(2))
    w = face(k[Z - 1], k1)
    top_wz, top_fz = group_rows(w), group_rows(w * (p1 - p[Z - 1]))

    (p_hi, p_lo), (k_hi, k_lo) = (
        own_sides(y_own, (yi % 2) == 0, lambda r, q=q: r[q]) for q in range(2)
    )
    p0, k0 = (from_low(yi, g.ny, y_in, lambda r, q=q: r[q]) for q in range(2))
    low_wy = face(k0, k_lo)
    low_fy = low_wy * (p_lo - p0)
    p1, k1 = (from_high(yi, g.ny, y_in, lambda r, q=q: r[q]) for q in range(2))
    top_wy = face(k_hi, k1)
    top_fy = top_wy * (p1 - p_hi)

    lane = lane_of((Y, LANES))
    own_hi, own_lo = own_sides(x_own, (xi % 2) == 0, lambda r: r[0])
    next_hi = from_high(xi, g.nx, x_in, lambda r: r[0])
    next_lo = from_low(xi, g.nx, x_in, lambda r: r[0])

    def side_sums(own, other, lane_in, flip):
        wk = face(roll(own, -Z * DEPTH, 1), roll(other, -Z * DEPTH, 1))
        diff = (other - own) if flip else (own - other)
        keep = (lane % DEPTH == lane_in) & (lane < Z * DEPTH)
        w = jnp.where(keep, wk, 0.0)
        result = []
        for value in (w, w * diff):
            total = group_rows(value)
            step = DEPTH
            while step < RATIO * DEPTH:
                total = total + roll(total, -step, 1)
                step *= 2
            result.append(total)
        return result

    low_wx, low_fx = side_sums(own_lo, roll(next_lo, -(DEPTH - 1), 1), 0, False)
    top_wx, top_fx = side_sums(own_hi, roll(next_hi, DEPTH - 1, 1), DEPTH - 1, True)
    lane8 = lane_of((ROWS, X))
    row8 = row_of((ROWS, X))

    def widen(value, at, cell):
        moved = roll(value, (at % LANES) - cell, 1)
        wide = jnp.concatenate([moved] * (X // LANES), axis=1)
        return jnp.where(lane8 == at, wide, 0.0)

    def at_row(row, values, cz):
        total = values[cz * RATIO : (cz + 1) * RATIO].sum(axis=0, keepdims=True)
        return jnp.where(row8 == row, jnp.broadcast_to(total, (ROWS, X)), 0.0)

    items = []
    for cz in range(g.cz):
        cell = cz * RATIO * DEPTH
        x_low = widen(low_wx, 0, cell)
        y_low = at_row(0, low_wy, cz)
        rhs = sums[0, cz] - at_row(0, low_fy, cz) + at_row(g.cy - 1, top_fy, cz)
        rhs = rhs - widen(low_fx, 0, cell) + widen(top_fx, X - 1, cell + DEPTH - 1)
        diagonal = sums[1, cz] + y_low + at_row(g.cy - 1, top_wy, cz)
        diagonal = diagonal + x_low + widen(top_wx, X - 1, cell + DEPTH - 1)
        wz = sums[2, cz]
        if cz == 0:
            rhs = rhs - low_fz
            diagonal = diagonal + low_wz
            wz = wz + low_wz
        if cz == g.cz - 1:
            rhs = rhs + top_fz
            diagonal = diagonal + top_wz
        items.append([rhs, diagonal, wz, sums[3, cz] + y_low, sums[4, cz] + x_low])
    items = [items[cz][q] for q in range(5) for cz in range(g.cz)]
    onehot = (
        lax.broadcasted_iota(jnp.int32, (X, LANES), 0) // RATIO
        == lax.broadcasted_iota(jnp.int32, (X, LANES), 1)
    ).astype(jnp.bfloat16)
    summed = exact_dot(jnp.concatenate(items, axis=0), onehot)
    per = LANES // g.cx
    cells = [jnp.zeros((ROWS, LANES), F32) for _ in range(coarse_blocks(g))]
    for m in range(len(items)):
        place = lax.rem(m % per + xi, per) * g.cx
        cells[m // per] = cells[m // per] + pltpu.roll(
            summed[m * ROWS : (m + 1) * ROWS], place, 1
        )
    for block, value in enumerate(cells):
        out[0, block] = value


def fill_relay(g, hy, ly, xh, xl, outs, zi):
    Z, X = g.Z, g.X
    for side, out in enumerate(outs):
        high = (zi % 2) == side

        def fill(top, out=out):
            first = Z - DEPTH if top else 0
            pieces = []
            for q in range(3):
                for d in range(DEPTH):
                    count = relay_rows(q, d)
                    if count:
                        part = row_halo(g, hy, ly, q, Z - 1 - d if top else d)
                        pieces += [part[:count], part[ROWS - count :]]
            missing = relay_tiles() * ROWS - sum(piece.shape[0] for piece in pieces)
            if missing:
                pieces.append(jnp.zeros((missing, X), F32))
            packed = jnp.concatenate(pieces, axis=0)
            for tile in range(relay_tiles()):
                for part in range(X // LANES):
                    out[tile * (X // LANES) + part] = packed[
                        tile * ROWS : (tile + 1) * ROWS, part * LANES : (part + 1) * LANES
                    ]
            at_block = relay_tiles() * (X // LANES)
            wide = lane_of((g.YE, LANES))
            acc = jnp.zeros((g.YE, LANES), F32)
            span = DEPTH * DEPTH
            for piece, (ref, q) in enumerate((r, q) for r in (xh, xl) for q in range(3)):
                block, lane_at = g.slot(q, first)
                moved = roll(ref[block], piece * span - lane_at, 1)
                acc = jnp.where((wide >= piece * span) & (wide < (piece + 1) * span), moved, acc)
            out[at_block:] = acc.reshape(g.YE // ROWS, ROWS, LANES)

        pl.when(high)(functools.partial(fill, True))
        pl.when(jnp.logical_not(high))(functools.partial(fill, False))


def coarse_blocks(g):
    per = LANES // g.cx
    return -(-5 * g.cz // per)


def pair_blocks(g):
    return 2 * coarse_blocks(g) - 1


def relay_rows(q, d):
    return max(0, DEPTH - 1 - d - (q == 2))


def relay_tiles():
    rows = sum(2 * relay_rows(q, d) for q in range(3) for d in range(DEPTH))
    return -(-rows // ROWS)


def relay_blocks(g):
    return relay_tiles() * (g.X // LANES) + g.YE // ROWS


def strip_tile(hi, lo):
    lane = lane_of(hi.shape)
    return jnp.where(lane < DEPTH, hi, jnp.where(lane >= LANES - DEPTH, lo, 0.0))


def side_faces(kz):
    wy = face(kz, roll(kz, 1, 0))
    wx = face(kz, roll(kz, 1, 1))
    return wy, wx, wy + roll(wy, -1, 0) + wx + roll(wx, -1, 1)


def scale_of(kz, total):
    return jnp.where(kz > 0.0, OMEGA / total, 0.0)


class Fields:
    def __init__(self, main, side, rows):
        self.parts = main, side, rows

    def __getitem__(self, z):
        main, side, rows = self.parts
        wide = jnp.concatenate([main[z], side[z]], axis=1)
        return jnp.concatenate([wide, rows[z]], axis=0)


class Rows:
    def __init__(self, main, edge, head, tail):
        self.main, self.edge, self.head, self.tail = main, edge, head, tail

    def __getitem__(self, z):
        rows = self.main.shape[1]
        middle = self.main[z, self.head * ROWS : rows - self.tail * ROWS]
        parts = [middle, self.edge[z, self.head * ROWS :]]
        if self.head:
            parts = [self.edge[z, : self.head * ROWS]] + parts
        return jnp.concatenate(parts, axis=0)


def extend_kernel(g, *refs):
    k, xk, fz, fy, fx = refs[:5]
    n = 5
    y_in = refs[n : n + g.ysides]
    n += g.ysides
    x_in = refs[n : n + g.xsides]
    n += g.xsides
    n += 1
    yp, yk, ys, fz_y, fx_y, fy_e, dinv_e, token = refs[n : n + 8]
    n += 8
    relay = refs[n : n + g.zsides]
    n += g.zsides
    hy, ly, xh, xl = refs[n:]
    zi, yi, xi = g.where()
    Z, Y, X = g.Z, g.Y, g.X
    token[...] = jnp.zeros((ROWS, LANES), F32)
    gather_rows(g, yi, y_in, hy, ly)
    gather_strips(g, xi, x_in, hy, ly, xh, xl)
    fill_relay(g, hy, ly, xh, xl, relay, zi)
    for q, out in enumerate((yp, yk, ys)):
        for z in range(Z):
            out[z, :, :X] = row_halo(g, hy, ly, q, z)
            block, at = g.slot(q, z)
            hi = roll(xh[block, Y:], -at, 1)
            lo = roll(xl[block, Y:], -at - DEPTH, 1)
            out[z, :, X:] = strip_tile(hi, lo)

    def edge_rows(z):
        first = jnp.concatenate([k[z, :ROWS], xk[z, :ROWS]], axis=1)
        last = jnp.concatenate([k[z, Y - ROWS :], xk[z, Y - ROWS :]], axis=1)
        return last, yk[z], first

    for z in range(Z):
        last, beyond, first = edge_rows(z)
        tiles = jnp.concatenate([last, beyond, first], axis=0)
        wy = face(tiles, roll(tiles, 1, 0))
        fy_e[z, :ROWS] = wy[2 * ROWS :]
        fy_e[z, ROWS:] = wy[ROWS : 2 * ROWS]
        wx = face(beyond, roll(beyond, 1, 1))
        fx_y[z] = wx
        if z > 0:
            fz_y[z] = face(beyond, yk[z - 1])
    for z in range(1, Z - 1):
        last, beyond, first = edge_rows(z)
        tiles = jnp.concatenate([last, beyond, first], axis=0)
        wy = jnp.concatenate(
            [fy[z, Y - ROWS :], fy_e[z, ROWS:], fy_e[z, :ROWS], fy[z, ROWS : 2 * ROWS]], axis=0
        )
        wy = (wy + roll(wy, -1, 0))[: 3 * ROWS]
        wx = jnp.concatenate([fx[z, Y - ROWS :], fx_y[z], fx[z, :ROWS]], axis=0)
        wz = [
            jnp.concatenate([fz[i, Y - ROWS :], fz_y[i], fz[i, :ROWS]], axis=0) for i in (z, z + 1)
        ]
        scale = scale_of(tiles, wy + wx + roll(wx, -1, 1) + wz[0] + wz[1])
        dinv_e[z, :ROWS] = scale[2 * ROWS :]
        dinv_e[z, ROWS : 2 * ROWS] = scale[:ROWS]
        dinv_e[z, 2 * ROWS :] = scale[ROWS : 2 * ROWS]


def beyond(g, z):
    return z + DEPTH if z < DEPTH else z - g.Z + 3 * DEPTH


def either(top, high, low):
    return (high if top else low) if isinstance(top, bool) else jnp.where(top, high, low)


def halo_at(top, d):
    return either(top, 3 * DEPTH + d, DEPTH - 1 - d)


def face_at(top, d):
    return either(top, DEPTH + d, DEPTH - 1 - d)


def scale_at(top, d):
    return either(top, DEPTH + 1 + d, DEPTH - 2 - d)


def on_sides(g, zi, act):
    if g.zsides == 1:
        act(zi == 0)
    else:
        pl.when(zi < g.nz - 1)(functools.partial(act, True))
        pl.when(zi > 0)(functools.partial(act, False))


def on_ends(g, zi, act):
    if g.zsides == 1:
        act(zi != 0)
    else:
        pl.when(zi == g.nz - 1)(functools.partial(act, True))
        pl.when(zi == 0)(functools.partial(act, False))


def own_weights(refs):
    fz, fz_y, fx, fx_y, fy, fy_e = refs
    return Rows(fz, fz_y, 0, 0), Rows(fx, fx_y, 0, 0), Rows(fy, fy_e, 1, 0)


def halo_kernel(g, *refs):
    own_k = Fields(*refs[:3])
    fz, fx, fy = own_weights(refs[3:9])
    n = 9
    near = refs[n : n + g.zsides]
    n += g.zsides
    deep = refs[n : n + g.zsides]
    n += g.zsides
    relay = refs[n : n + g.zsides]
    n += g.zsides
    n += 1
    ph, sh, hz, hy, hx, hd, token = refs[n : n + 7]
    kh = refs[n + 7]
    token[...] = jnp.zeros((ROWS, LANES), F32)
    zi, yi, xi = g.where()
    Z, Y, X = g.Z, g.Y, g.X
    parts = X // LANES
    rest = DEPTH - 1
    zero = jnp.zeros((g.YE, g.XE), F32)

    def own_faces(z):
        wy, wx = fy[z], fx[z]
        return wy + roll(wy, -1, 0) + wx + roll(wx, -1, 1)

    def fill(top):
        def received(bufs, at):
            if len(bufs) == 1:
                return bufs[0][at]
            return jnp.where((zi % 2 == 0) == top, bufs[0][at], bufs[1][at])

        count = relay_tiles() * parts
        skip = relay[0].shape[0] - relay_blocks(g)
        bufs = [relay[0].at[skip:]] + list(relay[1:])
        tiles = [received(bufs, i) for i in range(relay_blocks(g))]
        strip = jnp.concatenate(tiles[count:], axis=0)
        packed = jnp.concatenate(
            [
                jnp.concatenate(tiles[i : i + parts], axis=1)
                for i in range(0, count, parts)
            ],
            axis=0,
        )
        start = 0
        for q, out in enumerate((ph, kh, sh)):
            for d in range(DEPTH if q < 2 else rest):
                at = halo_at(top, d)
                layer = either(top, d, rest - d)
                if q == 2:
                    plane = received(deep, 2 * rest + either(top, d, rest - 1 - d))
                elif d == 0:
                    plane = received(near, q)
                else:
                    plane = received(deep, q * rest + either(top, d - 1, rest - d))
                out[at, :Y, :X] = plane
                used = relay_rows(q, d)
                if used:
                    rows = [packed[start : start + used], packed[start + used : start + 2 * used]]
                    if 2 * used < ROWS:
                        rows.insert(1, jnp.zeros((ROWS - 2 * used, X), F32))
                    out[at, Y:, :X] = jnp.concatenate(rows, axis=0)
                    start += 2 * used
                else:
                    out[at, Y:, :X] = jnp.zeros((ROWS, X), F32)
                hi = turn(strip, -(q * DEPTH + layer) * DEPTH)
                lo = turn(strip, -((3 + q) * DEPTH + layer) * DEPTH - DEPTH)
                out[at, :, X:] = strip_tile(hi, lo)
        z = either(top, Z - 1, 0)
        kz = own_k[z]
        beyond_k = kh[halo_at(top, 0)]
        outer = face(beyond_k, kz)
        hz[face_at(top, 0)] = outer
        inner = fz[either(top, Z - 1, 1)]
        hd[scale_at(top, -1)] = scale_of(kz, own_faces(z) + inner + outer)
        for d in range(DEPTH - 1):
            inner = outer
            kz = beyond_k
            beyond_k = kh[halo_at(top, d + 1)]
            outer = face(beyond_k, kz)
            hz[face_at(top, d + 1)] = outer
            wy, wx, total = side_faces(kz)
            hy[halo_at(top, d)] = wy
            hx[halo_at(top, d)] = wx
            hd[scale_at(top, d)] = scale_of(kz, total + inner + outer)

    def end(top):
        z = either(top, Z - 1, 0)
        kz = own_k[z]
        ph[halo_at(top, 0)] = zero
        hz[face_at(top, 0)] = kz
        hd[scale_at(top, -1)] = scale_of(kz, own_faces(z) + fz[either(top, Z - 1, 1)] + kz)

    on_sides(g, zi, fill)
    on_ends(g, zi, end)


def turn(values, shift):
    if isinstance(shift, int):
        return roll(values, shift, 1)
    return pltpu.roll(values, lax.rem(shift + 8 * LANES, LANES), 1)


def sweep_kernel(g, sweep, inside, *refs):
    refs = list(refs)
    Z = g.Z
    final = sweep == SWEEPS
    own_s = Fields(*refs[:3])
    fz, fx, fy = own_weights(refs[3:9])
    dinv = Rows(refs[9], refs[10], 1, 1)
    n = 11
    if sweep == 1:
        v = Fields(*refs[n : n + 3])
        n += 3
    else:
        v = refs[n]
        n += 1
    if not inside:
        vh, sh, hz, hy, hx, hd = refs[n : n + 6]
        n += 6
    out = refs[-2]
    refs[-1][...] = jnp.zeros((ROWS, LANES), F32)
    zi, yi, xi = g.where()
    reach = SWEEPS - sweep

    def update(vz, low, high, source, z_low, z_high, wy, wx, scale):
        total = source + z_low * low + z_high * high
        total = total + wy * roll(vz, 1, 0) + roll(wy * vz, -1, 0)
        total = total + wx * roll(vz, 1, 1) + roll(wx * vz, -1, 1)
        return (1.0 - OMEGA) * vz + scale * total

    if inside:

        for z in range(sweep, Z - sweep):
            new = update(
                v[z], v[z - 1], v[z + 1], own_s[z], fz[z], fz[z + 1], fy[z], fx[z], dinv[z]
            )
            if final:
                out[z] = new[: g.Y, : g.X]
            else:
                out[z] = new
        return

    def v_at(z):
        return v[z] if sweep - 1 <= z <= Z - sweep else vh[beyond(g, z)]

    def z_face(z):
        return fz[z] if 1 <= z < Z else hz[face_at(z >= Z, 0)]

    def own_edge(z):
        new = update(
            v_at(z),
            v_at(z - 1),
            v_at(z + 1),
            own_s[z],
            z_face(z),
            z_face(z + 1),
            fy[z],
            fx[z],
            dinv[z] if 0 < z < Z - 1 else hd[scale_at(z > 0, -1)],
        )
        if final:
            out[beyond(g, z) - DEPTH] = new[: g.Y, : g.X]
        else:
            out[beyond(g, z)] = new

    def halo(top):
        inner = v[either(top, Z - 1, 0)] if sweep == 1 else vh[halo_at(top, -1)]
        vz = vh[halo_at(top, 0)]
        for d in range(reach):
            at = halo_at(top, d)
            outer = vh[halo_at(top, d + 1)]
            z_inner, z_outer = hz[face_at(top, d)], hz[face_at(top, d + 1)]
            out[at] = update(
                vz, inner, outer, sh[at], z_inner, z_outer, hy[at], hx[at], hd[scale_at(top, d)]
            )
            inner, vz = vz, outer

    def clear(top):
        out[halo_at(top, 0)] = jnp.zeros((g.YE, g.XE), F32)

    for z in range(sweep):
        own_edge(z)
        own_edge(Z - 1 - z)
    if final:
        return
    on_sides(g, zi, halo)
    on_ends(g, zi, clear)


def extend_sweep_kernel(g, count, *refs):
    p, s, xp, xs, dinv = refs[:5]
    inputs = refs[5 : 5 + count]
    n = 5 + count
    outs = refs[n : n + 8 + g.zsides]
    n += 8 + g.zsides
    v = refs[n]
    scratch = refs[n + 1 :]
    xk, fz, fy, fx = inputs[1:5]
    yp, yk, ys, fz_y, fx_y, fy_e, dinv_e, token = outs[:8]
    extend_kernel(g, *inputs, *outs, *scratch)
    common = (s, xs, ys, fz, fz_y, fx, fx_y, fy, fy_e, dinv, dinv_e)
    sweep_kernel(g, 1, True, *common, p, xp, yp, v, token)


def inner_sweeps_kernel(g, *refs):
    common, v = refs[:11], refs[11]
    between, out, token = refs[-3:]
    sweep_kernel(g, 3, True, *common, v, between, token)
    sweep_kernel(g, 4, True, *common, between, out, token)


def halo_sweeps_kernel(g, count, *refs):
    common, start, v = refs[:11], refs[11:14], refs[14]
    inputs = refs[15 : 15 + count]
    sh, hz, hy, hx, hd, out, token = refs[15 + count : 22 + count]
    kh, ph, vh = refs[22 + count :]
    beyond_own = (sh, hz, hy, hx, hd)
    halo_kernel(g, *inputs, ph, *beyond_own, token, kh)
    sweep_kernel(g, 1, False, *common, *start, ph, *beyond_own, vh, token)
    sweep_kernel(g, 2, False, *common, v, vh, *beyond_own, out, token)


def last_sweeps_kernel(g, *refs):
    common, v = refs[:11], refs[11:13]
    vh, beyond_own = refs[13], refs[14:19]
    out, token, between = refs[19:]
    sweep_kernel(g, 3, False, *common, v[0], vh, *beyond_own, between, token)
    sweep_kernel(g, 4, False, *common, v[1], between, *beyond_own, out, token)


def solve_kernel(g, gathered, fine, edges, out, buffer, sems):
    zi, yi, xi = g.where()
    per = LANES // g.cx
    group = lane_of((ROWS, LANES)) // g.cx

    order = sum(g.steps(), [])

    def place(a, b, c):
        index = {"gx": a, "gy": b, "gz": c}
        at = 0
        for number, (axis, bit) in enumerate(order):
            at = at + (1 << number) * ((index[axis] & bit) // bit)
        return at

    here = place(zi, yi, xi)

    def relative(a, b, c):
        return jnp.bitwise_xor(here, place(a, b, c))

    last = coarse_blocks(g) - 1

    def block_of(at, block):
        return gathered[at >> 1, 2 * last if block == last else (at & 1) * last + block]

    layers = g.nz * g.cz
    height = g.ny * g.cy
    fields = []
    for q in range(5):
        planes = []
        for layer in range(layers):
            a, cz = divmod(layer, g.cz)
            m = q * g.cz + cz
            tiles = []
            for b in range(g.ny):
                value = block_of(relative(a, b, 0), m // per)
                for c in range(1, g.nx):
                    value = jnp.where(
                        group == (m % per + c) % per, block_of(relative(a, b, c), m // per), value
                    )
                tiles.append(roll(value, -(m % per) * g.cx, 1))
            planes.append(jnp.concatenate(tiles, axis=0))
        fields.append(planes)
    rhs, diagonal, wz, wy, wx = fields
    shape = (height, LANES)
    zero = jnp.zeros(shape, F32)
    wz = [zero] + wz[1:]
    wy = [jnp.where(row_of(shape) == 0, 0.0, w) for w in wy]
    wx = [jnp.where(lane_of(shape) == 0, 0.0, w) for w in wx]
    scale = [OMEGA_COARSE / d for d in diagonal]

    def flux(e):
        result = []
        for i in range(layers):
            total = wy[i] * roll(e[i], 1, 0) + roll(wy[i] * e[i], -1, 0)
            total = total + wx[i] * roll(e[i], 1, 1) + roll(wx[i] * e[i], -1, 1)
            if i > 0:
                total = total + wz[i] * e[i - 1]
            if i < layers - 1:
                total = total + wz[i + 1] * e[i + 1]
            result.append(total)
        return result

    start = [sc * r for sc, r in zip(scale, rhs)]
    below_y = [sc * w for sc, w in zip(scale, wy)]
    above_y = [sc * roll(w, -1, 0) for sc, w in zip(scale, wy)]
    below_x = [sc * w for sc, w in zip(scale, wx)]
    above_x = [sc * roll(w, -1, 1) for sc, w in zip(scale, wx)]
    below_z = [sc * w for sc, w in zip(scale, wz)]
    above_z = [sc * w for sc, w in zip(scale, wz[1:])]
    e = start
    for _ in range(COARSE_SWEEPS - 1):
        new = []
        for i in range(layers):
            total = start[i] + (1.0 - OMEGA_COARSE) * e[i]
            if i > 0:
                total = total + below_z[i] * e[i - 1]
            if i < layers - 1:
                total = total + above_z[i] * e[i + 1]
            total = total + below_y[i] * roll(e[i], 1, 0) + above_y[i] * roll(e[i], -1, 0)
            total = total + below_x[i] * roll(e[i], 1, 1) + above_x[i] * roll(e[i], -1, 1)
            new.append(total)
        e = new
    f = flux(e)
    left = zero
    total = zero
    for i in range(layers):
        left = left + (rhs[i] - diagonal[i] * e[i] + f[i])
        total = total + diagonal[i]
    shift = jnp.sum(left) / jnp.sum(total)

    own = []
    for cz in range(g.cz):
        mine = jnp.zeros((ROWS, LANES), F32)
        for a in range(g.nz):
            for b in range(g.ny):
                here = (zi == a) & (yi == b)
                mine = jnp.where(here, e[a * g.cz + cz][b * ROWS : (b + 1) * ROWS], mine)
        own.append(mine)
    onehot = (
        lax.broadcasted_iota(jnp.int32, (LANES, g.X), 0)
        == xi * g.cx + lax.broadcasted_iota(jnp.int32, (LANES, g.X), 1) // RATIO
    ).astype(jnp.bfloat16)
    wide = exact_dot(jnp.concatenate(own, axis=0), onehot) + shift
    copies = []
    for cz in range(g.cz):
        block = wide[cz * ROWS : (cz + 1) * ROWS]
        spread = jnp.broadcast_to(block[:, None, :], (g.cy, RATIO, g.X)).reshape(g.Y, g.X)
        for z in range(cz * RATIO, (cz + 1) * RATIO):
            if DEPTH <= z < g.Z - DEPTH:
                buffer[z] = fine[z] + spread
            else:
                buffer[z] = edges[beyond(g, z) - DEPTH] + spread
            if z % DEPTH == DEPTH - 1:
                part = pl.ds(z + 1 - DEPTH, DEPTH)
                copy = pltpu.make_async_copy(buffer.at[part], out.at[part], sems.at[z // DEPTH])
                copy.start()
                copies.append(copy)
    for copy in copies:
        copy.wait()


def copy_kernel(source, out):
    out[...] = source[...]


def merge_kernel(cells, got, token, out):
    count = cells.shape[0]
    out[:count] = cells[...]
    out[count:] = got[...]


def pair_kernel(g, cells, got, token, out):
    last = coarse_blocks(g) - 1
    for block in range(last):
        out[0, block] = cells[0, block]
        out[0, last + block] = got[0, block]
    out[0, 2 * last] = cells[0, last] + got[0, last]


def join_kernel(g, cells, got, relay, out):
    nc = pair_blocks(g)
    count = cells.shape[0]
    for at in range(count):
        out[at * nc : (at + 1) * nc] = cells[at]
        out[(count + at) * nc : (count + at + 1) * nc] = got[at]
    out[2 * count * nc :] = relay[...]


def split_kernel(g, joined, got, token, out):
    nc = pair_blocks(g)
    count = out.shape[0] // 2
    for at in range(count):
        out[at] = joined[at * nc : (at + 1) * nc]
        out[count + at] = got[at * nc : (at + 1) * nc]


def merge(cells, got, token):
    shape = (2 * cells.shape[0],) + cells.shape[1:]
    (out,) = run(merge_kernel, [shape], [cells, got, token], us=0.05, name="merge")
    return out


def exchange(bufs, axis, count, beside=None):
    got = [lax.ppermute(bufs[0], axis, pairs(count, 0))]
    if len(bufs) > 1:
        if beside is None:
            got.append(lax.ppermute(bufs[1], axis, pairs(count, 1)))
        else:
            perm = spread_pairs(count, lax.axis_size(beside))
            got.append(lax.ppermute(bufs[1], (axis, beside), perm))
    return got


def shards(pressure_start, source, permeability):
    g = Grid(pressure_start.shape)
    Z, Y, X = g.Z, g.Y, g.X
    tile = (ROWS, LANES)
    x_shape = (g.blocks, Y, LANES)
    y_shape = (3 * Z // 2 + 1, ROWS, X)
    sums_shape = (5, g.cz, ROWS, X)
    main = (Z, Y, g.XE)
    nc, nr = pair_blocks(g), relay_blocks(g)

    sent = run(
        functools.partial(pack_kernel, g),
        [(Z, Y, X)] * 3
        + [(2, Y, X)] * g.zsides
        + [x_shape] * g.xsides
        + [(2, Z, X)] * g.ysides,
        [pressure_start, permeability, source],
        scratch=[pltpu.SemaphoreType.DMA((3,))],
        name="pack_faces",
        far=True,
    )
    sent = list(sent)
    (p, k, s), near, sent = sent[:3], sent[3 : 3 + g.zsides], sent[3 + g.zsides :]
    x_sent, row_sent = sent[: g.xsides], sent[g.xsides :]
    near_got = exchange(near, "gx", g.nz, "gz")
    x_got = exchange(x_sent, "gz", g.nx)
    row_got = exchange(row_sent, "gy", g.ny, "gz")
    sums, token_l = run(
        functools.partial(local_kernel, g),
        [sums_shape, tile],
        [p, k, s],
        us=US["local"],
        name="local_sums",
    )
    cells, token = run(
        functools.partial(restrict_kernel, g),
        [(1, coarse_blocks(g)) + tile, tile],
        [p, k, sums] + near_got + row_got + row_sent + x_got + x_sent,
        us=US["restrict"],
        name="restrict",
    )
    y_sent = run(
        functools.partial(pack_rows_kernel, g),
        [y_shape] * g.ysides,
        [p, k, s] + x_got + near_got + [token],
        us=US["rows"],
        name="pack_rows",
    )
    y_got = exchange(y_sent, "gy", g.ny, "gz")
    y_got = list(y_got)
    y_got[:1] = run(copy_kernel, [y_shape], y_got[:1], us=0.05, name="first_rows")
    xp, xk, xs, fz, fy, fx, dinv, token_w = run(
        functools.partial(side_weights_kernel, g),
        [(Z, Y, LANES)] * 3 + [main] * 4 + [tile],
        [k] + x_got + [y_sent[0]],
        scratch=[pltpu.VMEM(x_shape, F32)] * 2,
        us=US["side"] + US["weights"],
        name="weights",
    )
    deep = run(
        functools.partial(deep_kernel, g),
        [(3 * (DEPTH - 1), Y, X)] * g.zsides,
        [p, k, s, token_l] + near_got + row_got + x_got,
        us=0.1,
        name="pack_deep",
    )
    deep_got = exchange(deep, "gx", g.nz, "gz")
    rows = (Z, ROWS, g.XE)
    halo_scratch = [pltpu.VMEM(y_shape, F32)] * 2 + [pltpu.VMEM((g.blocks, g.YE, LANES), F32)] * 2
    inputs = [k, xk, fz, fy, fx] + list(y_got) + x_got + [token_w]
    own = (Z, g.YE, g.XE)
    extended = run(
        functools.partial(extend_sweep_kernel, g, len(inputs)),
        [rows] * 5
        + [(Z, 2 * ROWS, g.XE), (Z, 3 * ROWS, g.XE), tile]
        + [(nr,) + tile] * g.zsides
        + [own],
        [p, s, xp, xs, dinv] + inputs,
        scratch=halo_scratch,
        us=US["extend"] + US["sweep"],
        name="extend",
    )
    yp, yk, ys, fz_y, fx_y, fy_e, dinv_e, token_e = extended[:8]
    before, _, after = g.steps()
    for number, (axis, bit) in enumerate(before):
        got = lax.ppermute(cells, axis, flips(lax.axis_size(axis), bit))
        if number == 0:
            (cells,) = run(
                functools.partial(pair_kernel, g),
                [(1, nc) + tile],
                [cells, got, token_w],
                us=0.05,
                name="pair",
            )
    count = 2 * cells.shape[0]
    (joined,) = run(
        functools.partial(join_kernel, g),
        [(count * nc + nr,) + tile],
        [cells, got, extended[8]],
        us=0.05,
        name="join",
    )
    relay = exchange([joined] + list(extended[9:-1]), "gx", g.nz, "gz")
    weights = [fz, fz_y, fx, fx_y, fy, fy_e]
    common = [s, xs, ys] + weights + [dinv, dinv_e]
    far = (4 * DEPTH, g.YE, g.XE)
    far8 = (2 * DEPTH, g.YE, g.XE)
    inner, tokens = [[p, xp, yp], [extended[-1]]], {"W": token_w, "I1": token_e}
    v, tokens["I2"] = run(
        functools.partial(sweep_kernel, g, 2, True),
        [own, tile],
        common + inner[1],
        us=US["sweep"],
        name="inner_2",
    )
    inner.append([v])
    between, v, tokens["I4"] = run(
        functools.partial(inner_sweeps_kernel, g),
        [own, (Z, Y, X), tile],
        common + inner[2],
        us=US["sweep"],
        name="inner_3_4",
    )
    inner += [[between], [v]]
    inputs = [k, xk, yk] + weights + near_got + deep_got + relay + [tokens["I2"]]
    sh, hz, hy, hx, hd, vh, tokens["O2"] = run(
        functools.partial(halo_sweeps_kernel, g, len(inputs)),
        [far, far8, far, far, far8, far, tile],
        common + inner[0] + inner[1] + inputs,
        scratch=[pltpu.VMEM(far, F32)] * 3,
        us=US["halo"] + 2 * US["outer"],
        name="halo_sweeps",
    )
    vh, tokens["O3"] = run(
        functools.partial(last_sweeps_kernel, g),
        [(2 * DEPTH, Y, X), tile],
        common + inner[2] + inner[3] + [vh, sh, hz, hy, hx, hd],
        scratch=[pltpu.VMEM(far, F32)],
        us=2 * US["outer"],
        name="last_sweeps",
    )
    (cells,) = run(
        functools.partial(split_kernel, g),
        [(2 * count, nc) + tile],
        [joined, relay[0], tokens[PLAN[0]]],
        us=0.05,
        name="split",
    )
    for number, (axis, bit) in enumerate(after):
        got = lax.ppermute(cells, axis, flips(lax.axis_size(axis), bit))
        name = PLAN[max(1, number - len(after) + len(PLAN))]
        cells = merge(cells, got, tokens[name])
    (out,) = run(
        functools.partial(solve_kernel, g),
        [(Z, Y, X)],
        [cells, v, vh],
        us=US["solve"],
        scratch=[pltpu.VMEM((Z, Y, X), F32), pltpu.SemaphoreType.DMA((Z // DEPTH,))],
        name="solve",
        far_out=True,
        spaces=[jax.ShapeDtypeStruct((Z, Y, X), F32)],
    )
    return out


def solution(mesh):
    return jax.shard_map(
        shards,
        mesh=mesh,
        in_specs=(P("gx", "gy", "gz"), P("gx", "gy", "gz"), P("gx", "gy", "gz")),
        out_specs=P("gx", "gy", "gz"),
        check_vma=False,
    )
```
